128 devices in a mesh: sec: 2 (over core), tile: 32 (over x, y_lo, z), lev: 2 (over y_hi).
Axes of the slice: x: 4, y: 4 (y_hi: 2, y_lo: 2; y = y_hi * 2 + y_lo), z: 4, core: 2. Of those that a mesh axis runs over, the one named last changes fastest.
Arguments:
- state: float32 [3, 80, 512, 128], P(None, 'lev', 'tile'), may hold values from -6 to 6
- sound: float32 [80, 512, 128], P('lev', 'tile'), may hold values from 0.5 to 2
- target: float32 [3, 80, 512, 128], P(None, 'lev', 'tile'), may hold values from -6 to 6
- edge_turn: int32 [32, 2], P('tile'), may hold values from 0 to 3
- w_first: bfloat16 [240, 512], replicated, may hold values from -0.375 to 0.375
- b_first: float32 [512], replicated, may hold values from -3 to 3
- w_second: bfloat16 [512, 512], replicated, may hold values from -0.25 to 0.25
- w_third: bfloat16 [512, 240], replicated, may hold values from -0.25 to 0.25
Outputs:
- state_grad: float32 [3, 80, 512, 128], P(None, 'lev', 'tile')
- grad_first: float32 [240, 512], replicated
- grad_bias: float32 [512], replicated
- grad_second: float32 [512, 512], replicated
- grad_third: float32 [512, 240], replicated
The draws below stay inside these ranges and needn't reach their ends.
Inputs may be any that keep to these rules, and one draw needn't show every extreme that they name: `edge_turn`: entry [t, 0] is the quarter turn from strip t - 1 into strip t, entry [t, 1] from strip t + 1.
All inputs are finite; a program needn't handle non-finite values.
Results may differ from the reference program's by a relative error of at most 0.0024.
Values may be sent and summed in bfloat16 or wider, within the bound.
No kernel may reach another device: no remote copies, remote signals or barrier semaphores. Data moves between devices by JAX's collectives and lax.ppermute only.
A program may use at most 128 MiB of HBM per device.

```python
import math
import jax
import jax.numpy as jnp
from jax import lax

LEV = 80
HID = 512
BY = 128
SUBSTEPS = 4
FEAT = 240
TILES = 32
NROWS = 512


def with_ends(values, key, smallest, largest):
    shape = values.shape
    index_at = [jax.random.randint(jax.random.fold_in(key, axis), (), 0, shape[axis]) for axis in range(len(shape))]
    values = values.at[tuple(index_at)].set(smallest)
    longest = shape.index(max(shape))
    index_at[longest] = (index_at[longest] + 1) % shape[longest]
    return values.at[tuple(index_at)].set(largest)


def steps_of(rng, dims, pieces, low, top_value):
    factor_of = 1.0
    for position, parts in pieces:
        heights = jax.random.uniform(jax.random.fold_in(jax.random.fold_in(rng, 6), position), (parts,), jnp.float32, low / len(pieces), top_value / len(pieces))
        factor_of = factor_of * jnp.repeat(jnp.exp(heights), dims[position] // parts).reshape((-1,) + (1,) * (len(dims) - 1 - position))
    return factor_of


def normal_values(key, extent, deviation, limit, pieces=(), dtype=jnp.bfloat16):
    factor_of = steps_of(key, extent, pieces, -0.22, 0.18) if pieces else 1.0
    array = jax.random.normal(key, extent, jnp.float32) * deviation * factor_of
    return jnp.minimum(jnp.maximum(array, -limit), limit).astype(dtype)


def setup_inputs(seed: int = 0) -> dict:
    arg_keys = jax.random.split(jax.random.key(seed), 9)
    return {
        "state": normal_values(arg_keys[0], (3, LEV, NROWS, BY), 1.0, 6.0, ((1, 2), (2, 32)), jnp.float32),
        "sound": jnp.clip(jnp.exp(math.log(2.0) - 1.3862944 * jax.random.uniform(arg_keys[1], (LEV, NROWS, BY), jnp.float32) ** steps_of(arg_keys[1], (LEV, NROWS, BY), ((0, 2), (1, 32)), -0.2, 0.2)), 0.5, 2.0),
        "target": normal_values(arg_keys[2], (3, LEV, NROWS, BY), 1.0, 6.0, ((1, 2), (2, 32)), jnp.float32),
        "edge_turn": with_ends(jax.random.randint(arg_keys[3], (TILES, 2), 0, 4), jax.random.fold_in(arg_keys[3], 1), 0, 3).astype(jnp.int32),
        "w_first": normal_values(arg_keys[4], (FEAT, HID), FEAT ** -0.5, 0.375),
        "b_first": normal_values(arg_keys[5], (HID,), 0.5, 3.0, (), jnp.float32),
        "w_second": normal_values(arg_keys[6], (HID, HID), HID ** -0.5, 0.25),
        "w_third": normal_values(arg_keys[7], (HID, FEAT), HID ** -0.5, 0.25),
    }


courant = 0.3
diffusion = 0.08

def pad_along(values, along, before, after):
    widths = [(0, 0)] * values.ndim
    widths[along] = (before, after)
    return jnp.pad(values, widths)

def diff_padded(padded, along, length):

    def take(offset):
        return lax.slice_in_dim(padded, offset, offset + length, axis=along)
    return (8.0 * (take(3) - take(1)) - (take(4) - take(0))) / 12.0

def diff_periodic(values, along):
    return (8.0 * (jnp.roll(values, -1, along) - jnp.roll(values, 1, along)) - (jnp.roll(values, -2, along) - jnp.roll(values, 2, along))) / 12.0

def vertical_mix(padded, length):

    def take(offset):
        return padded[offset:offset + length]
    return (16.0 * (take(3) + take(1)) - (take(4) + take(0)) - 30.0 * take(2)) / 12.0

def turn_factors(quarter):
    cosine = jnp.where(quarter == 0, 1.0, 0.0) - jnp.where(quarter == 2, 1.0, 0.0)
    sine = jnp.where(quarter == 1, 1.0, 0.0) - jnp.where(quarter == 3, 1.0, 0.0)
    return (cosine, sine)

def neighbour_rims(values):
    empty = jnp.zeros_like(values[:, :1, :2])
    below = jnp.concatenate([empty, values[:, :-1, -2:]], axis=1)
    above = jnp.concatenate([values[:, 1:, :2], empty], axis=1)
    return (below, above)

def substep(state, coeff, turn_low, turn_high):
    height, wind_x, wind_y = (state[0], state[1], state[2])
    levels, rows = (height.shape[0], height.shape[2])
    below, above = neighbour_rims(height)
    wind_x = wind_x - coeff * diff_padded(jnp.concatenate([below, height, above], axis=2), 2, rows)
    wind_y = wind_y - coeff * diff_periodic(height, 3)
    mixing = vertical_mix(pad_along(height, 0, 2, 2), levels)
    x_below, x_above = neighbour_rims(wind_x)
    y_below, y_above = neighbour_rims(wind_y)
    cos_low, sin_low = turn_factors(turn_low)
    cos_high, sin_high = turn_factors(turn_high)
    padded_x = jnp.concatenate([cos_low * x_below - sin_low * y_below, wind_x, cos_high * x_above - sin_high * y_above], axis=2)
    height = height - coeff * (diff_padded(padded_x, 2, rows) + diff_periodic(wind_y, 3)) + diffusion * mixing
    return jnp.stack([height, wind_x, wind_y])

def slope(values):
    sigma = jax.nn.sigmoid(values)
    return sigma * (1.0 + values * (1.0 - sigma))

def physics(inputs, moved, goal, w_first, b_first, w_second, w_third):
    features = inputs.shape[0] * inputs.shape[1]
    feat = inputs.astype(jnp.bfloat16).reshape(features, -1)
    first = jnp.dot(w_first.T, feat, preferred_element_type=jnp.float32) + b_first[:, None]
    hidden_one = jax.nn.silu(first).astype(jnp.bfloat16)
    second = jnp.dot(w_second.T, hidden_one, preferred_element_type=jnp.float32)
    hidden_two = jax.nn.silu(second).astype(jnp.bfloat16)
    tendency = jnp.dot(w_third.T, hidden_two, preferred_element_type=jnp.float32)
    resid = moved.reshape(features, -1) + tendency - goal.reshape(features, -1)
    resid_low = resid.astype(jnp.bfloat16)
    grad_third = jnp.dot(hidden_two, resid_low.T, preferred_element_type=jnp.float32)
    err_two = (jnp.dot(w_third, resid_low, preferred_element_type=jnp.float32) * slope(second)).astype(jnp.bfloat16)
    grad_second = jnp.dot(hidden_one, err_two.T, preferred_element_type=jnp.float32)
    err_one = (jnp.dot(w_second, err_two, preferred_element_type=jnp.float32) * slope(first)).astype(jnp.bfloat16)
    grad_first = jnp.dot(feat, err_one.T, preferred_element_type=jnp.float32)
    grad_bias = lax.optimization_barrier(jnp.sum(err_one.astype(jnp.float32), axis=1))
    input_grad = jnp.dot(w_first, err_one, preferred_element_type=jnp.float32)
    return (resid.reshape(inputs.shape), input_grad.reshape(inputs.shape), grad_first, grad_bias, grad_second, grad_third)

def reference(state, sound, target, edge_turn, w_first, b_first, w_second, w_third):
    tiles = edge_turn.shape[0]
    rows = state.shape[2] // tiles
    width = state.shape[3]
    levels = state.shape[1]
    shaped = state.reshape(3, levels, tiles, rows, width)
    goal_shaped = target.reshape(3, levels, tiles, rows, width)
    coeff = courant * sound.reshape(levels, tiles, rows, width)
    turn_low = edge_turn[:, 0].reshape(1, tiles, 1, 1)
    turn_high = edge_turn[:, 1].reshape(1, tiles, 1, 1)

    def forward(values):
        for step in range(SUBSTEPS):
            values = substep(values, coeff, turn_low, turn_high)
        return values
    evolved, pullback = jax.vjp(forward, shaped)

    def block(items):
        inputs, moved, goal = items
        return physics(inputs, moved, goal, w_first, b_first, w_second, w_third)
    resid, input_grad, g_first, g_bias, g_second, g_third = lax.map(block, (jnp.moveaxis(shaped, 2, 0), jnp.moveaxis(evolved, 2, 0), jnp.moveaxis(goal_shaped, 2, 0)))
    resid_full = jnp.moveaxis(resid, 0, 2)
    input_full = jnp.moveaxis(input_grad, 0, 2)
    adjoint = pullback(resid_full)[0]
    state_grad = (adjoint + input_full).reshape(3, levels, tiles * rows, width)
    ncols = tiles * rows * width
    return (state_grad, lax.optimization_barrier(jnp.sum(g_first, axis=0)) / ncols, lax.optimization_barrier(jnp.sum(g_bias, axis=0)) / ncols, lax.optimization_barrier(jnp.sum(g_second, axis=0)) / ncols, lax.optimization_barrier(jnp.sum(g_third, axis=0)) / ncols)
```

```python
import jax
import jax.numpy as jnp
from jax import lax
from jax.experimental import pallas as pl
from jax.experimental.pallas import tpu as pltpu
from jax.sharding import PartitionSpec as P

SUBSTEPS = 4
COURANT = 0.3
DIFFUSION = 0.08
NEAR = 8.0 / 12.0
FAR = 1.0 / 12.0

BLK = 8
OWN = 40
EDGE = 8
EXT = OWN + EDGE
ROWS = 7 * BLK
CHUNK = 4
WIND_BLOCKS = ((0, 5), (0, 5), (1, 4), (1, 4))
MASS_BLOCKS = ((0, 5), (1, 4), (1, 4), (2, 3))


def roll(values, steps, axis):
    return pltpu.roll(values, steps % values.shape[axis], axis)


def across(values):
    return NEAR * (roll(values, -1, 2) - roll(values, 1, 2)) - FAR * (
        roll(values, -2, 2) - roll(values, 2, 2)
    )


def along(ref, levels, row):
    def take(steps):
        return ref[levels, row + steps : row + steps + BLK, :]

    return NEAR * (take(1) - take(-1)) - FAR * (take(2) - take(-2))


def vertical(ref, k, row):
    v = ref[pl.ds(k, CHUNK + 4), row : row + BLK, :]
    mid = v[2 : 2 + CHUNK]
    near = v[3 : 3 + CHUNK] + v[1 : 1 + CHUNK]
    far = v[4 : 4 + CHUNK] + v[0:CHUNK]
    return mid, DIFFUSION * (16.0 / 12.0) * near - (DIFFUSION / 12.0) * far - (
        DIFFUSION * 30.0 / 12.0
    ) * mid


def edge_masks():
    i = lax.broadcasted_iota(jnp.int32, (1, 2 * BLK, 128), 1)

    def at(row, value):
        return jnp.where(i == row, value, 0.0)

    return at(8, -NEAR), at(8, FAR) + at(9, FAR), at(7, NEAR), at(7, -FAR) + at(6, -FAR)


def crossing(values, masks):
    m1, m2, m3, m4 = masks
    return (
        m1 * roll(values, 1, 1)
        + m2 * roll(values, 2, 1)
        + m3 * roll(values, -1, 1)
        + m4 * roll(values, -2, 1)
    )


def turn_rows(turn_ref, edge):
    i = lax.broadcasted_iota(jnp.int32, (1, 2 * BLK, 128), 1)
    low = i < BLK
    cosine = jnp.where(low, turn_ref[4 * edge], turn_ref[4 * edge + 2])
    sine = jnp.where(low, turn_ref[4 * edge + 1], turn_ref[4 * edge + 3])
    return cosine, sine


def clear(ref, levels):
    zeros = jnp.zeros((levels, BLK, 128), jnp.float32)
    ref[:, 0:BLK, :] = zeros
    ref[:, ROWS - BLK : ROWS, :] = zeros


def spread_block(src, comp, count, dst, level, row, scale):
    def body(i, _):
        rows = src[comp, pl.ds(pl.multiple_of(i * 16, 16), 16), :].astype(jnp.float32)
        if scale != 1.0:
            rows = rows * scale
        dst[pl.ds(level + 2 * i, 2), pl.ds(row, BLK), :] = rows.reshape(2, BLK, 128)
        return 0

    lax.fori_loop(0, count // 2, body, 0, unroll=4)


def places(place_ref):
    sec, lev = place_ref[0], place_ref[1]
    own_level = EDGE * lev
    edge_level = OWN * (1 - lev)
    partner_row = pl.multiple_of(16 + 16 * sec, BLK)
    other_row = pl.multiple_of(32 - 16 * sec, BLK)
    tile_row = pl.multiple_of(24 - 8 * sec, BLK)
    near_edge = pl.multiple_of(16 + 8 * sec, BLK)
    far_edge = pl.multiple_of(32 - 24 * sec, BLK)
    return own_level, edge_level, partner_row, other_row, tile_row, near_edge, far_edge


def forward_kernel(
    place_ref, turn_ref, state_ref, sound_ref, low_ref, high_ref, low_edge_ref, high_edge_ref,
    partner_ref, partner_edge_ref, other_edge_ref, own_edge_ref,
    out_ref, c_ref, pa, pb, u, v,
):
    own_level, edge_level, partner_row, other_row, tile_row, near_edge, far_edge = places(place_ref)
    for ref, levels in ((pa, EXT + 4), (pb, EXT + 4), (u, EXT), (v, EXT), (c_ref, EXT)):
        clear(ref, levels)
    for ref in (pa, pb):
        ref[0:2] = jnp.zeros((2, ROWS, 128), jnp.float32)
        ref[EXT + 2 : EXT + 4] = jnp.zeros((2, ROWS, 128), jnp.float32)
    for comp, dst, shift, scale in ((0, pa, 2, 1.0), (1, u, 0, 1.0), (2, v, 0, 1.0), (3, c_ref, 0, COURANT)):
        at = own_level + shift
        for src, edge, row in (
            (low_ref, low_edge_ref, BLK),
            (high_ref, high_edge_ref, 5 * BLK),
            (partner_ref, partner_edge_ref, partner_row),
        ):
            spread_block(src, comp, OWN, dst, at, row, scale)
            spread_block(edge, comp, EDGE, dst, edge_level + shift, row, scale)
        spread_block(other_edge_ref, comp, EDGE, dst, edge_level + shift, other_row, scale)
        spread_block(own_edge_ref, comp, EDGE, dst, edge_level + shift, 3 * BLK, scale)
        if comp < 3:
            dst[pl.ds(at, OWN), pl.ds(tile_row, 16), :] = state_ref[comp]
        else:
            dst[pl.ds(at, OWN), pl.ds(tile_row, 16), :] = COURANT * sound_ref[...]
    masks = edge_masks()
    turns = [turn_rows(turn_ref, 0), turn_rows(turn_ref, 1)]
    for step in range(SUBSTEPS):
        old, new = (pa, pb) if step % 2 == 0 else (pb, pa)

        def body(i, _, step=step, old=old, new=new):
            k = i * CHUNK
            levels = pl.ds(k, CHUNK)
            inner = pl.ds(k + 2, CHUNK)
            for block in range(*WIND_BLOCKS[step]):
                row = BLK + BLK * block
                rows = slice(row, row + BLK)
                c = c_ref[levels, rows, :]
                u[levels, rows, :] = u[levels, rows, :] - c * along(old, inner, row)
                v[levels, rows, :] = v[levels, rows, :] - c * across(old[inner, rows, :])
            for block in range(*MASS_BLOCKS[step]):
                row = BLK + BLK * block
                rows = slice(row, row + BLK)
                c = c_ref[levels, rows, :]
                mid, mixing = vertical(old, k, row)
                spread = along(u, levels, row) + across(v[levels, rows, :])
                new[inner, rows, :] = mid - c * spread + mixing
            for edge, start in enumerate((near_edge, far_edge)[: 2 if step < 2 else 1]):
                window = pl.ds(start, 2 * BLK)
                cosine, sine = turns[edge]
                delta = cosine * u[levels, window, :] - sine * v[levels, window, :]
                c = c_ref[levels, window, :]
                new[inner, window, :] = new[inner, window, :] - c * crossing(delta, masks)
            return 0

        lax.fori_loop(0, EXT // CHUNK, body, 0)
    final = pa if SUBSTEPS % 2 == 0 else pb
    own = slice(3 * BLK, 4 * BLK)
    out_ref[0] = final[pl.ds(own_level + 2, OWN), own, :]
    out_ref[1] = u[pl.ds(own_level, OWN), own, :]
    out_ref[2] = v[pl.ds(own_level, OWN), own, :]


def adjoint_kernel(
    place_ref, turn_ref, resid_ref, other_ref, low_ref, high_ref, low_edge_ref, high_edge_ref,
    partner_ref, partner_edge_ref, other_edge_ref, own_edge_ref, c_ref,
    out_ref, pa, pb, u, v, w,
):
    own_level, edge_level, partner_row, other_row, tile_row, near_edge, far_edge = places(place_ref)
    for ref, levels in ((pa, EXT + 4), (pb, EXT + 4), (u, EXT), (v, EXT), (w, CHUNK)):
        clear(ref, levels)
    for ref in (pa, pb):
        ref[0:2] = jnp.zeros((2, ROWS, 128), jnp.float32)
        ref[EXT + 2 : EXT + 4] = jnp.zeros((2, ROWS, 128), jnp.float32)
    for comp, dst, shift in ((0, pa, 2), (1, u, 0), (2, v, 0)):
        at = own_level + shift
        for src, edge, row in (
            (low_ref, low_edge_ref, BLK),
            (high_ref, high_edge_ref, 5 * BLK),
            (partner_ref, partner_edge_ref, partner_row),
        ):
            spread_block(src, comp, OWN, dst, at, row, 1.0)
            spread_block(edge, comp, EDGE, dst, edge_level + shift, row, 1.0)
        spread_block(other_edge_ref, comp, EDGE, dst, edge_level + shift, other_row, 1.0)
        spread_block(own_edge_ref, comp, EDGE, dst, edge_level + shift, 3 * BLK, 1.0)
        dst[pl.ds(at, OWN), 3 * BLK : 4 * BLK, :] = resid_ref[comp]
        dst[pl.ds(at, OWN), pl.ds(other_row, BLK), :] = other_ref[comp]
    masks = edge_masks()
    turns = [turn_rows(turn_ref, 0), turn_rows(turn_ref, 1)]
    whole = pl.ds(0, CHUNK)
    for step in range(SUBSTEPS):
        old, new = (pa, pb) if step % 2 == 0 else (pb, pa)

        def body(i, _, step=step, old=old, new=new):
            k = i * CHUNK
            levels = pl.ds(k, CHUNK)
            inner = pl.ds(k + 2, CHUNK)
            w[:, BLK : 6 * BLK, :] = c_ref[levels, BLK : 6 * BLK, :] * old[inner, BLK : 6 * BLK, :]
            for block in range(*WIND_BLOCKS[step]):
                row = BLK + BLK * block
                rows = slice(row, row + BLK)
                u[levels, rows, :] = u[levels, rows, :] + along(w, whole, row)
                v[levels, rows, :] = v[levels, rows, :] + across(w[:, rows, :])
            for edge, start in enumerate((near_edge, far_edge)[: 2 if step < 2 else 1]):
                window = pl.ds(start, 2 * BLK)
                cosine, sine = turns[edge]
                cross = crossing(w[:, window, :], masks)
                u[levels, window, :] = u[levels, window, :] + cosine * cross
                v[levels, window, :] = v[levels, window, :] - sine * cross
            w[:, BLK : 6 * BLK, :] = c_ref[levels, BLK : 6 * BLK, :] * u[levels, BLK : 6 * BLK, :]
            for block in range(*MASS_BLOCKS[step]):
                row = BLK + BLK * block
                rows = slice(row, row + BLK)
                mid, mixing = vertical(old, k, row)
                cv = c_ref[levels, rows, :] * v[levels, rows, :]
                new[inner, rows, :] = mid + mixing + along(w, whole, row) + across(cv)
            return 0

        lax.fori_loop(0, EXT // CHUNK, body, 0)
    final = pa if SUBSTEPS % 2 == 0 else pb
    own = slice(3 * BLK, 4 * BLK)
    out_ref[0] = final[pl.ds(own_level + 2, OWN), own, :]
    out_ref[1] = u[pl.ds(own_level, OWN), own, :]
    out_ref[2] = v[pl.ds(own_level, OWN), own, :]


def scratch(extra=()):
    mass = pltpu.VMEM((EXT + 4, ROWS, 128), jnp.float32)
    wind = pltpu.VMEM((EXT, ROWS, 128), jnp.float32)
    return [mass, mass, wind, wind, *extra]


def call(kernel, n_smem, n_vmem, outs, extra=()):
    vmem = pl.BlockSpec(memory_space=pltpu.VMEM)
    smem = pl.BlockSpec(memory_space=pltpu.SMEM)
    return pl.pallas_call(
        kernel,
        out_shape=outs,
        in_specs=[smem] * n_smem + [vmem] * n_vmem,
        out_specs=jax.tree.map(lambda _: vmem, outs),
        scratch_shapes=scratch(extra),
        compiler_params=pltpu.CompilerParams(vmem_limit_bytes=48 * 1024 * 1024),
        cost_estimate=pl.CostEstimate(flops=40_000_000, bytes_accessed=10_000_000, transcendentals=0),
    )


def swap(value, axis):
    return lax.ppermute(value, axis, [(0, 1), (1, 0)])


def strip_swaps(value, edges, tiles):
    odd = lax.rem(lax.axis_index("tile"), 2) == 1
    first = [(t, t ^ 1) for t in range(tiles)]
    second = [(t, ((t + 1) ^ 1) - 1) for t in range(1, tiles - 1)]

    def cross(pairs):
        return [(2 * a + lev, 2 * b + 1 - lev) for a, b in pairs for lev in range(2)]

    a = lax.ppermute(value, "tile", first)
    b = lax.ppermute(value, "tile", second)
    a_edge = lax.ppermute(edges, ("tile", "lev"), cross(first))
    b_edge = lax.ppermute(edges, ("tile", "lev"), cross(second))
    return (
        jnp.where(odd, a, b),
        jnp.where(odd, b, a),
        jnp.where(odd, a_edge, b_edge),
        jnp.where(odd, b_edge, a_edge),
    )


def turn_factors(quarter):
    cosine = jnp.where(quarter == 0, 1.0, 0.0) - jnp.where(quarter == 2, 1.0, 0.0)
    sine = jnp.where(quarter == 1, 1.0, 0.0) - jnp.where(quarter == 3, 1.0, 0.0)
    return (cosine, sine)


def slope(values):
    sigma = jax.nn.sigmoid(values)
    return sigma * (1.0 + values * (1.0 - sigma))


def product(left, right, left_dim, right_dim):
    return lax.dot_general(
        left, right, (((left_dim,), (right_dim,)), ((), ())), preferred_element_type=jnp.float32
    )


def local(state, sound, target, edge_turn, w_first, b_first, w_second, w_third):
    sec, lev = lax.axis_index("sec"), lax.axis_index("lev")
    tiles = lax.axis_size("tile")
    bf = jnp.bfloat16
    width = state.shape[3]
    hid = w_second.shape[0]
    feats = w_first.shape[0]
    cols = BLK * width

    def own_rows(values):
        return lax.dynamic_slice_in_dim(values, sec * BLK, BLK, values.ndim - 2)

    def edge_levels(values):
        return lax.dynamic_slice_in_dim(values, (OWN - EDGE) * (1 - lev), EDGE, 1)

    def packed(values):
        return values.reshape(values.shape[0], -1, width)

    def both_levels(own, other):
        own = own.reshape(3, OWN, cols)
        other = other.reshape(3, OWN, cols)
        low = jnp.where(lev == 0, own, other)
        high = jnp.where(lev == 0, other, own)
        return jnp.concatenate([low, high], axis=1).reshape(feats, cols)

    def near_far(value):
        low, high = value
        return jnp.where(sec == 0, high, low)

    own_state = own_rows(state)
    own_sound = own_rows(sound)
    block = jnp.concatenate([own_state, own_sound[None]], axis=0).astype(bf)
    cos_low, sin_low = turn_factors(edge_turn[0, 0])
    cos_high, sin_high = turn_factors(edge_turn[0, 1])
    factors = jnp.stack([cos_low, sin_low, cos_high, sin_high])
    turn_block = jnp.broadcast_to(
        jnp.concatenate([factors, jnp.zeros((12,), factors.dtype)])[:, None], (16, width)
    ).astype(bf)
    edges = edge_levels(block)
    payload = jnp.concatenate([block.reshape(-1, width), turn_block], axis=0)
    low, high, low_edge, high_edge = strip_swaps(payload, packed(edges), tiles)
    columns = swap(
        jnp.concatenate([block[:3].reshape(-1, width), edges[3].reshape(-1, width)], axis=0), "lev"
    )
    n_state = 3 * OWN * BLK
    other_state = columns[:n_state].reshape(3, OWN, BLK, width)
    lev_edge = lax.dynamic_slice_in_dim(other_state, (OWN - EDGE) * lev, EDGE, 1)
    own_edge = jnp.concatenate(
        [packed(lev_edge), columns[n_state:].reshape(1, EDGE * BLK, width)], axis=0
    )
    low_turn, high_turn = low[4 * OWN * BLK :, 0], high[4 * OWN * BLK :, 0]
    low = low[: 4 * OWN * BLK].reshape(4, OWN * BLK, width)
    high = high[: 4 * OWN * BLK].reshape(4, OWN * BLK, width)
    partner, partner_edge, other_edge = swap(
        (near_far((low, high)), near_far((low_edge, high_edge)), own_edge), "sec"
    )
    f32 = jnp.float32
    lower = jnp.stack([cos_low - 1, sin_low, low_turn[2].astype(f32) - 1, low_turn[3].astype(f32)])
    upper = jnp.stack(
        [high_turn[0].astype(f32) - 1, high_turn[1].astype(f32), cos_high - 1, sin_high]
    )
    turns = jnp.where(sec == 0, jnp.concatenate([lower, upper]), jnp.concatenate([upper, lower]))
    place = jnp.stack([sec, lev]).astype(jnp.int32)

    evolved, coeff = call(
        forward_kernel, 2, 10,
        (jax.ShapeDtypeStruct((3, OWN, BLK, width), f32), jax.ShapeDtypeStruct((EXT, ROWS, width), f32)),
    )(place, turns, state, sound, low, high, low_edge, high_edge, partner, partner_edge, other_edge, own_edge)

    feat = both_levels(block[:3], other_state)
    first = product(w_first, feat, 0, 0) + b_first[:, None]
    hidden_one = jax.nn.silu(first).astype(bf)
    second = product(w_second, hidden_one, 0, 0)
    hidden_two = jax.nn.silu(second).astype(bf)
    w_third_own = lax.dynamic_slice_in_dim(w_third.reshape(hid, 3, 2 * OWN), lev * OWN, OWN, 2)
    w_first_own = lax.dynamic_slice_in_dim(w_first.reshape(3, 2 * OWN, hid), lev * OWN, OWN, 1)
    tendency = product(w_third_own.reshape(hid, 3 * OWN), hidden_two, 0, 0)
    resid = evolved + tendency.reshape(3, OWN, BLK, width) - own_rows(target)

    resid_low = resid.astype(bf)
    other_block = swap(resid, "sec")
    r_edges = packed(edge_levels(resid_low))
    r_low, r_high, r_low_edge, r_high_edge = strip_swaps(packed(resid_low), r_edges, tiles)
    other_resid = swap(packed(resid_low), "lev").reshape(3, OWN, BLK, width)
    r_own_edge = packed(lax.dynamic_slice_in_dim(other_resid, (OWN - EDGE) * lev, EDGE, 1))
    r_partner, r_partner_edge, r_other_edge = swap(
        (near_far((r_low, r_high)), near_far((r_low_edge, r_high_edge)), r_own_edge), "sec"
    )

    resid_cols = both_levels(resid_low, other_resid)
    err_two = (product(w_third, resid_cols, 1, 0) * slope(second)).astype(bf)
    err_one = (product(w_second, err_two, 1, 0) * slope(first)).astype(bf)
    half = hid // 2

    def half_units(values):
        return lax.dynamic_slice_in_dim(values, lev * half, half, 0)

    err_half = half_units(err_one)
    n_rows = 1024
    grads = jnp.concatenate(
        [
            product(feat, err_half, 1, 1),
            product(hidden_one, half_units(err_two), 1, 1),
            product(resid_cols, half_units(hidden_two), 1, 1),
            jnp.sum(err_half.astype(f32), axis=1)[None],
            jnp.zeros((n_rows - 2 * feats - hid - 1, half), f32),
        ],
        axis=0,
    )
    quarter = half // 2
    kept = lax.dynamic_slice_in_dim(grads, sec * quarter, quarter, 1)
    given = lax.dynamic_slice_in_dim(grads, (1 - sec) * quarter, quarter, 1)
    kept = kept + swap(given, "sec")
    share = n_rows // tiles
    parts = lax.all_to_all(kept.astype(bf).reshape(tiles, share, quarter), "tile", 0, 0)
    ncols = cols * 2 * tiles
    total = jnp.sum(parts.astype(f32), axis=0) / ncols
    everywhere = jnp.broadcast_to(total[None], (2 * tiles, share, quarter))
    gathered = lax.all_to_all(everywhere, ("tile", "lev"), 0, 0)
    partner_half = swap(gathered, "sec")
    halves = jnp.stack(
        [jnp.where(sec == 0, gathered, partner_half), jnp.where(sec == 0, partner_half, gathered)]
    ).reshape(2, tiles, 2, share, quarter)
    full = halves.transpose(1, 3, 2, 0, 4).reshape(n_rows, hid)

    input_grad = product(w_first_own.reshape(3 * OWN, hid), err_one, 1, 0)
    adjoint = call(
        adjoint_kernel, 2, 11, jax.ShapeDtypeStruct((3, OWN, BLK, width), f32),
        (pltpu.VMEM((CHUNK, ROWS, 128), f32),),
    )(place, turns, resid, other_block, r_low, r_high, r_low_edge, r_high_edge, r_partner, r_partner_edge, r_other_edge, r_own_edge, coeff)
    mine = adjoint + input_grad.reshape(3, OWN, BLK, width)
    theirs = swap(mine, "sec")
    state_grad = jnp.concatenate(
        [jnp.where(sec == 0, mine, theirs), jnp.where(sec == 0, theirs, mine)], axis=2
    )
    return (
        state_grad,
        full[:feats],
        full[2 * feats + hid],
        full[feats : feats + hid],
        full[feats + hid : 2 * feats + hid].T,
    )


def solution(mesh):
    placed = (
        P(None, "lev", "tile", None),
        P("lev", "tile", None),
        P(None, "lev", "tile", None),
        P("tile", None),
        P(),
        P(),
        P(),
        P(),
    )
    return jax.shard_map(
        local,
        mesh=mesh,
        in_specs=placed,
        out_specs=(P(None, "lev", "tile", None), P(), P(), P(), P()),
        check_vma=False,
    )
```

```python
import jax
import jax.numpy as jnp
from jax import lax
from jax.experimental import pallas as pl
from jax.experimental.pallas import tpu as pltpu
from jax.sharding import PartitionSpec as P

SUBSTEPS = 4
COURANT = 0.3
DIFFUSION = 0.08
UNIT = 1.0 / 12.0

BLK = 8
OWN = 40
EDGE = 8
EXT = OWN + EDGE
ROWS = 7 * BLK
CHUNK = 24
WIND_BLOCKS = ((0, 5), (0, 5), (1, 4), (1, 4))
MASS_BLOCKS = ((0, 5), (1, 4), (1, 4), (2, 3))
FIELD = OWN * BLK
RIM = EDGE * BLK
COLS = BLK * 128
GROUP = 128
PAD = GROUP - 3 * OWN
STRIPE = 256
MIB = 1024 * 1024
F32 = jnp.float32
BF = jnp.bfloat16


def roll(values, steps, axis):
    return pltpu.roll(values, steps % values.shape[axis], axis)


def across_matrix():
    source = lax.broadcasted_iota(jnp.int32, (256, 128), 0)
    target = lax.broadcasted_iota(jnp.int32, (256, 128), 1)
    apart = (source - target) & 127
    near = jnp.where(apart == 1, 8.0, 0.0) - jnp.where(apart == 127, 8.0, 0.0)
    far = jnp.where(apart == 126, 1.0, 0.0) - jnp.where(apart == 2, 1.0, 0.0)
    return (near + far).astype(BF)


def across(values, matrix):
    flat = values.reshape(-1, 128)
    high = flat.astype(BF)
    low = (flat - high.astype(F32)).astype(BF)
    return dot(jnp.concatenate([high, low], axis=1), matrix[...]).reshape(values.shape)


def along(ref, levels, row):
    def take(steps):
        return ref[levels, row + steps : row + steps + BLK, :]

    return 8.0 * (take(1) - take(-1)) - (take(2) - take(-2))


def vertical(ref, k, row):
    v = ref[pl.ds(k, CHUNK + 4), row : row + BLK, :]
    near = v[3 : 3 + CHUNK] + v[1 : 1 + CHUNK]
    far = v[4 : 4 + CHUNK] + v[0:CHUNK]
    return (1.0 - 30.0 * UNIT * DIFFUSION) * v[2 : 2 + CHUNK] + (UNIT * DIFFUSION) * (16.0 * near - far)


def edge_masks():
    i = lax.broadcasted_iota(jnp.int32, (1, BLK, 128), 1)

    def at(row, value):
        return jnp.where(i == row, value, 0.0)

    return at(4, -8.0), at(4, 1.0) + at(5, 1.0), at(3, 8.0), at(3, -1.0) + at(2, -1.0)


def crossing(values, masks):
    m1, m2, m3, m4 = masks
    return (
        m1 * roll(values, 1, 1)
        + m2 * roll(values, 2, 1)
        + m3 * roll(values, -1, 1)
        + m4 * roll(values, -2, 1)
    )


def quarter_turn(quarter):
    cosine = jnp.where(quarter == 0, 1.0, 0.0) - jnp.where(quarter == 2, 1.0, 0.0)
    sine = jnp.where(quarter == 1, 1.0, 0.0) - jnp.where(quarter == 3, 1.0, 0.0)
    return cosine, sine


def clear(ref):
    levels = ref.shape[0]
    zeros = jnp.zeros((levels, BLK, 128), F32)
    ref[:, 0:BLK, :] = zeros
    ref[:, ROWS - BLK : ROWS, :] = zeros


def clear_levels(ref):
    for level in (0, 1, EXT + 2, EXT + 3):
        ref[level] = jnp.zeros((ROWS, 128), F32)


def spread(src, start, count, dst, level, row, scale=None):
    def body(i, _):
        rows = src[pl.ds(pl.multiple_of(start + i * 16, 16), 16), :].astype(F32)
        if scale is not None:
            rows = rows * scale
        dst[pl.ds(level + 2 * i, 2), row : row + BLK, :] = rows.reshape(2, BLK, 128)
        return 0

    lax.fori_loop(0, count // 2, body, 0, unroll=4)


def static_rows(sec):
    return 16 + 16 * sec, 32 - 16 * sec, 24 + 8 * sec, 40 - 24 * sec


def spread_rims(sec, lev, odd, a, b, a_edge, b_edge, partner, partner_edge, own_col, other_col, fields):
    partner_row, other_row, _, _ = static_rows(sec)
    own_level, edge_level = EDGE * lev, OWN * (1 - lev)

    def sides(low, high, low_edge, high_edge):
        for n, (dst, shift, scale) in enumerate(fields):
            for src, edge, row in ((low, low_edge, BLK), (high, high_edge, 5 * BLK)):
                spread(src, n * FIELD, OWN, dst, own_level + shift, row, scale)
                spread(edge, n * RIM, EDGE, dst, edge_level + shift, row, scale)

    pl.when(odd)(lambda: sides(a, b, a_edge, b_edge))
    pl.when(jnp.logical_not(odd))(lambda: sides(b, a, b_edge, a_edge))
    for n, (dst, shift, scale) in enumerate(fields):
        spread(partner, n * FIELD, OWN, dst, own_level + shift, partner_row, scale)
        spread(partner_edge, n * RIM, EDGE, dst, edge_level + shift, partner_row, scale)
        start = BLK * GROUP + n * RIM
        spread(other_col, start, EDGE, dst, edge_level + shift, other_row, scale)
        spread(own_col, start, EDGE, dst, edge_level + shift, 3 * BLK, scale)


def chunk_range(step, lev):
    trim = 2 * step // CHUNK
    return trim * lev, EXT // CHUNK - trim * (1 - lev)


def column_rows(ref, row, start, stride, step, fill):
    fields = [ref[pl.ds(n * step + start + row, OWN, stride=stride), :] for n in range(3)]
    return jnp.concatenate([*fields, jnp.full((PAD, 128), fill, F32)], axis=0).astype(BF)


def pack_kernel(turn_ref, state_ref, sound_ref, rows_ref, edge_ref, column_ref):
    sec, lev = lax.axis_index("sec"), lax.axis_index("lev")

    def run(row):
        for n in range(4):
            src = state_ref[n * OWN * 16 : (n + 1) * OWN * 16, :] if n < 3 else sound_ref[...]
            field = src.reshape(OWN, 16, 128)[:, row : row + BLK, :].reshape(FIELD, 128)
            rows_ref[n * FIELD : (n + 1) * FIELD, :] = field.astype(BF)
        for r in range(BLK):
            column_ref[r * GROUP : (r + 1) * GROUP, :] = column_rows(state_ref, r, row, 16, OWN * 16, 1.0)

    for half in range(2):
        pl.when(sec == half)(lambda half=half: run(BLK * half))
    for n in range(4):
        start = pl.multiple_of(n * FIELD + (FIELD - RIM) * (1 - lev), 16)
        rim = rows_ref[pl.ds(start, RIM), :]
        edge_ref[n * RIM : (n + 1) * RIM, :] = rim
        column_ref[BLK * GROUP + n * RIM : BLK * GROUP + (n + 1) * RIM, :] = rim
    i = lax.broadcasted_iota(jnp.int32, (16, 128), 0)
    factors = jnp.zeros((16, 128), F32)
    for n, value in enumerate((*quarter_turn(turn_ref[0, 0]), *quarter_turn(turn_ref[0, 1]))):
        factors = jnp.where(i == n, value, factors)
    rows_ref[4 * FIELD :, :] = factors.astype(BF)


def forward_kernel(
    turn_ref, state_ref, sound_ref, target_ref, tendency_ref,
    a, b, a_edge, b_edge, partner, partner_edge, own_col, other_col,
    resid_ref, rows_ref, edge_ref, column_ref, c_ref, factor_ref, pa, pb, u, v, matrix,
):
    section, lev = lax.axis_index("sec"), lax.axis_index("lev")
    odd = lax.rem(lax.axis_index("tile"), 2) == 1
    own_level = EDGE * lev
    for ref in (pa, pb, u, v, c_ref):
        clear(ref)
    clear_levels(pa)
    clear_levels(pb)
    cos_low, sin_low = quarter_turn(turn_ref[0, 0])
    cos_high, sin_high = quarter_turn(turn_ref[0, 1])
    below = lax.broadcasted_iota(jnp.int32, (BLK, 128), 0) < 4

    def factors(low, high):
        low = low[4 * FIELD :, :].astype(F32)
        high = high[4 * FIELD :, :].astype(F32)
        factor_ref[0] = jnp.where(below, cos_low, low[2:3, :]) - 1.0
        factor_ref[1] = jnp.where(below, sin_low, low[3:4, :])
        factor_ref[2] = jnp.where(below, high[0:1, :], cos_high) - 1.0
        factor_ref[3] = jnp.where(below, high[1:2, :], sin_high)

    pl.when(odd)(lambda: factors(a, b))
    pl.when(jnp.logical_not(odd))(lambda: factors(b, a))
    masks = edge_masks()
    matrix[...] = across_matrix()

    def run(sec):
        unit = COURANT * UNIT
        spread_rims(
            sec, lev, odd, a, b, a_edge, b_edge, partner, partner_edge, own_col, other_col,
            ((pa, 2, None), (u, 0, None), (v, 0, None), (c_ref, 0, unit)),
        )
        _, _, near_edge, far_edge = static_rows(sec)
        tile_row = 24 - 8 * sec
        for n, (dst, shift) in enumerate(((pa, 2), (u, 0), (v, 0))):
            field = state_ref[n * OWN * 16 : (n + 1) * OWN * 16, :].reshape(OWN, 16, 128)
            dst[pl.ds(own_level + shift, OWN), tile_row : tile_row + 16, :] = field
        field = unit * sound_ref[...].reshape(OWN, 16, 128)
        c_ref[pl.ds(own_level, OWN), tile_row : tile_row + 16, :] = field
        near_factor, far_factor = (0, 2) if sec == 0 else (2, 0)
        for step in range(SUBSTEPS):
            old, new = (pa, pb) if step % 2 == 0 else (pb, pa)

            def body(i, _, step=step, old=old, new=new):
                k = i * CHUNK
                levels = pl.ds(k, CHUNK)
                inner = pl.ds(k + 2, CHUNK)
                first, last = WIND_BLOCKS[step]
                wide = slice(BLK + BLK * first, BLK + BLK * last)
                slopes = across(old[inner, wide, :], matrix)
                for block in range(first, last):
                    row = BLK + BLK * block
                    rows = slice(row, row + BLK)
                    c = c_ref[levels, rows, :]
                    u[levels, rows, :] = u[levels, rows, :] - c * along(old, inner, row)
                    at = BLK * (block - first)
                    v[levels, rows, :] = v[levels, rows, :] - c * slopes[:, at : at + BLK, :]
                first, last = MASS_BLOCKS[step]
                narrow = slice(BLK + BLK * first, BLK + BLK * last)
                slopes = across(v[levels, narrow, :], matrix)
                for block in range(first, last):
                    row = BLK + BLK * block
                    rows = slice(row, row + BLK)
                    at = BLK * (block - first)
                    spread_uv = along(u, levels, row) + slopes[:, at : at + BLK, :]
                    new[inner, rows, :] = vertical(old, k, row) - c_ref[levels, rows, :] * spread_uv
                for edge, f in ((near_edge, near_factor), (far_edge, far_factor))[: 2 if step < 2 else 1]:
                    rows = slice(edge - 4, edge + 4)
                    delta = factor_ref[f] * u[levels, rows, :] - factor_ref[f + 1] * v[levels, rows, :]
                    new[inner, rows, :] = new[inner, rows, :] - c_ref[levels, rows, :] * crossing(delta, masks)
                return 0

            lax.fori_loop(*chunk_range(step, lev), body, 0)
        final = pa if SUBSTEPS % 2 == 0 else pb
        mine = slice(BLK * sec, BLK * sec + BLK)
        for n, (src, shift) in enumerate(((final, 2), (u, 0), (v, 0))):
            evolved = src[pl.ds(own_level + shift, OWN), 3 * BLK : 4 * BLK, :]
            goal = target_ref[n * OWN * 16 : (n + 1) * OWN * 16, :].reshape(OWN, 16, 128)[:, mine, :]
            packed = slice(n * FIELD, (n + 1) * FIELD)
            resid = evolved.reshape(FIELD, 128) + tendency_ref[packed, :] - goal.reshape(FIELD, 128)
            resid_ref[packed, :] = resid
            rows_ref[packed, :] = resid.astype(BF)

    for sec in range(2):
        pl.when(section == sec)(lambda sec=sec: run(sec))
    for r in range(BLK):
        column_ref[r * GROUP : (r + 1) * GROUP, :] = column_rows(resid_ref, r, 0, BLK, FIELD, 0.0)
    for n in range(3):
        start = pl.multiple_of(n * FIELD + (FIELD - RIM) * (1 - lev), 16)
        rim = rows_ref[pl.ds(start, RIM), :]
        edge_ref[n * RIM : (n + 1) * RIM, :] = rim
        column_ref[BLK * GROUP + n * RIM : BLK * GROUP + (n + 1) * RIM, :] = rim


def adjoint_kernel(
    resid_ref, other_ref, input_grad_ref, c_ref, factor_ref,
    a, b, a_edge, b_edge, partner, partner_edge, own_col, other_col,
    out_ref, pa, pb, u, v, matrix, w,
):
    section, lev = lax.axis_index("sec"), lax.axis_index("lev")
    odd = lax.rem(lax.axis_index("tile"), 2) == 1
    own_level = EDGE * lev
    for ref in (pa, pb, u, v, w):
        clear(ref)
    clear_levels(pa)
    clear_levels(pb)
    masks = edge_masks()
    matrix[...] = across_matrix()
    whole = pl.ds(0, CHUNK)

    def run(sec):
        spread_rims(
            sec, lev, odd, a, b, a_edge, b_edge, partner, partner_edge, own_col, other_col,
            ((pa, 2, None), (u, 0, None), (v, 0, None)),
        )
        _, other_row, near_edge, far_edge = static_rows(sec)
        for n, (dst, shift) in enumerate(((pa, 2), (u, 0), (v, 0))):
            at = pl.ds(own_level + shift, OWN)
            packed = slice(n * FIELD, (n + 1) * FIELD)
            dst[at, 3 * BLK : 4 * BLK, :] = resid_ref[packed, :].reshape(OWN, BLK, 128)
            dst[at, other_row : other_row + BLK, :] = other_ref[packed, :].reshape(OWN, BLK, 128)
        near_factor, far_factor = (0, 2) if sec == 0 else (2, 0)
        for step in range(SUBSTEPS):
            old, new = (pa, pb) if step % 2 == 0 else (pb, pa)
            first, last = WIND_BLOCKS[step]
            wide = slice(BLK + BLK * max(first - 1, 0), BLK + BLK * min(last + 1, 5))
            first, last = MASS_BLOCKS[step]
            narrow = slice(BLK + BLK * max(first - 1, 0), BLK + BLK * min(last + 1, 5))

            def body(i, _, step=step, old=old, new=new, wide=wide, narrow=narrow):
                k = i * CHUNK
                levels = pl.ds(k, CHUNK)
                inner = pl.ds(k + 2, CHUNK)
                w[:, wide, :] = c_ref[levels, wide, :] * old[inner, wide, :]
                first, last = WIND_BLOCKS[step]
                slopes = across(w[:, BLK + BLK * first : BLK + BLK * last, :], matrix)
                for block in range(first, last):
                    row = BLK + BLK * block
                    rows = slice(row, row + BLK)
                    u[levels, rows, :] = u[levels, rows, :] + along(w, whole, row)
                    at = BLK * (block - first)
                    v[levels, rows, :] = v[levels, rows, :] + slopes[:, at : at + BLK, :]
                for edge, f in ((near_edge, near_factor), (far_edge, far_factor))[: 2 if step < 2 else 1]:
                    rows = slice(edge - 4, edge + 4)
                    cross = crossing(w[:, rows, :], masks)
                    u[levels, rows, :] = u[levels, rows, :] + factor_ref[f] * cross
                    v[levels, rows, :] = v[levels, rows, :] - factor_ref[f + 1] * cross
                w[:, narrow, :] = c_ref[levels, narrow, :] * u[levels, narrow, :]
                first, last = MASS_BLOCKS[step]
                rows = slice(BLK + BLK * first, BLK + BLK * last)
                slopes = across(c_ref[levels, rows, :] * v[levels, rows, :], matrix)
                for block in range(first, last):
                    row = BLK + BLK * block
                    at = BLK * (block - first)
                    spread_uv = along(w, whole, row) + slopes[:, at : at + BLK, :]
                    new[inner, row : row + BLK, :] = vertical(old, k, row) + spread_uv
                return 0

            lax.fori_loop(*chunk_range(step, lev), body, 0)

    for sec in range(2):
        pl.when(section == sec)(lambda sec=sec: run(sec))
    final = pa if SUBSTEPS % 2 == 0 else pb
    for n, (src, shift) in enumerate(((final, 2), (u, 0), (v, 0))):
        packed = slice(n * FIELD, (n + 1) * FIELD)
        adjoint = src[pl.ds(own_level + shift, OWN), 3 * BLK : 4 * BLK, :].reshape(FIELD, 128)
        out_ref[packed, :] = adjoint + input_grad_ref[packed, :]


def dot(left, right):
    return lax.dot_general(left, right, (((1,), (0,)), ((), ())), preferred_element_type=F32)


def dot_columns(left, right):
    return lax.dot_general(left, right, (((1,), (1,)), ((), ())), preferred_element_type=F32)


def silu_and_slope(values):
    sigma = 0.5 * jnp.tanh(0.5 * values) + 0.5
    silu = values * sigma
    return silu.astype(BF), sigma + silu * (1.0 - sigma)


def both_groups(out_ref, own_ref, other_ref):
    for r in range(BLK):
        cols = slice(r * 128, (r + 1) * 128)
        out_ref[:GROUP, cols] = own_ref[r * GROUP : (r + 1) * GROUP, :]
        out_ref[GROUP:, cols] = other_ref[r * GROUP : (r + 1) * GROUP, :]


def to_fields(out_ref, start, values):
    for r in range(values.shape[1] // 128):
        for n in range(3):
            rows = pl.ds(n * FIELD + start // 128 + r, OWN, stride=BLK)
            out_ref[rows, :] = values[n * OWN : (n + 1) * OWN, r * 128 : (r + 1) * 128]


def network_kernel(
    own_ref, other_ref, first_t_ref, bias_ref, second_t_ref, third_t_ref,
    feat_ref, one_ref, two_ref, slope_one_ref, slope_two_ref, tendency_ref,
):
    both_groups(feat_ref, own_ref, other_ref)
    for start in range(0, COLS, STRIPE):
        cols = slice(start, start + STRIPE)
        one, slope = silu_and_slope(dot(first_t_ref[...], feat_ref[:, cols]) + bias_ref[...])
        one_ref[:, cols] = one
        slope_one_ref[:, cols] = slope
        two, slope = silu_and_slope(dot(second_t_ref[...], one))
        two_ref[:, cols] = two
        slope_two_ref[:, cols] = slope
        to_fields(tendency_ref, start, dot(third_t_ref[:GROUP, :], two))


def unit_gradients(out_ref, start, feat_ref, resid_ref, one_ref, two_ref, err_one_ref, err_two_ref):
    units = pl.ds(pl.multiple_of(start, 128), 128)
    feats, hid = feat_ref.shape[0], one_ref.shape[0]
    out_ref[:feats, :] = dot_columns(feat_ref[...], err_one_ref[units, :])
    out_ref[feats : feats + hid, :] = dot_columns(one_ref[...], err_two_ref[units, :])
    out_ref[feats + hid :, :] = dot_columns(resid_ref[...], two_ref[units, :])


def back_kernel(
    own_ref, other_ref, feat_ref, third_ref, second_ref, one_ref, two_ref, slope_one_ref, slope_two_ref,
    resid_ref, err_one_ref, err_two_ref, given_ref,
):
    both_groups(resid_ref, own_ref, other_ref)
    for start in range(0, COLS, STRIPE):
        cols = slice(start, start + STRIPE)
        err_two = (dot(third_ref[...], resid_ref[:, cols]) * slope_two_ref[:, cols]).astype(BF)
        err_two_ref[:, cols] = err_two
        err_one_ref[:, cols] = (dot(second_ref[...], err_two) * slope_one_ref[:, cols]).astype(BF)
    start = 256 * lax.axis_index("lev") + 128 * (1 - lax.axis_index("sec"))
    unit_gradients(given_ref, start, feat_ref, resid_ref, one_ref, two_ref, err_one_ref, err_two_ref)


def kept_kernel(
    resid_ref, feat_ref, first_ref, one_ref, two_ref, err_one_ref, err_two_ref, kept_ref, input_grad_ref
):
    start = 256 * lax.axis_index("lev") + 128 * lax.axis_index("sec")
    unit_gradients(kept_ref, start, feat_ref, resid_ref, one_ref, two_ref, err_one_ref, err_two_ref)
    for start in range(0, COLS, STRIPE):
        to_fields(input_grad_ref, start, dot(first_ref[:GROUP, :], err_one_ref[:, start : start + STRIPE]))


def spread_gradients_kernel(own_ref, partner_ref, first_ref, bias_ref, second_ref, third_t_ref):
    section = lax.axis_index("sec")
    hid = second_ref.shape[0]
    share = own_ref.shape[1]

    def feature_rows(out, row, lanes, lev, values):
        group, at = divmod(row, GROUP)
        if at < 3 * OWN:
            field, level = divmod(at, OWN)
            to = (2 * field + (lev + group) % 2) * OWN + level
            out[to : to + 8, lanes] = values

    def run(sec):
        for tile in range(own_ref.shape[0] // 2):
            for part in range(0, share, 8):
                row = tile * share + part
                for lev in range(2):
                    for core, src in ((sec, own_ref), (1 - sec, partner_ref)):
                        lanes = slice(256 * lev + 128 * core, 256 * lev + 128 * core + 128)
                        values = src[2 * tile + lev, part : part + 8, :]
                        if row < 2 * GROUP:
                            feature_rows(first_ref, row, lanes, lev, values)
                            if row == 3 * OWN:
                                bias_ref[:, lanes] = values
                        elif row < 2 * GROUP + hid:
                            second_ref[row - 2 * GROUP : row - 2 * GROUP + 8, lanes] = values
                        else:
                            feature_rows(third_t_ref, row - 2 * GROUP - hid, lanes, lev, values)

    for sec in range(2):
        pl.when(section == sec)(lambda sec=sec: run(sec))


def call(kernel, n_smem, operands, outs, scratch=(), flops=0, moved=0):
    def whole(value):
        return pl.BlockSpec(value.shape, lambda i: (0,) * len(value.shape), pipeline_mode=pl.Buffered(1))

    smem = pl.BlockSpec(memory_space=pltpu.SMEM)
    return pl.pallas_call(
        kernel,
        grid=(1,),
        out_shape=outs,
        in_specs=[smem] * n_smem + [whole(value) for value in operands[n_smem:]],
        out_specs=jax.tree.map(whole, outs),
        scratch_shapes=list(scratch),
        compiler_params=pltpu.CompilerParams(vmem_limit_bytes=60 * MIB),
        cost_estimate=pl.CostEstimate(flops=flops, bytes_accessed=moved, transcendentals=0),
    )(*operands)


def stencil_scratch(extra=()):
    mass = pltpu.VMEM((EXT + 4, ROWS, 128), F32)
    wind = pltpu.VMEM((EXT, ROWS, 128), F32)
    return [mass, mass, wind, wind, pltpu.VMEM((256, 128), BF), *extra]


def shape(*dims, dtype=F32):
    return jax.ShapeDtypeStruct(dims, dtype)


def swap(value, axis):
    return lax.ppermute(value, axis, [(0, 1), (1, 0)])


def strip_swaps(value, edges, tiles):
    first = [(t, t ^ 1) for t in range(tiles)]
    second = [(t, ((t + 1) ^ 1) - 1) for t in range(1, tiles - 1)]

    def cross(pairs):
        return [(2 * a + lev, 2 * b + 1 - lev) for a, b in pairs for lev in range(2)]

    return (
        lax.ppermute(value, "tile", first),
        lax.ppermute(value, "tile", second),
        lax.ppermute(edges, ("tile", "lev"), cross(first)),
        lax.ppermute(edges, ("tile", "lev"), cross(second)),
    )


def local(state, sound, target, edge_turn, w_first, b_first, w_second, w_third):
    sec, lev = lax.axis_index("sec"), lax.axis_index("lev")
    tiles = lax.axis_size("tile")
    hid, feats = w_second.shape[0], 2 * GROUP
    odd = lax.rem(lax.axis_index("tile"), 2) == 1
    second_swap = (sec == 0) == odd

    def by_group(weights):
        weights = weights.reshape(3, 2, OWN, hid).transpose(1, 0, 2, 3).reshape(2, 3 * OWN, hid)
        weights = jnp.pad(weights, ((0, 0), (0, PAD), (0, 0)))
        weights = jnp.where(lev == 0, weights, weights[::-1])
        return weights.reshape(feats, hid)

    state, sound, target = state.reshape(-1, 128), sound.reshape(-1, 128), target.reshape(-1, 128)
    rows, edges, columns = call(
        pack_kernel, 1, (edge_turn, state, sound),
        (shape(4 * FIELD + 16, 128, dtype=BF), shape(4 * RIM, 128, dtype=BF), shape(BLK * GROUP + 4 * RIM, 128, dtype=BF)),
    )
    own_col = swap(columns, "lev")
    a, b, a_edge, b_edge = strip_swaps(rows, edges, tiles)

    first, third_t = by_group(w_first), by_group(w_third.T)
    feat, one, two, slope_one, slope_two, tendency = call(
        network_kernel, 0, (columns, own_col, first.T, b_first[:, None], w_second.T, third_t),
        (shape(feats, COLS, dtype=BF), shape(hid, COLS, dtype=BF), shape(hid, COLS, dtype=BF), shape(hid, COLS), shape(hid, COLS), shape(3 * FIELD, 128)),
    )

    a, b, a_edge, b_edge, tendency = lax.optimization_barrier((a, b, a_edge, b_edge, tendency))
    partner = swap(jnp.where(second_swap, b, a), "sec")
    partner_edge = swap(jnp.where(second_swap, b_edge, a_edge), "sec")
    other_col = swap(own_col, "sec")
    resid, r_rows, r_edges, r_columns, coeff, factors = call(
        forward_kernel, 1,
        (edge_turn, state, sound, target, tendency, a, b, a_edge, b_edge, partner, partner_edge, own_col, other_col),
        (shape(3 * FIELD, 128), shape(3 * FIELD, 128, dtype=BF), shape(3 * RIM, 128, dtype=BF), shape(BLK * GROUP + 3 * RIM, 128, dtype=BF), shape(EXT, ROWS, 128), shape(4, BLK, 128)),
        stencil_scratch(), moved=20_000_000,
    )

    r_own_col = swap(r_columns, "lev")
    r_other = swap(resid, "sec")
    r_a, r_b, r_a_edge, r_b_edge = strip_swaps(r_rows, r_edges, tiles)

    r_own_col, r_a, r_b, r_a_edge, r_b_edge = lax.optimization_barrier((r_own_col, r_a, r_b, r_a_edge, r_b_edge))

    n_rows = 2 * feats + hid
    resid_cols, err_one, err_two, given = call(
        back_kernel, 0, (r_columns, r_own_col, feat, third_t.T, w_second, one, two, slope_one, slope_two),
        (shape(feats, COLS, dtype=BF), shape(hid, COLS, dtype=BF), shape(hid, COLS, dtype=BF), shape(n_rows, 128)),
    )
    received = swap(given, "sec")
    kept, input_grad = call(
        kept_kernel, 0, (resid_cols, feat, first, one, two, err_one, err_two),
        (shape(n_rows, 128), shape(3 * FIELD, 128)),
    )
    share = n_rows // tiles
    partial = (kept + received).astype(BF).reshape(tiles, share, 128)
    parts = lax.all_to_all(partial, "tile", 0, 0)
    total = jnp.sum(parts.astype(F32), axis=0) / (COLS * 2 * tiles)
    everywhere = jnp.broadcast_to(total[None], (2 * tiles, share, 128))
    gathered = lax.all_to_all(everywhere, ("tile", "lev"), 0, 0)

    r_partner = swap(jnp.where(second_swap, r_b, r_a), "sec")
    r_partner_edge = swap(jnp.where(second_swap, r_b_edge, r_a_edge), "sec")
    r_other_col = swap(r_own_col, "sec")
    mine = call(
        adjoint_kernel, 0,
        (resid, r_other, input_grad, coeff, factors, r_a, r_b, r_a_edge, r_b_edge, r_partner, r_partner_edge, r_own_col, r_other_col),
        shape(3 * FIELD, 128), stencil_scratch((pltpu.VMEM((CHUNK, ROWS, 128), F32),)), moved=20_000_000,
    )
    mine, gathered = lax.optimization_barrier((mine, gathered))
    theirs = swap(mine, "sec")
    mine, theirs = mine.reshape(3, OWN, BLK, 128), theirs.reshape(3, OWN, BLK, 128)
    state_grad = jnp.concatenate(
        [jnp.where(sec == 0, mine, theirs), jnp.where(sec == 0, theirs, mine)], axis=2
    )
    g_first, g_bias, g_second, g_third_t = call(
        spread_gradients_kernel, 0, (gathered, swap(gathered, "sec")),
        (shape(6 * OWN, hid), shape(8, hid), shape(hid, hid), shape(6 * OWN, hid)),
    )
    return (state_grad, g_first, g_bias[0], g_second, g_third_t.T)


def solution(mesh):
    placed = (
        P(None, "lev", "tile", None),
        P("lev", "tile", None),
        P(None, "lev", "tile", None),
        P("tile", None),
        P(),
        P(),
        P(),
        P(),
    )
    return jax.shard_map(
        local,
        mesh=mesh,
        in_specs=placed,
        out_specs=(P(None, "lev", "tile", None), P(), P(), P(), P()),
        check_vma=False,
    )
```

```python
import jax
import jax.numpy as jnp
from jax import lax
from jax.experimental import pallas as pl
from jax.experimental.pallas import tpu as pltpu
from jax.sharding import PartitionSpec as P

SUBSTEPS = 4
COURANT = 0.3
DIFFUSION = 0.08
UNIT = 1.0 / 12.0

BLK = 8
OWN = 40
EDGE = 8
EXT = OWN + EDGE
ROWS = 7 * BLK
CHUNK = 24
WIND_BLOCKS = ((0, 5), (0, 5), (1, 4), (1, 4))
MASS_BLOCKS = ((0, 5), (1, 4), (1, 4), (2, 3))
FIELD = OWN * BLK
RIM = EDGE * BLK
COLS = BLK * 128
GROUP = 128
PAD = GROUP - 3 * OWN
STRIPE = 512
MIB = 1024 * 1024
LONG = 20_000_000_000
F32 = jnp.float32
BF = jnp.bfloat16


def roll(values, steps, axis):
    return pltpu.roll(values, steps % values.shape[axis], axis)


def across_matrix():
    source = lax.broadcasted_iota(jnp.int32, (256, 128), 0)
    target = lax.broadcasted_iota(jnp.int32, (256, 128), 1)
    apart = (source - target) & 127
    near = jnp.where(apart == 1, 8.0, 0.0) - jnp.where(apart == 127, 8.0, 0.0)
    far = jnp.where(apart == 126, 1.0, 0.0) - jnp.where(apart == 2, 1.0, 0.0)
    return (near + far).astype(BF)


def across(values, matrix):
    flat = values.reshape(-1, 128)
    high = flat.astype(BF)
    low = (flat - high.astype(F32)).astype(BF)
    return dot(jnp.concatenate([high, low], axis=1), matrix[...]).reshape(values.shape)


def along(ref, levels, row):
    def take(steps):
        return ref[levels, row + steps : row + steps + BLK, :]

    return 8.0 * (take(1) - take(-1)) - (take(2) - take(-2))


def vertical(ref, k, row):
    v = ref[pl.ds(k, CHUNK + 4), row : row + BLK, :]
    near = v[3 : 3 + CHUNK] + v[1 : 1 + CHUNK]
    far = v[4 : 4 + CHUNK] + v[0:CHUNK]
    return (1.0 - 30.0 * UNIT * DIFFUSION) * v[2 : 2 + CHUNK] + (UNIT * DIFFUSION) * (16.0 * near - far)


def edge_masks():
    i = lax.broadcasted_iota(jnp.int32, (1, BLK, 128), 1)

    def at(row, value):
        return jnp.where(i == row, value, 0.0)

    return at(4, -8.0), at(4, 1.0) + at(5, 1.0), at(3, 8.0), at(3, -1.0) + at(2, -1.0)


def crossing(values, masks):
    m1, m2, m3, m4 = masks
    return (
        m1 * roll(values, 1, 1)
        + m2 * roll(values, 2, 1)
        + m3 * roll(values, -1, 1)
        + m4 * roll(values, -2, 1)
    )


def quarter_turn(quarter):
    cosine = jnp.where(quarter == 0, 1.0, 0.0) - jnp.where(quarter == 2, 1.0, 0.0)
    sine = jnp.where(quarter == 1, 1.0, 0.0) - jnp.where(quarter == 3, 1.0, 0.0)
    return cosine, sine


def clear(ref):
    levels = ref.shape[0]
    zeros = jnp.zeros((levels, BLK, 128), F32)
    ref[:, 0:BLK, :] = zeros
    ref[:, ROWS - BLK : ROWS, :] = zeros


def clear_levels(ref):
    for level in (0, 1, EXT + 2, EXT + 3):
        ref[level] = jnp.zeros((ROWS, 128), F32)


def spread(src, start, count, dst, level, row, scale=None):
    def body(i, _):
        rows = src[pl.ds(pl.multiple_of(start + i * 16, 16), 16), :].astype(F32)
        if scale is not None:
            rows = rows * scale
        dst[pl.ds(level + 2 * i, 2), row : row + BLK, :] = rows.reshape(2, BLK, 128)
        return 0

    lax.fori_loop(0, count // 2, body, 0, unroll=4)


def static_rows(sec):
    return 32 - 16 * sec, 24 + 8 * sec, 40 - 24 * sec


def spread_rims(sec, lev, near, far, partner, rims, partner_rims, own_edge, other_edge, fields):
    own_level, edge_level = EDGE * lev, OWN * (1 - lev)
    count = len(fields)
    rows = (8, 16, 40) if sec == 0 else (40, 32, 8)
    sources = ((far, rims, count * RIM, rows[0]), (near, rims, 0, rows[1]), (partner, partner_rims, 0, rows[2]))
    for n, (dst, shift, scale) in enumerate(fields):
        for src, edge, start, row in sources:
            spread(src, n * FIELD, OWN, dst, own_level + shift, row, scale)
            spread(edge, start + n * RIM, EDGE, dst, edge_level + shift, row, scale)
        for (edge, start), row in ((own_edge, 3 * BLK), (other_edge, static_rows(sec)[0])):
            spread(edge, start + n * RIM, EDGE, dst, edge_level + shift, row, scale)


def chunk_range(step, lev):
    trim = 2 * step // CHUNK
    return trim * lev, EXT // CHUNK - trim * (1 - lev)


def column_rows(ref, row, start, stride, step, fill):
    fields = [ref[pl.ds(n * step + start + row, OWN, stride=stride), :] for n in range(3)]
    return jnp.concatenate([*fields, jnp.full((PAD, 128), fill, F32)], axis=0).astype(BF)


def by_group(out_ref, weights_ref, lev, bias_ref=None):
    hid = out_ref.shape[1]
    values = weights_ref[...].astype(F32)
    padding = jnp.zeros((PAD, hid), F32)
    own_padding = padding
    if bias_ref is not None:
        rest = bias_ref[...]
        row = lax.broadcasted_iota(jnp.int32, (PAD, hid), 0)
        for n in range(3):
            part = rest.astype(BF).astype(F32)
            own_padding = jnp.where(row == n, part, own_padding)
            rest = rest - part
    groups = [[values[(2 * n + g) * OWN : (2 * n + g + 1) * OWN] for n in range(3)] for g in range(2)]
    for group in range(2):

        def run(group=group):
            parts = [*groups[group], own_padding, *groups[1 - group], padding]
            out_ref[...] = jnp.concatenate(parts, axis=0).astype(BF)

        pl.when(lev == group)(run)


def pack_kernel(
    turn_ref, state_ref, sound_ref, first_ref, third_t_ref, bias_ref,
    near_ref, far_ref, edge_ref, column_ref, first_out_ref, third_out_ref,
):
    sec, lev = lax.axis_index("sec"), lax.axis_index("lev")
    by_group(first_out_ref, first_ref, lev, bias_ref)
    by_group(third_out_ref, third_t_ref, lev)
    for half in range(2):

        def run(half=half):
            for n in range(4):
                src = state_ref[n * OWN * 16 : (n + 1) * OWN * 16, :] if n < 3 else sound_ref[...]
                for out, block in ((near_ref, half), (far_ref, 1 - half)):
                    field = src.reshape(OWN, 16, 128)[:, block * BLK : block * BLK + BLK, :]
                    out[n * FIELD : (n + 1) * FIELD, :] = field.reshape(FIELD, 128).astype(BF)
            for r in range(BLK):
                features = column_rows(state_ref, r, BLK * half, 16, OWN * 16, 1.0)
                column_ref[r * GROUP : (r + 1) * GROUP, :] = features

        pl.when(sec == half)(run)
    for n in range(4):
        start = pl.multiple_of(n * FIELD + (FIELD - RIM) * (1 - lev), 16)
        edge_ref[n * RIM : (n + 1) * RIM, :] = near_ref[pl.ds(start, RIM), :]
        edge_ref[(4 + n) * RIM : (5 + n) * RIM, :] = far_ref[pl.ds(start, RIM), :]
    column_ref[BLK * GROUP :, :] = edge_ref[...]
    i = lax.broadcasted_iota(jnp.int32, (16, 128), 0)
    factors = jnp.zeros((16, 128), F32)
    for n, value in enumerate((*quarter_turn(turn_ref[0, 0]), *quarter_turn(turn_ref[0, 1]))):
        factors = jnp.where(i == n, value, factors)
    near_ref[4 * FIELD :, :] = factors.astype(BF)


def forward_kernel(
    turn_ref, state_ref, sound_ref, target_ref, tendency_ref,
    near, far, partner, rims, partner_rims, own_col,
    resid_ref, rows_ref, edge_ref, column_ref, c_ref, factor_ref, pa, pb, u, v, matrix,
):
    section, lev = lax.axis_index("sec"), lax.axis_index("lev")
    own_level = EDGE * lev
    for ref in (pa, pb, u, v, c_ref):
        clear(ref)
    clear_levels(pa)
    clear_levels(pb)
    cos_low, sin_low = quarter_turn(turn_ref[0, 0])
    cos_high, sin_high = quarter_turn(turn_ref[0, 1])
    below = lax.broadcasted_iota(jnp.int32, (BLK, 128), 0) < 4

    def factors(low, high):
        low = low[4 * FIELD :, :].astype(F32)
        high = high[4 * FIELD :, :].astype(F32)
        factor_ref[0] = jnp.where(below, cos_low, low[2:3, :]) - 1.0
        factor_ref[1] = jnp.where(below, sin_low, low[3:4, :])
        factor_ref[2] = jnp.where(below, high[0:1, :], cos_high) - 1.0
        factor_ref[3] = jnp.where(below, high[1:2, :], sin_high)

    pl.when(section == 0)(lambda: factors(near, partner))
    pl.when(section == 1)(lambda: factors(partner, near))
    masks = edge_masks()
    matrix[...] = across_matrix()

    def run(sec):
        unit = COURANT * UNIT
        spread_rims(
            sec, lev, near, far, partner, rims, partner_rims,
            (own_col, BLK * GROUP), (own_col, BLK * GROUP + 4 * RIM),
            ((pa, 2, None), (u, 0, None), (v, 0, None), (c_ref, 0, unit)),
        )
        _, near_edge, far_edge = static_rows(sec)
        tile_row = 24 - 8 * sec
        for n, (dst, shift) in enumerate(((pa, 2), (u, 0), (v, 0))):
            field = state_ref[n * OWN * 16 : (n + 1) * OWN * 16, :].reshape(OWN, 16, 128)
            dst[pl.ds(own_level + shift, OWN), tile_row : tile_row + 16, :] = field
        field = unit * sound_ref[...].reshape(OWN, 16, 128)
        c_ref[pl.ds(own_level, OWN), tile_row : tile_row + 16, :] = field
        near_factor, far_factor = (0, 2) if sec == 0 else (2, 0)
        for step in range(SUBSTEPS):
            old, new = (pa, pb) if step % 2 == 0 else (pb, pa)

            def body(i, _, step=step, old=old, new=new):
                k = i * CHUNK
                levels = pl.ds(k, CHUNK)
                inner = pl.ds(k + 2, CHUNK)
                first, last = WIND_BLOCKS[step]
                wide = slice(BLK + BLK * first, BLK + BLK * last)
                slopes = across(old[inner, wide, :], matrix)
                for block in range(first, last):
                    row = BLK + BLK * block
                    rows = slice(row, row + BLK)
                    c = c_ref[levels, rows, :]
                    u[levels, rows, :] = u[levels, rows, :] - c * along(old, inner, row)
                    at = BLK * (block - first)
                    v[levels, rows, :] = v[levels, rows, :] - c * slopes[:, at : at + BLK, :]
                first, last = MASS_BLOCKS[step]
                narrow = slice(BLK + BLK * first, BLK + BLK * last)
                slopes = across(v[levels, narrow, :], matrix)
                for block in range(first, last):
                    row = BLK + BLK * block
                    rows = slice(row, row + BLK)
                    at = BLK * (block - first)
                    spread_uv = along(u, levels, row) + slopes[:, at : at + BLK, :]
                    new[inner, rows, :] = vertical(old, k, row) - c_ref[levels, rows, :] * spread_uv
                for edge, f in ((near_edge, near_factor), (far_edge, far_factor))[: 2 if step < 2 else 1]:
                    rows = slice(edge - 4, edge + 4)
                    delta = factor_ref[f] * u[levels, rows, :] - factor_ref[f + 1] * v[levels, rows, :]
                    new[inner, rows, :] = new[inner, rows, :] - c_ref[levels, rows, :] * crossing(delta, masks)
                return 0

            lax.fori_loop(*chunk_range(step, lev), body, 0)
        final = pa if SUBSTEPS % 2 == 0 else pb
        mine = slice(BLK * sec, BLK * sec + BLK)
        for n, (src, shift) in enumerate(((final, 2), (u, 0), (v, 0))):
            evolved = src[pl.ds(own_level + shift, OWN), 3 * BLK : 4 * BLK, :]
            goal = target_ref[n * OWN * 16 : (n + 1) * OWN * 16, :].reshape(OWN, 16, 128)[:, mine, :]
            packed = slice(n * FIELD, (n + 1) * FIELD)
            resid = evolved.reshape(FIELD, 128) + tendency_ref[packed, :] - goal.reshape(FIELD, 128)
            resid_ref[packed, :] = resid
            rows_ref[packed, :] = resid.astype(BF)

    for sec in range(2):
        pl.when(section == sec)(lambda sec=sec: run(sec))
    for r in range(BLK):
        column_ref[r * GROUP : (r + 1) * GROUP, :] = column_rows(resid_ref, r, 0, BLK, FIELD, 0.0)
    for n in range(3):
        start = pl.multiple_of(n * FIELD + (FIELD - RIM) * (1 - lev), 16)
        rim = rows_ref[pl.ds(start, RIM), :]
        edge_ref[n * RIM : (n + 1) * RIM, :] = rim
        column_ref[BLK * GROUP + n * RIM : BLK * GROUP + (n + 1) * RIM, :] = rim


def adjoint_kernel(
    resid_ref, other_ref, input_grad_ref, c_ref, factor_ref,
    near, far, partner, rims, partner_rims, own_col, other_col,
    out_ref, pa, pb, u, v, matrix, w,
):
    section, lev = lax.axis_index("sec"), lax.axis_index("lev")
    own_level = EDGE * lev
    for ref in (pa, pb, u, v, w):
        clear(ref)
    clear_levels(pa)
    clear_levels(pb)
    masks = edge_masks()
    matrix[...] = across_matrix()
    whole = pl.ds(0, CHUNK)

    def run(sec):
        spread_rims(
            sec, lev, near, far, partner, rims, partner_rims,
            (own_col, BLK * GROUP), (other_col, BLK * GROUP),
            ((pa, 2, None), (u, 0, None), (v, 0, None)),
        )
        other_row, near_edge, far_edge = static_rows(sec)
        for n, (dst, shift) in enumerate(((pa, 2), (u, 0), (v, 0))):
            at = pl.ds(own_level + shift, OWN)
            packed = slice(n * FIELD, (n + 1) * FIELD)
            dst[at, 3 * BLK : 4 * BLK, :] = resid_ref[packed, :].reshape(OWN, BLK, 128)
            dst[at, other_row : other_row + BLK, :] = other_ref[packed, :].reshape(OWN, BLK, 128)
        near_factor, far_factor = (0, 2) if sec == 0 else (2, 0)
        for step in range(SUBSTEPS):
            old, new = (pa, pb) if step % 2 == 0 else (pb, pa)
            first, last = WIND_BLOCKS[step]
            wide = slice(BLK + BLK * max(first - 1, 0), BLK + BLK * min(last + 1, 5))
            first, last = MASS_BLOCKS[step]
            narrow = slice(BLK + BLK * max(first - 1, 0), BLK + BLK * min(last + 1, 5))

            def body(i, _, step=step, old=old, new=new, wide=wide, narrow=narrow):
                k = i * CHUNK
                levels = pl.ds(k, CHUNK)
                inner = pl.ds(k + 2, CHUNK)
                w[:, wide, :] = c_ref[levels, wide, :] * old[inner, wide, :]
                first, last = WIND_BLOCKS[step]
                slopes = across(w[:, BLK + BLK * first : BLK + BLK * last, :], matrix)
                for block in range(first, last):
                    row = BLK + BLK * block
                    rows = slice(row, row + BLK)
                    u[levels, rows, :] = u[levels, rows, :] + along(w, whole, row)
                    at = BLK * (block - first)
                    v[levels, rows, :] = v[levels, rows, :] + slopes[:, at : at + BLK, :]
                for edge, f in ((near_edge, near_factor), (far_edge, far_factor))[: 2 if step < 2 else 1]:
                    rows = slice(edge - 4, edge + 4)
                    cross = crossing(w[:, rows, :], masks)
                    u[levels, rows, :] = u[levels, rows, :] + factor_ref[f] * cross
                    v[levels, rows, :] = v[levels, rows, :] - factor_ref[f + 1] * cross
                w[:, narrow, :] = c_ref[levels, narrow, :] * u[levels, narrow, :]
                first, last = MASS_BLOCKS[step]
                rows = slice(BLK + BLK * first, BLK + BLK * last)
                slopes = across(c_ref[levels, rows, :] * v[levels, rows, :], matrix)
                for block in range(first, last):
                    row = BLK + BLK * block
                    at = BLK * (block - first)
                    spread_uv = along(w, whole, row) + slopes[:, at : at + BLK, :]
                    new[inner, row : row + BLK, :] = vertical(old, k, row) + spread_uv
                return 0

            lax.fori_loop(*chunk_range(step, lev), body, 0)

    for sec in range(2):
        pl.when(section == sec)(lambda sec=sec: run(sec))
    final = pa if SUBSTEPS % 2 == 0 else pb
    for n, (src, shift) in enumerate(((final, 2), (u, 0), (v, 0))):
        packed = slice(n * FIELD, (n + 1) * FIELD)
        adjoint = src[pl.ds(own_level + shift, OWN), 3 * BLK : 4 * BLK, :].reshape(FIELD, 128)
        out_ref[packed, :] = adjoint + input_grad_ref[packed, :]


def dot(left, right):
    return lax.dot_general(left, right, (((1,), (0,)), ((), ())), preferred_element_type=F32)


def dot_t(left, right):
    return lax.dot_general(left, right, (((0,), (0,)), ((), ())), preferred_element_type=F32)


def dot_columns(left, right):
    return lax.dot_general(left, right, (((1,), (1,)), ((), ())), preferred_element_type=F32)


def silu_and_slope(values):
    sigma = 0.5 * jnp.tanh(0.5 * values) + 0.5
    silu = values * sigma
    return silu.astype(BF), sigma + silu * (1.0 - sigma)


def both_groups(own_ref, other_ref):
    parts = [
        jnp.concatenate([ref[r * GROUP : (r + 1) * GROUP, :] for ref in (own_ref, other_ref)], axis=0)
        for r in range(STRIPE // 128)
    ]
    return jnp.concatenate(parts, axis=1)


def to_fields(out_ref, first, values):
    for r in range(STRIPE // 128):
        for n in range(3):
            rows = pl.ds(n * FIELD + first + r, OWN, stride=BLK)
            out_ref[rows, :] = values[n * OWN : (n + 1) * OWN, r * 128 : (r + 1) * 128]


def network_kernel(
    own_ref, other_ref, first_ref, second_ref, third_t_ref,
    feat_ref, one_ref, two_ref, slope_one_ref, slope_two_ref, tendency_ref,
):
    feat = both_groups(own_ref, other_ref)
    feat_ref[...] = feat
    one, slope = silu_and_slope(dot_t(first_ref[...], feat))
    one_ref[...] = one
    slope_one_ref[...] = slope
    two, slope = silu_and_slope(dot_t(second_ref[...], one))
    two_ref[...] = two
    slope_two_ref[...] = slope
    to_fields(tendency_ref, pl.program_id(0) * (STRIPE // 128), dot(third_t_ref[:GROUP, :], two))


def gather_kernel(own_ref, other_ref, out_ref):
    for start in range(0, COLS, STRIPE):
        rows = slice(start // 128 * GROUP, (start + STRIPE) // 128 * GROUP)
        out_ref[:, start : start + STRIPE] = both_groups(own_ref.at[rows, :], other_ref.at[rows, :])


def back_kernel(
    resid_ref, feat_ref, third_t_ref, second_ref, first_ref, one_ref, two_ref, slope_one_ref, slope_two_ref,
    given_ref, kept_ref, input_grad_ref, err_one_ref, err_two_ref, total_ref,
):
    step = pl.program_id(0)
    resid = resid_ref[...]
    err_two = (dot_t(third_t_ref[...], resid) * slope_two_ref[...]).astype(BF)
    err_two_ref[...] = err_two
    err_one = (dot(second_ref[...], err_two) * slope_one_ref[...]).astype(BF)
    err_one_ref[...] = err_one
    to_fields(input_grad_ref, step * (STRIPE // 128), dot(first_ref[:GROUP, :], err_one))
    feats, hid = feat_ref.shape[0], one_ref.shape[0]
    half = pl.ds(pl.multiple_of(256 * lax.axis_index("lev"), 256), 256)

    def clear_total():
        total_ref[...] = jnp.zeros(total_ref.shape, F32)

    pl.when(step == 0)(clear_total)

    def add(rows, left, right):
        total_ref[rows, :] = total_ref[rows, :] + dot_columns(left, right)

    add(slice(0, feats), feat_ref[...], err_one_ref[half, :])
    add(slice(feats, feats + hid), one_ref[...], err_two_ref[half, :])
    add(slice(feats + hid, 2 * feats + hid), resid, two_ref[half, :])

    def finish():
        for sec in range(2):

            def share(sec=sec):
                kept_ref[...] = total_ref[:, 128 * sec : 128 * sec + 128]
                given_ref[...] = total_ref[:, 128 - 128 * sec : 256 - 128 * sec].astype(BF)

            pl.when(lax.axis_index("sec") == sec)(share)

    pl.when(step == COLS // STRIPE - 1)(finish)


def place_rows_kernel(mine_ref, theirs_ref, out_ref):
    for sec in range(2):

        def run(sec=sec):
            for n in range(3):
                packed = slice(n * FIELD, (n + 1) * FIELD)
                for core, ref in ((sec, mine_ref), (1 - sec, theirs_ref)):
                    out_ref[n, :, BLK * core : BLK * core + BLK, :] = ref[packed, :].reshape(OWN, BLK, 128)

        pl.when(lax.axis_index("sec") == sec)(run)


def spread_gradients_kernel(own_ref, partner_ref, first_ref, bias_ref, second_ref, third_t_ref):
    section = lax.axis_index("sec")
    hid = second_ref.shape[0]
    share = own_ref.shape[1]

    def feature_rows(out, row, lanes, lev, values):
        group, at = divmod(row, GROUP)
        if at < 3 * OWN:
            field, level = divmod(at, OWN)
            to = (2 * field + (lev + group) % 2) * OWN + level
            out[to : to + 8, lanes] = values

    def run(sec):
        blocks = [(tile, lev, core) for tile in range(own_ref.shape[0] // 2) for lev in range(2) for core in range(2)]
        for tile, lev, core in blocks:
            lanes = slice(256 * lev + 128 * core, 256 * lev + 128 * core + 128)
            block = (own_ref if core == sec else partner_ref)[2 * tile + lev].astype(F32)
            for part in range(0, share, 8):
                row = tile * share + part
                values = block[part : part + 8, :]
                if row < 2 * GROUP:
                    feature_rows(first_ref, row, lanes, lev, values)
                    if row == 3 * OWN:
                        bias_ref[:, lanes] = values[:1, :]
                elif row < 2 * GROUP + hid:
                    second_ref[row - 2 * GROUP : row - 2 * GROUP + 8, lanes] = values
                else:
                    feature_rows(third_t_ref, row - 2 * GROUP - hid, lanes, lev, values)

    for sec in range(2):
        pl.when(section == sec)(lambda sec=sec: run(sec))


def whole(value):
    return pl.BlockSpec(value.shape, lambda i: (0,) * len(value.shape), pipeline_mode=pl.Buffered(1))


def stripes(value, along):
    if along:
        return pl.BlockSpec((value.shape[0], STRIPE), lambda i: (0, i))
    return pl.BlockSpec((STRIPE // 128 * GROUP, 128), lambda i: (i, 0))


def call(kernel, n_smem, operands, outs, scratch=(), flops=0, steps=1, in_along=None, out_along=None):
    def specs(values, along):
        along = along or [None] * len(values)
        return [whole(v) if at is None else stripes(v, at) for v, at in zip(values, along, strict=True)]

    smem = pl.BlockSpec(memory_space=pltpu.SMEM)
    return pl.pallas_call(
        kernel,
        grid=(steps,),
        out_shape=outs,
        in_specs=[smem] * n_smem + specs(operands[n_smem:], in_along),
        out_specs=specs(outs, out_along),
        scratch_shapes=list(scratch),
        compiler_params=pltpu.CompilerParams(vmem_limit_bytes=60 * MIB),
        cost_estimate=pl.CostEstimate(flops=flops, bytes_accessed=0, transcendentals=0),
    )(*operands)


def stencil_scratch(extra=()):
    mass = pltpu.VMEM((EXT + 4, ROWS, 128), F32)
    wind = pltpu.VMEM((EXT, ROWS, 128), F32)
    return [mass, mass, wind, wind, pltpu.VMEM((256, 128), BF), *extra]


def shape(*dims, dtype=F32):
    return jax.ShapeDtypeStruct(dims, dtype)


def swap(value, axis):
    return lax.ppermute(value, axis, [(0, 1), (1, 0)])


def strip_swaps(near, far, edges, tiles):
    pairs = [(tiles + t, t + 1) for t in range(tiles - 1)]
    pairs += [(b, a) for a, b in pairs]
    cross = [(2 * a + lev, 2 * b + 1 - lev) for a, b in pairs for lev in range(2)]
    return (
        lax.ppermute(near, ("sec", "tile"), pairs),
        lax.ppermute(far, ("sec", "tile"), pairs),
        lax.ppermute(edges, ("sec", "tile", "lev"), cross),
    )


def local(state, sound, target, edge_turn, w_first, b_first, w_second, w_third):
    tiles = lax.axis_size("tile")
    hid, feats = w_second.shape[0], 2 * GROUP

    state, sound, target = state.reshape(-1, 128), sound.reshape(-1, 128), target.reshape(-1, 128)
    near, far, edges, columns, first, third_t = call(
        pack_kernel, 1, (edge_turn, state, sound, w_first, w_third.T, b_first[None]),
        (shape(4 * FIELD + 16, 128, dtype=BF), shape(4 * FIELD, 128, dtype=BF), shape(8 * RIM, 128, dtype=BF), shape(BLK * GROUP + 8 * RIM, 128, dtype=BF), shape(feats, hid, dtype=BF), shape(feats, hid, dtype=BF)),
    )
    own_col = swap(columns, "lev")
    near, far, rims = strip_swaps(near, far, edges, tiles)

    activations = (shape(feats, COLS, dtype=BF), shape(hid, COLS, dtype=BF), shape(hid, COLS, dtype=BF), shape(hid, COLS), shape(hid, COLS))
    feat, one, two, slope_one, slope_two, tendency = call(
        network_kernel, 0, (columns, own_col, first, w_second, third_t),
        (*activations, shape(3 * FIELD, 128)),
        steps=COLS // STRIPE, flops=LONG, in_along=(0, 0, None, None, None), out_along=(1, 1, 1, 1, 1, None),
    )

    near, far, rims, tendency = lax.optimization_barrier((near, far, rims, tendency))
    resid, r_rows, r_edges, r_columns, coeff, factors = call(
        forward_kernel, 1,
        (edge_turn, state, sound, target, tendency, near, far, swap(near, "sec"), rims, swap(rims, "sec"), own_col),
        (shape(3 * FIELD, 128), shape(3 * FIELD, 128, dtype=BF), shape(3 * RIM, 128, dtype=BF), shape(BLK * GROUP + 3 * RIM, 128, dtype=BF), shape(EXT, ROWS, 128), shape(4, BLK, 128)),
        stencil_scratch(), flops=LONG,
    )

    r_own_col = swap(r_columns, "lev")
    r_other = swap(resid, "sec")
    both_edges = jnp.concatenate([r_edges, swap(r_edges, "sec")], axis=0)
    r_near, r_far, r_rims = strip_swaps(r_rows, swap(r_rows, "sec"), both_edges, tiles)
    (resid_cols,) = call(
        gather_kernel, 0, (r_columns, r_own_col), (shape(feats, COLS, dtype=BF),), flops=LONG
    )
    resid_cols, r_near, r_far, r_rims = lax.optimization_barrier((resid_cols, r_near, r_far, r_rims))

    n_rows = 2 * feats + hid
    given, kept, input_grad = call(
        back_kernel, 0, (resid_cols, feat, third_t, w_second, first, one, two, slope_one, slope_two),
        (shape(n_rows, 128, dtype=BF), shape(n_rows, 128), shape(3 * FIELD, 128)),
        (pltpu.VMEM((hid, STRIPE), BF), pltpu.VMEM((hid, STRIPE), BF), pltpu.VMEM((n_rows, 256), F32)),
        flops=LONG, steps=COLS // STRIPE, in_along=(1, 1, None, None, None, 1, 1, 1, 1),
    )
    r_partner, r_partner_rims, r_other_col = swap(r_near, "sec"), swap(r_rims, "sec"), swap(r_own_col, "sec")
    given, r_other, r_partner, r_partner_rims, r_other_col = lax.optimization_barrier(
        (given, r_other, r_partner, r_partner_rims, r_other_col)
    )
    received = swap(given, "sec")
    share = n_rows // tiles
    partial = (kept + received.astype(F32)).astype(BF).reshape(tiles, share, 128)
    parts = lax.all_to_all(partial, "tile", 0, 0)
    total = jnp.sum(parts.astype(F32), axis=0) / (COLS * 2 * tiles)
    (mine,) = call(
        adjoint_kernel, 0,
        (resid, r_other, input_grad, coeff, factors, r_near, r_far, r_partner, r_rims, r_partner_rims, r_own_col, r_other_col),
        (shape(3 * FIELD, 128),), stencil_scratch((pltpu.VMEM((CHUNK, ROWS, 128), F32),)), flops=LONG,
    )
    total, mine = lax.optimization_barrier((total, mine))
    everywhere = jnp.broadcast_to(total.astype(BF)[None], (2 * tiles, share, 128))
    gathered = lax.all_to_all(everywhere, ("tile", "lev"), 0, 0)
    (state_grad,) = call(place_rows_kernel, 0, (mine, swap(mine, "sec")), (shape(3, OWN, 2 * BLK, 128),))
    state_grad, gathered = lax.optimization_barrier((state_grad, gathered))
    g_first, g_bias, g_second, g_third_t = call(
        spread_gradients_kernel, 0, (gathered, swap(gathered, "sec")),
        (shape(6 * OWN, hid), shape(1, hid), shape(hid, hid), shape(6 * OWN, hid)),
    )
    return (state_grad, g_first, g_bias.reshape(hid), g_second, g_third_t.T)


def solution(mesh):
    placed = (
        P(None, "lev", "tile", None),
        P("lev", "tile", None),
        P(None, "lev", "tile", None),
        P("tile", None),
        P(),
        P(),
        P(),
        P(),
    )
    return jax.shard_map(
        local,
        mesh=mesh,
        in_specs=placed,
        out_specs=(P(None, "lev", "tile", None), P(), P(), P(), P()),
        check_vma=False,
    )
```

```python
import jax
import jax.numpy as jnp
from jax import lax
from jax.experimental import pallas as pl
from jax.experimental.pallas import tpu as pltpu
from jax.sharding import PartitionSpec as P

SUBSTEPS = 4
COURANT = 0.3
DIFFUSION = 0.08
UNIT = 1.0 / 12.0

BLK = 8
OWN = 40
EDGE = 8
EXT = OWN + EDGE
ROWS = 7 * BLK
WIND_BLOCKS = ((0, 5), (0, 5), (1, 4), (1, 4))
MASS_BLOCKS = ((0, 5), (1, 4), (1, 4), (2, 3))
FIELD = OWN * BLK
RIM = EDGE * BLK
NEAR_EDGE, FAR_EDGE = 6, 2
COLS = BLK * 128
GROUP = 128
PAD = GROUP - 3 * OWN
STRIPE = 512
MIB = 1024 * 1024
LONG = 20_000_000_000
F32 = jnp.float32
BF = jnp.bfloat16


def roll(values, steps, axis):
    return pltpu.roll(values, steps % values.shape[axis], axis)


def across_matrix():
    source = lax.broadcasted_iota(jnp.int32, (256, 128), 0)
    target = lax.broadcasted_iota(jnp.int32, (256, 128), 1)
    apart = (source - target) & 127
    near = jnp.where(apart == 1, 8.0, 0.0) - jnp.where(apart == 127, 8.0, 0.0)
    far = jnp.where(apart == 126, 1.0, 0.0) - jnp.where(apart == 2, 1.0, 0.0)
    return (near + far).astype(BF)


def across(values, matrix):
    flat = values.reshape(-1, 128)
    high = flat.astype(BF)
    low = (flat - high.astype(F32)).astype(BF)
    return dot(jnp.concatenate([high, low], axis=1), matrix[...]).reshape(values.shape)


def along(ref, levels, row):
    def take(steps):
        return ref[levels, row + steps : row + steps + BLK, :]

    return 8.0 * (take(1) - take(-1)) - (take(2) - take(-2))


def vertical(ref, k, size, row):
    v = ref[pl.ds(k, size + 4), row : row + BLK, :]
    near = v[3 : 3 + size] + v[1 : 1 + size]
    far = v[4 : 4 + size] + v[0:size]
    return (1.0 - 30.0 * UNIT * DIFFUSION) * v[2 : 2 + size] + (UNIT * DIFFUSION) * (16.0 * near - far)


def edge_masks():
    i = lax.broadcasted_iota(jnp.int32, (1, BLK, 128), 1)

    def at(row, value):
        return jnp.where(i == row, value, 0.0)

    return at(4, -8.0), at(4, 1.0) + at(5, 1.0), at(3, 8.0), at(3, -1.0) + at(2, -1.0)


def crossing(values, masks):
    m1, m2, m3, m4 = masks
    return (
        m1 * roll(values, 1, 1)
        + m2 * roll(values, 2, 1)
        + m3 * roll(values, -1, 1)
        + m4 * roll(values, -2, 1)
    )


def quarter_turn(quarter):
    cosine = jnp.where(quarter == 0, 1.0, 0.0) - jnp.where(quarter == 2, 1.0, 0.0)
    sine = jnp.where(quarter == 1, 1.0, 0.0) - jnp.where(quarter == 3, 1.0, 0.0)
    return cosine, sine


def clear(ref):
    levels = ref.shape[0]
    zeros = jnp.zeros((levels, BLK, 128), F32)
    ref[:, 0:BLK, :] = zeros
    ref[:, ROWS - BLK : ROWS, :] = zeros


def clear_levels(ref):
    for level in (0, 1, EXT + 2, EXT + 3):
        ref[level] = jnp.zeros((ROWS, 128), F32)


def spread(src, start, count, dst, level, row, scale=None):
    def body(i, _):
        rows = src[pl.ds(pl.multiple_of(start + i * 16, 16), 16), :].astype(F32)
        if scale is not None:
            rows = rows * scale
        dst[pl.ds(level + 2 * i, 2), row : row + BLK, :] = rows.reshape(2, BLK, 128)
        return 0

    if count > EDGE:
        lax.fori_loop(0, count // 2, body, 0, unroll=20)
    else:
        for i in range(count // 2):
            body(i, 0)


def spread_column_edge(columns, n, dst, level, row, lev, scale=None):
    if n == 3:
        spread(columns, BLK * GROUP, EDGE, dst, level, row, scale)
        return
    skip = n * OWN % 16
    for r in range(BLK):
        start = pl.multiple_of(r * GROUP + n * OWN - skip + (OWN - EDGE) * lev, 16)
        values = columns[pl.ds(start, 16), :].astype(F32)
        dst[pl.ds(level, EDGE), row + r, :] = values[skip : skip + EDGE, :]


def static_rows(sec):
    return 32 - 16 * sec, 24 + 8 * sec, 40 - 24 * sec


def spread_rims(sec, lev, strip, partner, rims, partner_rims, own_col, other_col, fields):
    own_level, edge_level = EDGE * lev, OWN * (1 - lev)
    count = len(fields)
    far_start = strip.shape[0] - count * FIELD
    far_row, near_row, partner_row = (8, 16, 40) if sec == 0 else (40, 32, 8)
    near_level, far_level = edge_level + (EDGE - NEAR_EDGE) * lev, edge_level + (EDGE - FAR_EDGE) * lev
    for n, (dst, shift, scale) in enumerate(fields):
        dst[pl.ds(edge_level + shift, EDGE), :, :] = jnp.zeros((EDGE, ROWS, 128), F32)
        spread(strip, far_start + n * FIELD, OWN, dst, own_level + shift, far_row, scale)
        spread(strip, n * FIELD, OWN, dst, own_level + shift, near_row, scale)
        spread(partner, n * FIELD, OWN, dst, own_level + shift, partner_row, scale)
        spread(rims, n * RIM, NEAR_EDGE, dst, near_level + shift, near_row, scale)
        spread(partner_rims, n * RIM, NEAR_EDGE, dst, near_level + shift, partner_row, scale)
        spread(rims, n * RIM + NEAR_EDGE * BLK, FAR_EDGE, dst, far_level + shift, far_row, scale)
        for columns, row in ((own_col, 3 * BLK), (other_col, static_rows(sec)[0])):
            spread_column_edge(columns, n, dst, edge_level + shift, row, lev, scale)


def column_rows(ref, row, start, stride, step, fill):
    fields = [ref[pl.ds(n * step + start + row, OWN, stride=stride), :] for n in range(3)]
    return jnp.concatenate([*fields, jnp.full((PAD, 128), fill, F32)], axis=0).astype(BF)


def by_group(out_ref, weights_ref, lev, bias_ref=None):
    hid = out_ref.shape[1]
    values = weights_ref[...].astype(F32)
    padding = jnp.zeros((PAD, hid), F32)
    own_padding = padding
    if bias_ref is not None:
        rest = bias_ref[...]
        row = lax.broadcasted_iota(jnp.int32, (PAD, hid), 0)
        for n in range(3):
            part = rest.astype(BF).astype(F32)
            own_padding = jnp.where(row == n, part, own_padding)
            rest = rest - part
    groups = [[values[(2 * n + g) * OWN : (2 * n + g + 1) * OWN] for n in range(3)] for g in range(2)]
    for group in range(2):

        def run(group=group):
            parts = [*groups[group], own_padding, *groups[1 - group], padding]
            out_ref[...] = jnp.concatenate(parts, axis=0).astype(BF)

        pl.when(lev == group)(run)


def corner(edge_ref, n, near_ref, near, far_ref, far, lev):
    for src, start, at, levels in ((near_ref, near, 0, NEAR_EDGE), (far_ref, far, NEAR_EDGE, FAR_EDGE)):
        rows = pl.ds(pl.multiple_of(start + (OWN - levels) * BLK * (1 - lev), 16), levels * BLK)
        edge_ref[n * RIM + at * BLK : n * RIM + (at + levels) * BLK, :] = src[rows, :]


def pack_kernel(
    turn_ref, state_ref, sound_ref, first_ref, third_t_ref, bias_ref,
    strip_ref, edge_ref, column_ref, first_out_ref, third_out_ref,
):
    sec, lev = lax.axis_index("sec"), lax.axis_index("lev")
    by_group(first_out_ref, first_ref, lev, bias_ref)
    by_group(third_out_ref, third_t_ref, lev)
    far_start = 4 * FIELD + 16
    for half in range(2):

        def run(half=half):
            for n in range(4):
                src = state_ref[n * OWN * 16 : (n + 1) * OWN * 16, :] if n < 3 else sound_ref[...]
                for at, block in ((n * FIELD, half), (far_start + n * FIELD, 1 - half)):
                    field = src.reshape(OWN, 16, 128)[:, block * BLK : block * BLK + BLK, :]
                    strip_ref[at : at + FIELD, :] = field.reshape(FIELD, 128).astype(BF)
            for r in range(BLK):
                features = column_rows(state_ref, r, BLK * half, 16, OWN * 16, 1.0)
                column_ref[r * GROUP : (r + 1) * GROUP, :] = features

        pl.when(sec == half)(run)
    for n in range(4):
        near, far = n * FIELD, far_start + n * FIELD
        if n == 3:
            start = pl.multiple_of(near + (FIELD - RIM) * (1 - lev), 16)
            column_ref[BLK * GROUP :, :] = strip_ref[pl.ds(start, RIM), :]
        corner(edge_ref, n, strip_ref, near, strip_ref, far, lev)
    i = lax.broadcasted_iota(jnp.int32, (16, 128), 0)
    factors = jnp.zeros((16, 128), F32)
    for n, value in enumerate((*quarter_turn(turn_ref[0, 0]), *quarter_turn(turn_ref[0, 1]))):
        factors = jnp.where(i == n, value, factors)
    strip_ref[4 * FIELD : far_start, :] = factors.astype(BF)


def forward_kernel(
    turn_ref, state_ref, sound_ref, tendency_ref,
    strip, partner, rims, partner_rims, own_col, other_col,
    resid_ref, rows_ref, column_ref, c_ref, factor_ref, pa, pb, u, v, matrix,
):
    section, lev = lax.axis_index("sec"), lax.axis_index("lev")
    own_level = EDGE * lev
    for ref in (pa, pb, u, v, c_ref):
        clear(ref)
    clear_levels(pa)
    clear_levels(pb)
    cos_low, sin_low = quarter_turn(turn_ref[0, 0])
    cos_high, sin_high = quarter_turn(turn_ref[0, 1])
    below = lax.broadcasted_iota(jnp.int32, (BLK, 128), 0) < 4

    def factors(low, high):
        low = low[4 * FIELD : 4 * FIELD + 16, :].astype(F32)
        high = high[4 * FIELD : 4 * FIELD + 16, :].astype(F32)
        factor_ref[0] = jnp.where(below, cos_low, low[2:3, :]) - 1.0
        factor_ref[1] = jnp.where(below, sin_low, low[3:4, :])
        factor_ref[2] = jnp.where(below, high[0:1, :], cos_high) - 1.0
        factor_ref[3] = jnp.where(below, high[1:2, :], sin_high)

    pl.when(section == 0)(lambda: factors(strip, partner))
    pl.when(section == 1)(lambda: factors(partner, strip))
    masks = edge_masks()
    matrix[...] = across_matrix()

    def run(sec):
        unit = COURANT * UNIT
        spread_rims(
            sec, lev, strip, partner, rims, partner_rims, own_col, other_col,
            ((pa, 2, None), (u, 0, None), (v, 0, None), (c_ref, 0, unit)),
        )
        _, near_edge, far_edge = static_rows(sec)
        tile_row = 24 - 8 * sec
        for n, (dst, shift) in enumerate(((pa, 2), (u, 0), (v, 0))):
            field = state_ref[n * OWN * 16 : (n + 1) * OWN * 16, :].reshape(OWN, 16, 128)
            dst[pl.ds(own_level + shift, OWN), tile_row : tile_row + 16, :] = field
        field = unit * sound_ref[...].reshape(OWN, 16, 128)
        c_ref[pl.ds(own_level, OWN), tile_row : tile_row + 16, :] = field
        near_factor, far_factor = (0, 2) if sec == 0 else (2, 0)
        for step in range(SUBSTEPS):
            old, new = (pa, pb) if step % 2 == 0 else (pb, pa)

            def body(step=step, old=old, new=new):
                k, size = 0, EXT
                levels = pl.ds(k, size)
                inner = pl.ds(k + 2, size)
                first, last = WIND_BLOCKS[step]
                wide = slice(BLK + BLK * first, BLK + BLK * last)
                slopes = across(old[inner, wide, :], matrix)
                for block in range(first, last):
                    row = BLK + BLK * block
                    rows = slice(row, row + BLK)
                    c = c_ref[levels, rows, :]
                    u[levels, rows, :] = u[levels, rows, :] - c * along(old, inner, row)
                    at = BLK * (block - first)
                    v[levels, rows, :] = v[levels, rows, :] - c * slopes[:, at : at + BLK, :]
                first, last = MASS_BLOCKS[step]
                narrow = slice(BLK + BLK * first, BLK + BLK * last)
                slopes = across(v[levels, narrow, :], matrix)
                for block in range(first, last):
                    row = BLK + BLK * block
                    rows = slice(row, row + BLK)
                    at = BLK * (block - first)
                    spread_uv = along(u, levels, row) + slopes[:, at : at + BLK, :]
                    new[inner, rows, :] = vertical(old, k, size, row) - c_ref[levels, rows, :] * spread_uv
                for edge, f in ((near_edge, near_factor), (far_edge, far_factor))[: 2 if step < 2 else 1]:
                    rows = slice(edge - 4, edge + 4)
                    delta = factor_ref[f] * u[levels, rows, :] - factor_ref[f + 1] * v[levels, rows, :]
                    new[inner, rows, :] = new[inner, rows, :] - c_ref[levels, rows, :] * crossing(delta, masks)

            body()
        final = pa if SUBSTEPS % 2 == 0 else pb
        for n, (src, shift) in enumerate(((final, 2), (u, 0), (v, 0))):
            evolved = src[pl.ds(own_level + shift, OWN), 3 * BLK : 4 * BLK, :]
            packed = slice(n * FIELD, (n + 1) * FIELD)
            resid = evolved.reshape(FIELD, 128) + tendency_ref[packed, :]
            resid_ref[packed, :] = resid
            rows_ref[packed, :] = resid.astype(BF)

    for sec in range(2):
        pl.when(section == sec)(lambda sec=sec: run(sec))
    for r in range(BLK):
        column_ref[r * GROUP : (r + 1) * GROUP, :] = column_rows(resid_ref, r, 0, BLK, FIELD, 0.0)


def adjoint_kernel(
    resid_ref, other_ref, input_grad_ref, c_ref, factor_ref,
    strip, partner, rims, partner_rims, own_col, other_col,
    out_ref, pa, pb, u, v, matrix, w,
):
    section, lev = lax.axis_index("sec"), lax.axis_index("lev")
    own_level = EDGE * lev
    for ref in (pa, pb, u, v, w):
        clear(ref)
    clear_levels(pa)
    clear_levels(pb)
    masks = edge_masks()
    matrix[...] = across_matrix()

    def run(sec):
        spread_rims(
            sec, lev, strip, partner, rims, partner_rims, own_col, other_col,
            ((pa, 2, None), (u, 0, None), (v, 0, None)),
        )
        other_row, near_edge, far_edge = static_rows(sec)
        for n, (dst, shift) in enumerate(((pa, 2), (u, 0), (v, 0))):
            at = pl.ds(own_level + shift, OWN)
            packed = slice(n * FIELD, (n + 1) * FIELD)
            dst[at, 3 * BLK : 4 * BLK, :] = resid_ref[packed, :].reshape(OWN, BLK, 128)
            dst[at, other_row : other_row + BLK, :] = other_ref[packed, :].reshape(OWN, BLK, 128)
        near_factor, far_factor = (0, 2) if sec == 0 else (2, 0)
        for step in range(SUBSTEPS):
            old, new = (pa, pb) if step % 2 == 0 else (pb, pa)
            first, last = WIND_BLOCKS[step]
            wide = slice(BLK + BLK * max(first - 1, 0), BLK + BLK * min(last + 1, 5))
            first, last = MASS_BLOCKS[step]
            narrow = slice(BLK + BLK * max(first - 1, 0), BLK + BLK * min(last + 1, 5))

            def body(step=step, old=old, new=new, wide=wide, narrow=narrow):
                k, size = 0, EXT
                whole = pl.ds(0, size)
                levels = pl.ds(k, size)
                inner = pl.ds(k + 2, size)
                w[whole, wide, :] = c_ref[levels, wide, :] * old[inner, wide, :]
                first, last = WIND_BLOCKS[step]
                slopes = across(w[whole, BLK + BLK * first : BLK + BLK * last, :], matrix)
                for block in range(first, last):
                    row = BLK + BLK * block
                    rows = slice(row, row + BLK)
                    u[levels, rows, :] = u[levels, rows, :] + along(w, whole, row)
                    at = BLK * (block - first)
                    v[levels, rows, :] = v[levels, rows, :] + slopes[:, at : at + BLK, :]
                for edge, f in ((near_edge, near_factor), (far_edge, far_factor))[: 2 if step < 2 else 1]:
                    rows = slice(edge - 4, edge + 4)
                    cross = crossing(w[whole, rows, :], masks)
                    u[levels, rows, :] = u[levels, rows, :] + factor_ref[f] * cross
                    v[levels, rows, :] = v[levels, rows, :] - factor_ref[f + 1] * cross
                w[whole, narrow, :] = c_ref[levels, narrow, :] * u[levels, narrow, :]
                first, last = MASS_BLOCKS[step]
                rows = slice(BLK + BLK * first, BLK + BLK * last)
                slopes = across(c_ref[levels, rows, :] * v[levels, rows, :], matrix)
                for block in range(first, last):
                    row = BLK + BLK * block
                    at = BLK * (block - first)
                    spread_uv = along(w, whole, row) + slopes[:, at : at + BLK, :]
                    new[inner, row : row + BLK, :] = vertical(old, k, size, row) + spread_uv

            body()

    for sec in range(2):
        pl.when(section == sec)(lambda sec=sec: run(sec))
    final = pa if SUBSTEPS % 2 == 0 else pb
    for n, (src, shift) in enumerate(((final, 2), (u, 0), (v, 0))):
        packed = slice(n * FIELD, (n + 1) * FIELD)
        adjoint = src[pl.ds(own_level + shift, OWN), 3 * BLK : 4 * BLK, :].reshape(FIELD, 128)
        out_ref[packed, :] = adjoint + input_grad_ref[packed, :]


def dot(left, right):
    return lax.dot_general(left, right, (((1,), (0,)), ((), ())), preferred_element_type=F32)


def dot_t(left, right):
    return lax.dot_general(left, right, (((0,), (0,)), ((), ())), preferred_element_type=F32)


def dot_columns(left, right):
    return lax.dot_general(left, right, (((1,), (1,)), ((), ())), preferred_element_type=F32)


def silu_and_slope(values):
    sigma = 0.5 * jnp.tanh(0.5 * values) + 0.5
    silu = values * sigma
    return silu.astype(BF), sigma + silu * (1.0 - sigma)


def both_groups(own_ref, other_ref):
    parts = [
        jnp.concatenate([ref[r * GROUP : (r + 1) * GROUP, :] for ref in (own_ref, other_ref)], axis=0)
        for r in range(STRIPE // 128)
    ]
    return jnp.concatenate(parts, axis=1)


def to_fields(out_ref, first, values, minus_ref=None, minus_first=None):
    for r in range(STRIPE // 128):
        for n in range(3):
            value = values[n * OWN : (n + 1) * OWN, r * 128 : (r + 1) * 128]
            if minus_ref is not None:
                value = value - minus_ref[pl.ds(n * OWN * 16 + minus_first + r, OWN, stride=16), :]
            out_ref[pl.ds(n * FIELD + first + r, OWN, stride=BLK), :] = value


def network_kernel(
    own_ref, other_ref, first_ref, second_ref, third_t_ref, target_ref,
    feat_ref, one_ref, two_ref, slope_one_ref, slope_two_ref, tendency_ref,
):
    feat = both_groups(own_ref, other_ref)
    feat_ref[...] = feat
    one, slope = silu_and_slope(dot_t(first_ref[...], feat))
    one_ref[...] = one
    slope_one_ref[...] = slope
    two, slope = silu_and_slope(dot_t(second_ref[...], one))
    two_ref[...] = two
    slope_two_ref[...] = slope
    row = pl.program_id(0) * (STRIPE // 128)
    at = BLK * lax.axis_index("sec") + row
    to_fields(tendency_ref, row, dot(third_t_ref[:GROUP, :], two), target_ref, at)


def back_kernel(
    own_ref, other_ref, feat_ref, third_t_ref, second_ref, first_ref, one_ref, two_ref, slope_one_ref, slope_two_ref,
    given_ref, kept_ref, input_grad_ref, err_one_ref, err_two_ref, total_ref,
):
    step = pl.program_id(0)
    resid = both_groups(own_ref, other_ref)
    err_two = (dot_t(third_t_ref[...], resid) * slope_two_ref[...]).astype(BF)
    err_two_ref[...] = err_two
    err_one = (dot(second_ref[...], err_two) * slope_one_ref[...]).astype(BF)
    err_one_ref[...] = err_one
    to_fields(input_grad_ref, step * (STRIPE // 128), dot(first_ref[:GROUP, :], err_one))
    feats, hid = feat_ref.shape[0], one_ref.shape[0]
    half = pl.ds(pl.multiple_of(256 * lax.axis_index("lev"), 256), 256)

    def clear_total():
        total_ref[...] = jnp.zeros(total_ref.shape, F32)

    pl.when(step == 0)(clear_total)

    def add(rows, left, right):
        total_ref[rows, :] = total_ref[rows, :] + dot_columns(left, right)

    add(slice(0, feats), feat_ref[...], err_one_ref[half, :])
    add(slice(feats, feats + hid), one_ref[...], err_two_ref[half, :])
    add(slice(feats + hid, 2 * feats + hid), resid, two_ref[half, :])

    def finish():
        for sec in range(2):

            def share(sec=sec):
                kept_ref[...] = total_ref[:, 128 * sec : 128 * sec + 128]
                given_ref[...] = total_ref[:, 128 - 128 * sec : 256 - 128 * sec].astype(BF)

            pl.when(lax.axis_index("sec") == sec)(share)

    pl.when(step == COLS // STRIPE - 1)(finish)


def join_kernel(near_ref, far_ref, strip_ref, edge_ref):
    strip_ref[: 3 * FIELD, :] = near_ref[...]
    strip_ref[3 * FIELD :, :] = far_ref[...]
    for n in range(3):
        corner(edge_ref, n, near_ref, n * FIELD, far_ref, n * FIELD, lax.axis_index("lev"))


def add_kernel(kept_ref, received_ref, out_ref):
    out_ref[...] = (kept_ref[...] + received_ref[...].astype(F32)).astype(BF)


def mean_kernel(parts_ref, out_ref):
    total = parts_ref[0].astype(F32)
    for tile in range(1, parts_ref.shape[0]):
        total = total + parts_ref[tile].astype(F32)
    mean = (total / (COLS * out_ref.shape[0])).astype(BF)
    for device in range(out_ref.shape[0]):
        out_ref[device] = mean


def place_rows_kernel(mine_ref, theirs_ref, out_ref):
    for sec in range(2):

        def run(sec=sec):
            for n in range(3):
                packed = slice(n * FIELD, (n + 1) * FIELD)
                for core, ref in ((sec, mine_ref), (1 - sec, theirs_ref)):
                    out_ref[n, :, BLK * core : BLK * core + BLK, :] = ref[packed, :].reshape(OWN, BLK, 128)

        pl.when(lax.axis_index("sec") == sec)(run)


def spread_gradients_kernel(own_ref, partner_ref, first_ref, bias_ref, second_ref, third_t_ref):
    section = lax.axis_index("sec")
    hid = second_ref.shape[0]
    share = own_ref.shape[1]

    def feature_rows(out, row, lanes, lev, values):
        group, at = divmod(row, GROUP)
        if at < 3 * OWN:
            field, level = divmod(at, OWN)
            to = (2 * field + (lev + group) % 2) * OWN + level
            out[to : to + 8, lanes] = values

    def run(sec):
        blocks = [(tile, lev, core) for tile in range(own_ref.shape[0] // 2) for lev in range(2) for core in range(2)]
        for tile, lev, core in blocks:
            lanes = slice(256 * lev + 128 * core, 256 * lev + 128 * core + 128)
            block = (own_ref if core == sec else partner_ref)[2 * tile + lev].astype(F32)
            for part in range(0, share, 8):
                row = tile * share + part
                values = block[part : part + 8, :]
                if row < 2 * GROUP:
                    feature_rows(first_ref, row, lanes, lev, values)
                    if row == 3 * OWN:
                        bias_ref[:, lanes] = values[:1, :]
                elif row < 2 * GROUP + hid:
                    second_ref[row - 2 * GROUP : row - 2 * GROUP + 8, lanes] = values
                else:
                    feature_rows(third_t_ref, row - 2 * GROUP - hid, lanes, lev, values)

    for sec in range(2):
        pl.when(section == sec)(lambda sec=sec: run(sec))


def whole(value):
    return pl.BlockSpec(value.shape, lambda i: (0,) * len(value.shape), pipeline_mode=pl.Buffered(1))


def stripes(value, along):
    if along:
        return pl.BlockSpec((value.shape[0], STRIPE), lambda i: (0, i))
    return pl.BlockSpec((STRIPE // 128 * GROUP, 128), lambda i: (i, 0))


def first_rows(rows, value):
    return pl.BlockSpec((rows, *value.shape[1:]), lambda i: (0,) * len(value.shape), pipeline_mode=pl.Buffered(1))


def call(kernel, n_smem, operands, outs, scratch=(), flops=0, limit=60, steps=1, in_along=None, out_along=None):
    def specs(values, along):
        along = along or [None] * len(values)
        return [whole(v) if at is None else first_rows(at, v) if at > 1 else stripes(v, at) for v, at in zip(values, along, strict=True)]

    smem = pl.BlockSpec(memory_space=pltpu.SMEM)
    return pl.pallas_call(
        kernel,
        grid=(steps,),
        out_shape=outs,
        in_specs=[smem] * n_smem + specs(operands[n_smem:], in_along),
        out_specs=specs(outs, out_along),
        scratch_shapes=list(scratch),
        compiler_params=pltpu.CompilerParams(vmem_limit_bytes=limit * MIB),
        cost_estimate=pl.CostEstimate(flops=flops, bytes_accessed=0, transcendentals=0),
    )(*operands)


def stencil_scratch(extra=()):
    mass = pltpu.VMEM((EXT + 4, ROWS, 128), F32)
    wind = pltpu.VMEM((EXT, ROWS, 128), F32)
    return [mass, mass, wind, wind, pltpu.VMEM((256, 128), BF), *extra]


def shape(*dims, dtype=F32):
    return jax.ShapeDtypeStruct(dims, dtype)


def swap(value, axis):
    return lax.ppermute(value, axis, [(0, 1), (1, 0)])


def strip_swaps(strip, edges, tiles):
    pairs = [(tiles + t, t + 1) for t in range(tiles - 1)]
    pairs += [(b, a) for a, b in pairs]
    cross = [(2 * a + lev, 2 * b + 1 - lev) for a, b in pairs for lev in range(2)]
    return lax.ppermute(strip, ("sec", "tile"), pairs), lax.ppermute(edges, ("sec", "tile", "lev"), cross)


def local(state, sound, target, edge_turn, w_first, b_first, w_second, w_third):
    tiles = lax.axis_size("tile")
    hid, feats = w_second.shape[0], 2 * GROUP

    state, sound, target = state.reshape(-1, 128), sound.reshape(-1, 128), target.reshape(-1, 128)
    strip, edges, columns, first, third_t = call(
        pack_kernel, 1, (edge_turn, state, sound, w_first, w_third.T, b_first[None]),
        (shape(8 * FIELD + 16, 128, dtype=BF), shape(4 * RIM, 128, dtype=BF), shape(BLK * GROUP + RIM, 128, dtype=BF), shape(feats, hid, dtype=BF), shape(feats, hid, dtype=BF)),
    )
    own_col = swap(columns, "lev")
    strip, rims = strip_swaps(strip, edges, tiles)

    activations = (shape(feats, COLS, dtype=BF), shape(hid, COLS, dtype=BF), shape(hid, COLS, dtype=BF), shape(hid, COLS), shape(hid, COLS))
    feat, one, two, slope_one, slope_two, tendency = call(
        network_kernel, 0, (columns, own_col, first, w_second, third_t, target),
        (*activations, shape(3 * FIELD, 128)),
        steps=COLS // STRIPE, flops=LONG, in_along=(0, 0, None, None, None, None), out_along=(1, 1, 1, 1, 1, None),
    )

    other_col = swap(own_col, "sec")
    strip, rims, tendency = lax.optimization_barrier((strip, rims, tendency))
    resid, r_rows, r_columns, coeff, factors = call(
        forward_kernel, 1,
        (edge_turn, state, sound, tendency, strip, swap(strip, "sec"), rims, swap(rims, "sec"), own_col, other_col),
        (shape(3 * FIELD, 128), shape(3 * FIELD, 128, dtype=BF), shape(BLK * GROUP, 128, dtype=BF), shape(EXT, ROWS, 128), shape(4, BLK, 128)),
        stencil_scratch(), flops=LONG, in_along=(*[None] * 4, 4 * FIELD + 16, *[None] * 4),
    )

    r_own_col = swap(r_columns, "lev")
    r_other = swap(resid, "sec")
    r_strip, r_edges = call(
        join_kernel, 0, (r_rows, swap(r_rows, "sec")),
        (shape(6 * FIELD, 128, dtype=BF), shape(3 * RIM, 128, dtype=BF)), limit=16,
    )
    r_strip, r_rims = strip_swaps(r_strip, r_edges, tiles)
    n_rows = 2 * feats + hid
    given, kept, input_grad = call(
        back_kernel, 0, (r_columns, r_own_col, feat, third_t, w_second, first, one, two, slope_one, slope_two),
        (shape(n_rows, 128, dtype=BF), shape(n_rows, 128), shape(3 * FIELD, 128)),
        (pltpu.VMEM((hid, STRIPE), BF), pltpu.VMEM((hid, STRIPE), BF), pltpu.VMEM((n_rows, 256), F32)),
        flops=LONG, steps=COLS // STRIPE, in_along=(0, 0, 1, None, None, None, 1, 1, 1, 1),
    )
    given, r_strip, r_rims = lax.optimization_barrier((given, r_strip, r_rims))
    r_partner, r_partner_rims, r_other_col = swap(r_strip, "sec"), swap(r_rims, "sec"), swap(r_own_col, "sec")
    received = swap(given, "sec")
    share = n_rows // tiles
    (partial,) = call(add_kernel, 0, (kept, received), (shape(n_rows, 128, dtype=BF),), limit=16)
    partial = partial.reshape(tiles, share, 128)
    parts = lax.all_to_all(partial, "tile", 0, 0)
    (mine,) = call(
        adjoint_kernel, 0,
        (resid, r_other, input_grad, coeff, factors, r_strip, r_partner, r_rims, r_partner_rims, r_own_col, r_other_col),
        (shape(3 * FIELD, 128),), stencil_scratch((pltpu.VMEM((EXT, ROWS, 128), F32),)), flops=LONG,
        in_along=(*[None] * 6, 3 * FIELD, *[None] * 4),
    )
    parts, mine = lax.optimization_barrier((parts, mine))
    (everywhere,) = call(mean_kernel, 0, (parts,), (shape(2 * tiles, share, 128, dtype=BF),), limit=16)
    gathered = lax.all_to_all(everywhere, ("tile", "lev"), 0, 0)
    (state_grad,) = call(place_rows_kernel, 0, (mine, swap(mine, "sec")), (shape(3, OWN, 2 * BLK, 128),), limit=16)
    state_grad, gathered = lax.optimization_barrier((state_grad, gathered))
    g_first, g_bias, g_second, g_third_t = call(
        spread_gradients_kernel, 0, (gathered, swap(gathered, "sec")),
        (shape(6 * OWN, hid), shape(1, hid), shape(hid, hid), shape(6 * OWN, hid)), limit=16,
    )
    return (state_grad, g_first, g_bias.reshape(hid), g_second, g_third_t.T)


def solution(mesh):
    placed = (
        P(None, "lev", "tile", None),
        P("lev", "tile", None),
        P(None, "lev", "tile", None),
        P("tile", None),
        P(),
        P(),
        P(),
        P(),
    )
    return jax.shard_map(
        local,
        mesh=mesh,
        in_specs=placed,
        out_specs=(P(None, "lev", "tile", None), P(), P(), P(), P()),
        check_vma=False,
    )
```

```python
import jax
import jax.numpy as jnp
from jax import lax
from jax.experimental import pallas as pl
from jax.experimental.pallas import tpu as pltpu
from jax.sharding import PartitionSpec as P

SUBSTEPS = 4
COURANT = 0.3
DIFFUSION = 0.08
UNIT = 1.0 / 12.0

BLK = 8
OWN = 40
EDGE = 8
EXT = OWN + EDGE
ROWS = 7 * BLK
WIND_BLOCKS = ((0, 5), (0, 5), (1, 4), (1, 4))
MASS_BLOCKS = ((0, 5), (1, 4), (1, 4), (2, 3))
FIELD = OWN * BLK
RIM = EDGE * BLK
NEAR_EDGE, FAR_EDGE = 6, 2
COLS = BLK * 128
GROUP = 128
PAD = GROUP - 3 * OWN
STRIPE = 512
MIB = 1024 * 1024
LONG = 20_000_000_000
F32 = jnp.float32
BF = jnp.bfloat16


def roll(values, steps, axis):
    return pltpu.roll(values, steps % values.shape[axis], axis)


def across_matrix():
    source = lax.broadcasted_iota(jnp.int32, (256, 128), 0)
    target = lax.broadcasted_iota(jnp.int32, (256, 128), 1)
    apart = (source - target) & 127
    near = jnp.where(apart == 1, 8.0, 0.0) - jnp.where(apart == 127, 8.0, 0.0)
    far = jnp.where(apart == 126, 1.0, 0.0) - jnp.where(apart == 2, 1.0, 0.0)
    return (near + far).astype(BF)


def across(values, matrix):
    flat = values.reshape(-1, 128)
    high = flat.astype(BF)
    low = (flat - high.astype(F32)).astype(BF)
    return dot(jnp.concatenate([high, low], axis=1), matrix[...]).reshape(values.shape)


def along(ref, levels, row):
    def take(steps):
        return ref[levels, row + steps : row + steps + BLK, :]

    return 8.0 * (take(1) - take(-1)) - (take(2) - take(-2))


def vertical(ref, k, size, row):
    v = ref[pl.ds(k, size + 4), row : row + BLK, :]
    near = v[3 : 3 + size] + v[1 : 1 + size]
    far = v[4 : 4 + size] + v[0:size]
    return (1.0 - 30.0 * UNIT * DIFFUSION) * v[2 : 2 + size] + (UNIT * DIFFUSION) * (16.0 * near - far)


def edge_masks():
    i = lax.broadcasted_iota(jnp.int32, (1, BLK, 128), 1)

    def at(row, value):
        return jnp.where(i == row, value, 0.0)

    return at(4, -8.0), at(4, 1.0) + at(5, 1.0), at(3, 8.0), at(3, -1.0) + at(2, -1.0)


def crossing(values, masks):
    m1, m2, m3, m4 = masks
    return (
        m1 * roll(values, 1, 1)
        + m2 * roll(values, 2, 1)
        + m3 * roll(values, -1, 1)
        + m4 * roll(values, -2, 1)
    )


def quarter_turn(quarter):
    cosine = jnp.where(quarter == 0, 1.0, 0.0) - jnp.where(quarter == 2, 1.0, 0.0)
    sine = jnp.where(quarter == 1, 1.0, 0.0) - jnp.where(quarter == 3, 1.0, 0.0)
    return cosine, sine


def clear(ref):
    levels = ref.shape[0]
    zeros = jnp.zeros((levels, BLK, 128), F32)
    ref[:, 0:BLK, :] = zeros
    ref[:, ROWS - BLK : ROWS, :] = zeros


def clear_levels(ref):
    for level in (0, 1, EXT + 2, EXT + 3):
        ref[level] = jnp.zeros((ROWS, 128), F32)


def spread(src, start, count, dst, level, row, scale=None):
    def body(i, _):
        rows = src[pl.ds(pl.multiple_of(start + i * 16, 16), 16), :].astype(F32)
        if scale is not None:
            rows = rows * scale
        dst[pl.ds(level + 2 * i, 2), row : row + BLK, :] = rows.reshape(2, BLK, 128)
        return 0

    if count > EDGE:
        lax.fori_loop(0, count // 2, body, 0, unroll=20)
    else:
        for i in range(count // 2):
            body(i, 0)


def spread_column_edge(columns, n, dst, level, row, lev, scale=None):
    if n == 3:
        spread(columns, BLK * GROUP, EDGE, dst, level, row, scale)
        return
    skip = n * OWN % 16
    for r in range(BLK):
        start = pl.multiple_of(r * GROUP + n * OWN - skip + (OWN - EDGE) * lev, 16)
        values = columns[pl.ds(start, 16), :].astype(F32)
        dst[pl.ds(level, EDGE), row + r, :] = values[skip : skip + EDGE, :]


def static_rows(sec):
    return 32 - 16 * sec, 24 + 8 * sec, 40 - 24 * sec


def spread_rims(sec, lev, strip, partner, rims, partner_rims, own_col, other_col, fields):
    own_level, edge_level = EDGE * lev, OWN * (1 - lev)
    count = len(fields)
    far_start = strip.shape[0] - count * FIELD
    far_row, near_row, partner_row = (8, 16, 40) if sec == 0 else (40, 32, 8)
    near_level, far_level = edge_level + (EDGE - NEAR_EDGE) * lev, edge_level + (EDGE - FAR_EDGE) * lev
    for n, (dst, shift, scale) in enumerate(fields):
        dst[pl.ds(edge_level + shift, EDGE), :, :] = jnp.zeros((EDGE, ROWS, 128), F32)
        spread(strip, far_start + n * FIELD, OWN, dst, own_level + shift, far_row, scale)
        spread(strip, n * FIELD, OWN, dst, own_level + shift, near_row, scale)
        spread(partner, n * FIELD, OWN, dst, own_level + shift, partner_row, scale)
        spread(rims, n * RIM, NEAR_EDGE, dst, near_level + shift, near_row, scale)
        spread(partner_rims, n * RIM, NEAR_EDGE, dst, near_level + shift, partner_row, scale)
        spread(rims, n * RIM + NEAR_EDGE * BLK, FAR_EDGE, dst, far_level + shift, far_row, scale)
        for columns, row in ((own_col, 3 * BLK), (other_col, static_rows(sec)[0])):
            spread_column_edge(columns, n, dst, edge_level + shift, row, lev, scale)


def column_rows(ref, row, start, stride, step, fill):
    fields = [ref[pl.ds(n * step + start + row, OWN, stride=stride), :] for n in range(3)]
    return jnp.concatenate([*fields, jnp.full((PAD, 128), fill, F32)], axis=0).astype(BF)


def by_group(out_ref, weights_ref, lev, bias_ref=None):
    hid = out_ref.shape[1]
    values = weights_ref[...].astype(F32)
    padding = jnp.zeros((PAD, hid), F32)
    own_padding = padding
    if bias_ref is not None:
        rest = bias_ref[...]
        row = lax.broadcasted_iota(jnp.int32, (PAD, hid), 0)
        for n in range(3):
            part = rest.astype(BF).astype(F32)
            own_padding = jnp.where(row == n, part, own_padding)
            rest = rest - part
    groups = [[values[(2 * n + g) * OWN : (2 * n + g + 1) * OWN] for n in range(3)] for g in range(2)]
    for group in range(2):

        def run(group=group):
            parts = [*groups[group], own_padding, *groups[1 - group], padding]
            out_ref[...] = jnp.concatenate(parts, axis=0).astype(BF)

        pl.when(lev == group)(run)


def corner(edge_ref, n, near_ref, near, far_ref, far, lev):
    for src, start, at, levels in ((near_ref, near, 0, NEAR_EDGE), (far_ref, far, NEAR_EDGE, FAR_EDGE)):
        rows = pl.ds(pl.multiple_of(start + (OWN - levels) * BLK * (1 - lev), 16), levels * BLK)
        edge_ref[n * RIM + at * BLK : n * RIM + (at + levels) * BLK, :] = src[rows, :]


def pack_kernel(
    turn_ref, state_ref, sound_ref, first_ref, third_t_ref, bias_ref,
    strip_ref, edge_ref, column_ref, first_out_ref, third_out_ref,
):
    sec, lev = lax.axis_index("sec"), lax.axis_index("lev")
    by_group(first_out_ref, first_ref, lev, bias_ref)
    by_group(third_out_ref, third_t_ref, lev)
    far_start = 4 * FIELD + 16
    for half in range(2):

        def run(half=half):
            for n in range(4):
                src = state_ref[n * OWN * 16 : (n + 1) * OWN * 16, :] if n < 3 else sound_ref[...]
                for at, block in ((n * FIELD, half), (far_start + n * FIELD, 1 - half)):
                    field = src.reshape(OWN, 16, 128)[:, block * BLK : block * BLK + BLK, :]
                    strip_ref[at : at + FIELD, :] = field.reshape(FIELD, 128).astype(BF)
            for r in range(BLK):
                features = column_rows(state_ref, r, BLK * half, 16, OWN * 16, 1.0)
                column_ref[r * GROUP : (r + 1) * GROUP, :] = features

        pl.when(sec == half)(run)
    for n in range(4):
        near, far = n * FIELD, far_start + n * FIELD
        if n == 3:
            start = pl.multiple_of(near + (FIELD - RIM) * (1 - lev), 16)
            column_ref[BLK * GROUP :, :] = strip_ref[pl.ds(start, RIM), :]
        corner(edge_ref, n, strip_ref, near, strip_ref, far, lev)
    i = lax.broadcasted_iota(jnp.int32, (16, 128), 0)
    factors = jnp.zeros((16, 128), F32)
    for n, value in enumerate((*quarter_turn(turn_ref[0, 0]), *quarter_turn(turn_ref[0, 1]))):
        factors = jnp.where(i == n, value, factors)
    strip_ref[4 * FIELD : far_start, :] = factors.astype(BF)


def forward_kernel(
    turn_ref, state_ref, sound_ref, tendency_ref,
    strip, partner, rims, partner_rims, own_col, other_col,
    resid_ref, rows_ref, column_ref, c_ref, factor_ref, pa, pb, u, v, matrix,
):
    section, lev = lax.axis_index("sec"), lax.axis_index("lev")
    own_level = EDGE * lev
    for ref in (pa, pb, u, v, c_ref):
        clear(ref)
    clear_levels(pa)
    clear_levels(pb)
    cos_low, sin_low = quarter_turn(turn_ref[0, 0])
    cos_high, sin_high = quarter_turn(turn_ref[0, 1])
    below = lax.broadcasted_iota(jnp.int32, (BLK, 128), 0) < 4

    def factors(low, high):
        low = low[4 * FIELD : 4 * FIELD + 16, :].astype(F32)
        high = high[4 * FIELD : 4 * FIELD + 16, :].astype(F32)
        factor_ref[0] = jnp.where(below, cos_low, low[2:3, :]) - 1.0
        factor_ref[1] = jnp.where(below, sin_low, low[3:4, :])
        factor_ref[2] = jnp.where(below, high[0:1, :], cos_high) - 1.0
        factor_ref[3] = jnp.where(below, high[1:2, :], sin_high)

    pl.when(section == 0)(lambda: factors(strip, partner))
    pl.when(section == 1)(lambda: factors(partner, strip))
    masks = edge_masks()
    matrix[...] = across_matrix()

    def run(sec):
        unit = COURANT * UNIT
        spread_rims(
            sec, lev, strip, partner, rims, partner_rims, own_col, other_col,
            ((pa, 2, None), (u, 0, None), (v, 0, None), (c_ref, 0, unit)),
        )
        _, near_edge, far_edge = static_rows(sec)
        tile_row = 24 - 8 * sec
        for n, (dst, shift) in enumerate(((pa, 2), (u, 0), (v, 0))):
            field = state_ref[n * OWN * 16 : (n + 1) * OWN * 16, :].reshape(OWN, 16, 128)
            dst[pl.ds(own_level + shift, OWN), tile_row : tile_row + 16, :] = field
        field = unit * sound_ref[...].reshape(OWN, 16, 128)
        c_ref[pl.ds(own_level, OWN), tile_row : tile_row + 16, :] = field
        near_factor, far_factor = (0, 2) if sec == 0 else (2, 0)
        for step in range(SUBSTEPS):
            old, new = (pa, pb) if step % 2 == 0 else (pb, pa)

            def body(step=step, old=old, new=new):
                k, size = 0, EXT
                levels = pl.ds(k, size)
                inner = pl.ds(k + 2, size)
                first, last = WIND_BLOCKS[step]
                wide = slice(BLK + BLK * first, BLK + BLK * last)
                slopes = across(old[inner, wide, :], matrix)
                for block in range(first, last):
                    row = BLK + BLK * block
                    rows = slice(row, row + BLK)
                    c = c_ref[levels, rows, :]
                    u[levels, rows, :] = u[levels, rows, :] - c * along(old, inner, row)
                    at = BLK * (block - first)
                    v[levels, rows, :] = v[levels, rows, :] - c * slopes[:, at : at + BLK, :]
                first, last = MASS_BLOCKS[step]
                narrow = slice(BLK + BLK * first, BLK + BLK * last)
                slopes = across(v[levels, narrow, :], matrix)
                for block in range(first, last):
                    row = BLK + BLK * block
                    rows = slice(row, row + BLK)
                    at = BLK * (block - first)
                    spread_uv = along(u, levels, row) + slopes[:, at : at + BLK, :]
                    new[inner, rows, :] = vertical(old, k, size, row) - c_ref[levels, rows, :] * spread_uv
                for edge, f in ((near_edge, near_factor), (far_edge, far_factor))[: 2 if step < 2 else 1]:
                    rows = slice(edge - 4, edge + 4)
                    delta = factor_ref[f] * u[levels, rows, :] - factor_ref[f + 1] * v[levels, rows, :]
                    new[inner, rows, :] = new[inner, rows, :] - c_ref[levels, rows, :] * crossing(delta, masks)

            body()
        final = pa if SUBSTEPS % 2 == 0 else pb
        for n, (src, shift) in enumerate(((final, 2), (u, 0), (v, 0))):
            evolved = src[pl.ds(own_level + shift, OWN), 3 * BLK : 4 * BLK, :]
            packed = slice(n * FIELD, (n + 1) * FIELD)
            resid = evolved.reshape(FIELD, 128) + tendency_ref[packed, :]
            resid_ref[packed, :] = resid
            rows_ref[packed, :] = resid.astype(BF)

    for sec in range(2):
        pl.when(section == sec)(lambda sec=sec: run(sec))
    for r in range(BLK):
        column_ref[r * GROUP : (r + 1) * GROUP, :] = column_rows(resid_ref, r, 0, BLK, FIELD, 0.0)


def adjoint_kernel(
    resid_ref, other_ref, input_grad_ref, c_ref, factor_ref,
    strip, partner, rims, partner_rims, own_col, other_col,
    out_ref, pa, pb, u, v, matrix, w,
):
    section, lev = lax.axis_index("sec"), lax.axis_index("lev")
    own_level = EDGE * lev
    for ref in (pa, pb, u, v, w):
        clear(ref)
    clear_levels(pa)
    clear_levels(pb)
    masks = edge_masks()
    matrix[...] = across_matrix()

    def run(sec):
        spread_rims(
            sec, lev, strip, partner, rims, partner_rims, own_col, other_col,
            ((pa, 2, None), (u, 0, None), (v, 0, None)),
        )
        other_row, near_edge, far_edge = static_rows(sec)
        for n, (dst, shift) in enumerate(((pa, 2), (u, 0), (v, 0))):
            at = pl.ds(own_level + shift, OWN)
            packed = slice(n * FIELD, (n + 1) * FIELD)
            dst[at, 3 * BLK : 4 * BLK, :] = resid_ref[packed, :].reshape(OWN, BLK, 128)
            dst[at, other_row : other_row + BLK, :] = other_ref[packed, :].reshape(OWN, BLK, 128)
        near_factor, far_factor = (0, 2) if sec == 0 else (2, 0)
        for step in range(SUBSTEPS):
            old, new = (pa, pb) if step % 2 == 0 else (pb, pa)
            first, last = WIND_BLOCKS[step]
            wide = slice(BLK + BLK * max(first - 1, 0), BLK + BLK * min(last + 1, 5))
            first, last = MASS_BLOCKS[step]
            narrow = slice(BLK + BLK * max(first - 1, 0), BLK + BLK * min(last + 1, 5))

            def body(step=step, old=old, new=new, wide=wide, narrow=narrow):
                k, size = 0, EXT
                whole = pl.ds(0, size)
                levels = pl.ds(k, size)
                inner = pl.ds(k + 2, size)
                w[whole, wide, :] = c_ref[levels, wide, :] * old[inner, wide, :]
                first, last = WIND_BLOCKS[step]
                slopes = across(w[whole, BLK + BLK * first : BLK + BLK * last, :], matrix)
                for block in range(first, last):
                    row = BLK + BLK * block
                    rows = slice(row, row + BLK)
                    u[levels, rows, :] = u[levels, rows, :] + along(w, whole, row)
                    at = BLK * (block - first)
                    v[levels, rows, :] = v[levels, rows, :] + slopes[:, at : at + BLK, :]
                for edge, f in ((near_edge, near_factor), (far_edge, far_factor))[: 2 if step < 2 else 1]:
                    rows = slice(edge - 4, edge + 4)
                    cross = crossing(w[whole, rows, :], masks)
                    u[levels, rows, :] = u[levels, rows, :] + factor_ref[f] * cross
                    v[levels, rows, :] = v[levels, rows, :] - factor_ref[f + 1] * cross
                w[whole, narrow, :] = c_ref[levels, narrow, :] * u[levels, narrow, :]
                first, last = MASS_BLOCKS[step]
                rows = slice(BLK + BLK * first, BLK + BLK * last)
                slopes = across(c_ref[levels, rows, :] * v[levels, rows, :], matrix)
                for block in range(first, last):
                    row = BLK + BLK * block
                    at = BLK * (block - first)
                    spread_uv = along(w, whole, row) + slopes[:, at : at + BLK, :]
                    new[inner, row : row + BLK, :] = vertical(old, k, size, row) + spread_uv

            body()

    for sec in range(2):
        pl.when(section == sec)(lambda sec=sec: run(sec))
    final = pa if SUBSTEPS % 2 == 0 else pb
    for n, (src, shift) in enumerate(((final, 2), (u, 0), (v, 0))):
        packed = slice(n * FIELD, (n + 1) * FIELD)
        adjoint = src[pl.ds(own_level + shift, OWN), 3 * BLK : 4 * BLK, :].reshape(FIELD, 128)
        out_ref[packed, :] = adjoint + input_grad_ref[packed, :]


def dot(left, right):
    return lax.dot_general(left, right, (((1,), (0,)), ((), ())), preferred_element_type=F32)


def dot_t(left, right):
    return lax.dot_general(left, right, (((0,), (0,)), ((), ())), preferred_element_type=F32)


def dot_columns(left, right):
    return lax.dot_general(left, right, (((1,), (1,)), ((), ())), preferred_element_type=F32)


def silu_and_slope(values):
    sigma = 0.5 * jnp.tanh(0.5 * values) + 0.5
    silu = values * sigma
    return silu.astype(BF), sigma + silu * (1.0 - sigma)


def both_groups(own_ref, other_ref):
    parts = [
        jnp.concatenate([ref[r * GROUP : (r + 1) * GROUP, :] for ref in (own_ref, other_ref)], axis=0)
        for r in range(STRIPE // 128)
    ]
    return jnp.concatenate(parts, axis=1)


def to_fields(out_ref, first, values, minus_ref=None, minus_first=None):
    for r in range(STRIPE // 128):
        for n in range(3):
            value = values[n * OWN : (n + 1) * OWN, r * 128 : (r + 1) * 128]
            if minus_ref is not None:
                value = value - minus_ref[pl.ds(n * OWN * 16 + minus_first + r, OWN, stride=16), :]
            out_ref[pl.ds(n * FIELD + first + r, OWN, stride=BLK), :] = value


def network_kernel(
    own_ref, other_ref, first_ref, second_ref, third_t_ref, target_ref,
    feat_ref, one_ref, two_ref, slope_one_ref, slope_two_ref, tendency_ref,
):
    feat = both_groups(own_ref, other_ref)
    feat_ref[...] = feat
    one, slope = silu_and_slope(dot_t(first_ref[...], feat))
    one_ref[...] = one
    slope_one_ref[...] = slope
    two, slope = silu_and_slope(dot_t(second_ref[...], one))
    two_ref[...] = two
    slope_two_ref[...] = slope
    row = pl.program_id(0) * (STRIPE // 128)
    at = BLK * lax.axis_index("sec") + row
    to_fields(tendency_ref, row, dot(third_t_ref[:GROUP, :], two), target_ref, at)


def back_kernel(
    own_ref, other_ref, feat_ref, third_t_ref, second_ref, first_ref, one_ref, two_ref, slope_one_ref, slope_two_ref,
    given_ref, kept_ref, input_grad_ref, err_one_ref, err_two_ref, total_ref,
):
    step = pl.program_id(0)
    resid = both_groups(own_ref, other_ref)
    err_two = (dot_t(third_t_ref[...], resid) * slope_two_ref[...]).astype(BF)
    err_two_ref[...] = err_two
    err_one = (dot(second_ref[...], err_two) * slope_one_ref[...]).astype(BF)
    err_one_ref[...] = err_one
    to_fields(input_grad_ref, step * (STRIPE // 128), dot(first_ref[:GROUP, :], err_one))
    feats, hid = feat_ref.shape[0], one_ref.shape[0]
    half = pl.ds(pl.multiple_of(256 * lax.axis_index("lev"), 256), 256)

    def clear_total():
        total_ref[...] = jnp.zeros(total_ref.shape, F32)

    pl.when(step == 0)(clear_total)

    def add(rows, left, right):
        total_ref[rows, :] = total_ref[rows, :] + dot_columns(left, right)

    add(slice(0, feats), feat_ref[...], err_one_ref[half, :])
    add(slice(feats, feats + hid), one_ref[...], err_two_ref[half, :])
    add(slice(feats + hid, 2 * feats + hid), resid, two_ref[half, :])

    def finish():
        for sec in range(2):

            def share(sec=sec):
                kept_ref[...] = total_ref[:, 128 * sec : 128 * sec + 128]
                given_ref[...] = total_ref[:, 128 - 128 * sec : 256 - 128 * sec].astype(BF)

            pl.when(lax.axis_index("sec") == sec)(share)

    pl.when(step == COLS // STRIPE - 1)(finish)


def join_kernel(near_ref, far_ref, strip_ref, edge_ref):
    strip_ref[: 3 * FIELD, :] = near_ref[...]
    strip_ref[3 * FIELD :, :] = far_ref[...]
    for n in range(3):
        corner(edge_ref, n, near_ref, n * FIELD, far_ref, n * FIELD, lax.axis_index("lev"))


def add_kernel(kept_ref, received_ref, out_ref):
    out_ref[...] = (kept_ref[...] + received_ref[...].astype(F32)).astype(BF)


def mean_kernel(parts_ref, out_ref):
    total = parts_ref[0].astype(F32)
    for tile in range(1, parts_ref.shape[0]):
        total = total + parts_ref[tile].astype(F32)
    mean = (total / (COLS * out_ref.shape[0])).astype(BF)
    for device in range(out_ref.shape[0]):
        out_ref[device] = mean


def place_rows_kernel(mine_ref, theirs_ref, out_ref):
    for sec in range(2):

        def run(sec=sec):
            for n in range(3):
                packed = slice(n * FIELD, (n + 1) * FIELD)
                for core, ref in ((sec, mine_ref), (1 - sec, theirs_ref)):
                    out_ref[n, :, BLK * core : BLK * core + BLK, :] = ref[packed, :].reshape(OWN, BLK, 128)

        pl.when(lax.axis_index("sec") == sec)(run)


def spread_gradients_kernel(own_ref, partner_ref, first_ref, bias_ref, second_ref, third_t_ref):
    section = lax.axis_index("sec")
    hid = second_ref.shape[0]
    share = own_ref.shape[1]

    def feature_rows(out, row, lanes, lev, values):
        group, at = divmod(row, GROUP)
        if at < 3 * OWN:
            field, level = divmod(at, OWN)
            to = (2 * field + (lev + group) % 2) * OWN + level
            out[to : to + 8, lanes] = values

    def run(sec):
        blocks = [(tile, lev, core) for tile in range(own_ref.shape[0] // 2) for lev in range(2) for core in range(2)]
        for tile, lev, core in blocks:
            lanes = slice(256 * lev + 128 * core, 256 * lev + 128 * core + 128)
            block = (own_ref if core == sec else partner_ref)[2 * tile + lev].astype(F32)
            for part in range(0, share, 8):
                row = tile * share + part
                values = block[part : part + 8, :]
                if row < 2 * GROUP:
                    feature_rows(first_ref, row, lanes, lev, values)
                    if row == 3 * OWN:
                        bias_ref[:, lanes] = values[:1, :]
                elif row < 2 * GROUP + hid:
                    second_ref[row - 2 * GROUP : row - 2 * GROUP + 8, lanes] = values
                else:
                    feature_rows(third_t_ref, row - 2 * GROUP - hid, lanes, lev, values)

    for sec in range(2):
        pl.when(section == sec)(lambda sec=sec: run(sec))


def whole(value):
    return pl.BlockSpec(value.shape, lambda i: (0,) * len(value.shape), pipeline_mode=pl.Buffered(1))


def stripes(value, along):
    if along:
        return pl.BlockSpec((value.shape[0], STRIPE), lambda i: (0, i))
    return pl.BlockSpec((STRIPE // 128 * GROUP, 128), lambda i: (i, 0))


def first_rows(rows, value):
    return pl.BlockSpec((rows, *value.shape[1:]), lambda i: (0,) * len(value.shape), pipeline_mode=pl.Buffered(1))


def call(kernel, n_smem, operands, outs, scratch=(), flops=0, limit=40, steps=1, in_along=None, out_along=None):
    def specs(values, along):
        along = along or [None] * len(values)
        return [whole(v) if at is None else first_rows(at, v) if at > 1 else stripes(v, at) for v, at in zip(values, along, strict=True)]

    smem = pl.BlockSpec(memory_space=pltpu.SMEM)
    return pl.pallas_call(
        kernel,
        grid=(steps,),
        out_shape=outs,
        in_specs=[smem] * n_smem + specs(operands[n_smem:], in_along),
        out_specs=specs(outs, out_along),
        scratch_shapes=list(scratch),
        compiler_params=pltpu.CompilerParams(vmem_limit_bytes=limit * MIB),
        cost_estimate=pl.CostEstimate(flops=flops, bytes_accessed=0, transcendentals=0),
    )(*operands)


def stencil_scratch(extra=()):
    mass = pltpu.VMEM((EXT + 4, ROWS, 128), F32)
    wind = pltpu.VMEM((EXT, ROWS, 128), F32)
    return [mass, mass, wind, wind, pltpu.VMEM((256, 128), BF), *extra]


def shape(*dims, dtype=F32):
    return jax.ShapeDtypeStruct(dims, dtype)


def swap(value, axis):
    return lax.ppermute(value, axis, [(0, 1), (1, 0)])


def strip_swaps(strip, edges, tiles):
    pairs = [(tiles + t, t + 1) for t in range(tiles - 1)]
    pairs += [(b, a) for a, b in pairs]
    cross = [(2 * a + lev, 2 * b + 1 - lev) for a, b in pairs for lev in range(2)]
    return lax.ppermute(strip, ("sec", "tile"), pairs), lax.ppermute(edges, ("sec", "tile", "lev"), cross)


def local(state, sound, target, edge_turn, w_first, b_first, w_second, w_third):
    tiles = lax.axis_size("tile")
    hid, feats = w_second.shape[0], 2 * GROUP

    state, sound, target = state.reshape(-1, 128), sound.reshape(-1, 128), target.reshape(-1, 128)
    strip, edges, columns, first, third_t = call(
        pack_kernel, 1, (edge_turn, state, sound, w_first, w_third.T, b_first[None]),
        (shape(8 * FIELD + 16, 128, dtype=BF), shape(4 * RIM, 128, dtype=BF), shape(BLK * GROUP + RIM, 128, dtype=BF), shape(feats, hid, dtype=BF), shape(feats, hid, dtype=BF)),
        limit=60,
    )
    own_col = swap(columns, "lev")
    strip, rims = strip_swaps(strip, edges, tiles)

    activations = (shape(feats, COLS, dtype=BF), shape(hid, COLS, dtype=BF), shape(hid, COLS, dtype=BF), shape(hid, COLS), shape(hid, COLS))
    feat, one, two, slope_one, slope_two, tendency = call(
        network_kernel, 0, (columns, own_col, first, w_second, third_t, target),
        (*activations, shape(3 * FIELD, 128)),
        steps=COLS // STRIPE, flops=LONG, in_along=(0, 0, None, None, None, None), out_along=(1, 1, 1, 1, 1, None),
    )

    other_col = swap(own_col, "sec")
    strip, rims, tendency = lax.optimization_barrier((strip, rims, tendency))
    resid, r_rows, r_columns, coeff, factors = call(
        forward_kernel, 1,
        (edge_turn, state, sound, tendency, strip, swap(strip, "sec"), rims, swap(rims, "sec"), own_col, other_col),
        (shape(3 * FIELD, 128), shape(3 * FIELD, 128, dtype=BF), shape(BLK * GROUP, 128, dtype=BF), shape(EXT, ROWS, 128), shape(4, BLK, 128)),
        stencil_scratch(), flops=LONG, in_along=(*[None] * 4, 4 * FIELD + 16, *[None] * 4),
    )

    r_own_col = swap(r_columns, "lev")
    r_other = swap(resid, "sec")
    r_strip, r_edges = call(
        join_kernel, 0, (r_rows, swap(r_rows, "sec")),
        (shape(6 * FIELD, 128, dtype=BF), shape(3 * RIM, 128, dtype=BF)), limit=16,
    )
    r_strip, r_rims = strip_swaps(r_strip, r_edges, tiles)
    n_rows = 2 * feats + hid
    given, kept, input_grad = call(
        back_kernel, 0, (r_columns, r_own_col, feat, third_t, w_second, first, one, two, slope_one, slope_two),
        (shape(n_rows, 128, dtype=BF), shape(n_rows, 128), shape(3 * FIELD, 128)),
        (pltpu.VMEM((hid, STRIPE), BF), pltpu.VMEM((hid, STRIPE), BF), pltpu.VMEM((n_rows, 256), F32)),
        flops=LONG, steps=COLS // STRIPE, in_along=(0, 0, 1, None, None, None, 1, 1, 1, 1),
    )
    received = swap(given, "sec")
    share = n_rows // tiles
    (partial,) = call(add_kernel, 0, (kept, received), (shape(n_rows, 128, dtype=BF),), limit=16)
    partial = partial.reshape(tiles, share, 128)
    parts = lax.all_to_all(partial, "tile", 0, 0)
    (everywhere,) = call(mean_kernel, 0, (parts,), (shape(2 * tiles, share, 128, dtype=BF),), limit=16)
    everywhere, coeff, r_strip, r_rims = lax.optimization_barrier((everywhere, coeff, r_strip, r_rims))
    r_partner, r_partner_rims, r_other_col = swap(r_strip, "sec"), swap(r_rims, "sec"), swap(r_own_col, "sec")
    gathered = lax.all_to_all(everywhere, ("tile", "lev"), 0, 0)
    (mine,) = call(
        adjoint_kernel, 0,
        (resid, r_other, input_grad, coeff, factors, r_strip, r_partner, r_rims, r_partner_rims, r_own_col, r_other_col),
        (shape(3 * FIELD, 128),), stencil_scratch((pltpu.VMEM((EXT, ROWS, 128), F32),)), flops=LONG, limit=60,
        in_along=(*[None] * 6, 3 * FIELD, *[None] * 4),
    )
    theirs, gathered = lax.optimization_barrier((swap(mine, "sec"), gathered))
    (state_grad,) = call(place_rows_kernel, 0, (mine, theirs), (shape(3, OWN, 2 * BLK, 128),), limit=16)
    g_first, g_bias, g_second, g_third_t = call(
        spread_gradients_kernel, 0, (gathered, swap(gathered, "sec")),
        (shape(6 * OWN, hid), shape(1, hid), shape(hid, hid), shape(6 * OWN, hid)), limit=16,
    )
    return (state_grad, g_first, g_bias.reshape(hid), g_second, g_third_t.T)


def solution(mesh):
    placed = (
        P(None, "lev", "tile", None),
        P("lev", "tile", None),
        P(None, "lev", "tile", None),
        P("tile", None),
        P(),
        P(),
        P(),
        P(),
    )
    return jax.shard_map(
        local,
        mesh=mesh,
        in_specs=placed,
        out_specs=(P(None, "lev", "tile", None), P(), P(), P(), P()),
        check_vma=False,
    )
```

```python
import jax
import jax.numpy as jnp
from jax import lax
from jax.experimental import pallas as pl
from jax.experimental.pallas import tpu as pltpu
from jax.sharding import PartitionSpec as P

SUBSTEPS = 4
COURANT = 0.3
DIFFUSION = 0.08
UNIT = 1.0 / 12.0

BLK = 8
OWN = 40
EDGE = 8
EXT = OWN + EDGE
ROWS = 7 * BLK
WIND_BLOCKS = ((0, 5), (0, 5), (1, 4), (1, 4))
MASS_BLOCKS = ((0, 5), (1, 4), (1, 4), (2, 3))
FIELD = OWN * BLK
RIM = EDGE * BLK
NEAR_EDGE, FAR_EDGE = 6, 2
COLS = BLK * 128
GROUP = 128
PAD = GROUP - 3 * OWN
STRIPE = 512
MIB = 1024 * 1024
LONG = 20_000_000_000
F32 = jnp.float32
BF = jnp.bfloat16


def roll(values, steps, axis):
    return pltpu.roll(values, steps % values.shape[axis], axis)


def across_matrix():
    source = lax.broadcasted_iota(jnp.int32, (256, 128), 0)
    target = lax.broadcasted_iota(jnp.int32, (256, 128), 1)
    apart = (source - target) & 127
    near = jnp.where(apart == 1, 8.0, 0.0) - jnp.where(apart == 127, 8.0, 0.0)
    far = jnp.where(apart == 126, 1.0, 0.0) - jnp.where(apart == 2, 1.0, 0.0)
    return (near + far).astype(BF)


def across(values, matrix):
    flat = values.reshape(-1, 128)
    high = flat.astype(BF)
    low = (flat - high.astype(F32)).astype(BF)
    return dot(jnp.concatenate([high, low], axis=1), matrix[...]).reshape(values.shape)


def along(ref, levels, row):
    def take(steps):
        return ref[levels, row + steps : row + steps + BLK, :]

    return 8.0 * (take(1) - take(-1)) - (take(2) - take(-2))


def vertical(ref, k, size, row):
    v = ref[pl.ds(k, size + 4), row : row + BLK, :]
    near = v[3 : 3 + size] + v[1 : 1 + size]
    far = v[4 : 4 + size] + v[0:size]
    return (1.0 - 30.0 * UNIT * DIFFUSION) * v[2 : 2 + size] + (UNIT * DIFFUSION) * (16.0 * near - far)


def edge_masks():
    i = lax.broadcasted_iota(jnp.int32, (1, BLK, 128), 1)

    def at(row, value):
        return jnp.where(i == row, value, 0.0)

    return at(4, -8.0), at(4, 1.0) + at(5, 1.0), at(3, 8.0), at(3, -1.0) + at(2, -1.0)


def crossing(values, masks):
    m1, m2, m3, m4 = masks
    return (
        m1 * roll(values, 1, 1)
        + m2 * roll(values, 2, 1)
        + m3 * roll(values, -1, 1)
        + m4 * roll(values, -2, 1)
    )


def quarter_turn(quarter):
    cosine = jnp.where(quarter == 0, 1.0, 0.0) - jnp.where(quarter == 2, 1.0, 0.0)
    sine = jnp.where(quarter == 1, 1.0, 0.0) - jnp.where(quarter == 3, 1.0, 0.0)
    return cosine, sine


def clear(ref):
    levels = ref.shape[0]
    zeros = jnp.zeros((levels, BLK, 128), F32)
    ref[:, 0:BLK, :] = zeros
    ref[:, ROWS - BLK : ROWS, :] = zeros


def clear_levels(ref):
    for level in (0, 1, EXT + 2, EXT + 3):
        ref[level] = jnp.zeros((ROWS, 128), F32)


def spread(src, start, count, dst, level, row, scale=None):
    def body(i, _):
        rows = src[pl.ds(pl.multiple_of(start + i * 16, 16), 16), :].astype(F32)
        if scale is not None:
            rows = rows * scale
        dst[pl.ds(level + 2 * i, 2), row : row + BLK, :] = rows.reshape(2, BLK, 128)
        return 0

    if count > EDGE:
        lax.fori_loop(0, count // 2, body, 0, unroll=20)
    else:
        for i in range(count // 2):
            body(i, 0)


def spread_column_edge(columns, n, dst, level, row, lev, scale=None):
    if n == 3:
        spread(columns, BLK * GROUP, EDGE, dst, level, row, scale)
        return
    skip = n * OWN % 16
    for r in range(BLK):
        start = pl.multiple_of(r * GROUP + n * OWN - skip + (OWN - EDGE) * lev, 16)
        values = columns[pl.ds(start, 16), :].astype(F32)
        dst[pl.ds(level, EDGE), row + r, :] = values[skip : skip + EDGE, :]


def static_rows(sec):
    return 32 - 16 * sec, 24 + 8 * sec, 40 - 24 * sec


def spread_rims(sec, lev, strip, partner, rims, partner_rims, own_col, other_col, fields):
    own_level, edge_level = EDGE * lev, OWN * (1 - lev)
    count = len(fields)
    far_start = strip.shape[0] - count * FIELD
    far_row, near_row, partner_row = (8, 16, 40) if sec == 0 else (40, 32, 8)
    near_level, far_level = edge_level + (EDGE - NEAR_EDGE) * lev, edge_level + (EDGE - FAR_EDGE) * lev
    for n, (dst, shift, scale) in enumerate(fields):
        dst[pl.ds(edge_level + shift, EDGE), :, :] = jnp.zeros((EDGE, ROWS, 128), F32)
        spread(strip, far_start + n * FIELD, OWN, dst, own_level + shift, far_row, scale)
        spread(strip, n * FIELD, OWN, dst, own_level + shift, near_row, scale)
        spread(partner, n * FIELD, OWN, dst, own_level + shift, partner_row, scale)
        spread(rims, n * RIM, NEAR_EDGE, dst, near_level + shift, near_row, scale)
        spread(partner_rims, n * RIM, NEAR_EDGE, dst, near_level + shift, partner_row, scale)
        spread(rims, n * RIM + NEAR_EDGE * BLK, FAR_EDGE, dst, far_level + shift, far_row, scale)
        for columns, row in ((own_col, 3 * BLK), (other_col, static_rows(sec)[0])):
            spread_column_edge(columns, n, dst, edge_level + shift, row, lev, scale)


def column_rows(ref, row, start, stride, step, fill):
    fields = [ref[pl.ds(n * step + start + row, OWN, stride=stride), :] for n in range(3)]
    return jnp.concatenate([*fields, jnp.full((PAD, 128), fill, F32)], axis=0).astype(BF)


def by_group(out_ref, weights_ref, lev, bias_ref=None):
    hid = out_ref.shape[1]
    values = weights_ref[...].astype(F32)
    padding = jnp.zeros((PAD, hid), F32)
    own_padding = padding
    if bias_ref is not None:
        rest = bias_ref[...]
        row = lax.broadcasted_iota(jnp.int32, (PAD, hid), 0)
        for n in range(3):
            part = rest.astype(BF).astype(F32)
            own_padding = jnp.where(row == n, part, own_padding)
            rest = rest - part
    groups = [[values[(2 * n + g) * OWN : (2 * n + g + 1) * OWN] for n in range(3)] for g in range(2)]
    for group in range(2):

        def run(group=group):
            parts = [*groups[group], own_padding, *groups[1 - group], padding]
            out_ref[...] = jnp.concatenate(parts, axis=0).astype(BF)

        pl.when(lev == group)(run)


def corner(edge_ref, n, near_ref, near, far_ref, far, lev):
    for src, start, at, levels in ((near_ref, near, 0, NEAR_EDGE), (far_ref, far, NEAR_EDGE, FAR_EDGE)):
        rows = pl.ds(pl.multiple_of(start + (OWN - levels) * BLK * (1 - lev), 16), levels * BLK)
        edge_ref[n * RIM + at * BLK : n * RIM + (at + levels) * BLK, :] = src[rows, :]


def pack_kernel(
    turn_ref, state_ref, sound_ref, first_ref, third_t_ref, bias_ref,
    strip_ref, edge_ref, column_ref, first_out_ref, third_out_ref,
):
    sec, lev = lax.axis_index("sec"), lax.axis_index("lev")
    by_group(first_out_ref, first_ref, lev, bias_ref)
    by_group(third_out_ref, third_t_ref, lev)
    far_start = 4 * FIELD + 16
    for half in range(2):

        def run(half=half):
            for n in range(4):
                src = state_ref[n * OWN * 16 : (n + 1) * OWN * 16, :] if n < 3 else sound_ref[...]
                for at, block in ((n * FIELD, half), (far_start + n * FIELD, 1 - half)):
                    field = src.reshape(OWN, 16, 128)[:, block * BLK : block * BLK + BLK, :]
                    strip_ref[at : at + FIELD, :] = field.reshape(FIELD, 128).astype(BF)
            for r in range(BLK):
                features = column_rows(state_ref, r, BLK * half, 16, OWN * 16, 1.0)
                column_ref[r * GROUP : (r + 1) * GROUP, :] = features

        pl.when(sec == half)(run)
    for n in range(4):
        near, far = n * FIELD, far_start + n * FIELD
        if n == 3:
            start = pl.multiple_of(near + (FIELD - RIM) * (1 - lev), 16)
            column_ref[BLK * GROUP :, :] = strip_ref[pl.ds(start, RIM), :]
        corner(edge_ref, n, strip_ref, near, strip_ref, far, lev)
    i = lax.broadcasted_iota(jnp.int32, (16, 128), 0)
    factors = jnp.zeros((16, 128), F32)
    for n, value in enumerate((*quarter_turn(turn_ref[0, 0]), *quarter_turn(turn_ref[0, 1]))):
        factors = jnp.where(i == n, value, factors)
    strip_ref[4 * FIELD : far_start, :] = factors.astype(BF)


def forward_kernel(
    turn_ref, state_ref, sound_ref, tendency_ref,
    strip, partner, rims, partner_rims, own_col, other_col,
    resid_ref, rows_ref, column_ref, c_ref, factor_ref, pa, pb, u, v, matrix,
):
    section, lev = lax.axis_index("sec"), lax.axis_index("lev")
    own_level = EDGE * lev
    for ref in (pa, pb, u, v, c_ref):
        clear(ref)
    clear_levels(pa)
    clear_levels(pb)
    cos_low, sin_low = quarter_turn(turn_ref[0, 0])
    cos_high, sin_high = quarter_turn(turn_ref[0, 1])
    below = lax.broadcasted_iota(jnp.int32, (BLK, 128), 0) < 4

    def factors(low, high):
        low = low[4 * FIELD : 4 * FIELD + 16, :].astype(F32)
        high = high[4 * FIELD : 4 * FIELD + 16, :].astype(F32)
        factor_ref[0] = jnp.where(below, cos_low, low[2:3, :]) - 1.0
        factor_ref[1] = jnp.where(below, sin_low, low[3:4, :])
        factor_ref[2] = jnp.where(below, high[0:1, :], cos_high) - 1.0
        factor_ref[3] = jnp.where(below, high[1:2, :], sin_high)

    pl.when(section == 0)(lambda: factors(strip, partner))
    pl.when(section == 1)(lambda: factors(partner, strip))
    masks = edge_masks()
    matrix[...] = across_matrix()

    def run(sec):
        unit = COURANT * UNIT
        spread_rims(
            sec, lev, strip, partner, rims, partner_rims, own_col, other_col,
            ((pa, 2, None), (u, 0, None), (v, 0, None), (c_ref, 0, unit)),
        )
        _, near_edge, far_edge = static_rows(sec)
        tile_row = 24 - 8 * sec
        for n, (dst, shift) in enumerate(((pa, 2), (u, 0), (v, 0))):
            field = state_ref[n * OWN * 16 : (n + 1) * OWN * 16, :].reshape(OWN, 16, 128)
            dst[pl.ds(own_level + shift, OWN), tile_row : tile_row + 16, :] = field
        field = unit * sound_ref[...].reshape(OWN, 16, 128)
        c_ref[pl.ds(own_level, OWN), tile_row : tile_row + 16, :] = field
        near_factor, far_factor = (0, 2) if sec == 0 else (2, 0)
        for step in range(SUBSTEPS):
            old, new = (pa, pb) if step % 2 == 0 else (pb, pa)

            def body(step=step, old=old, new=new):
                k, size = 0, EXT
                levels = pl.ds(k, size)
                inner = pl.ds(k + 2, size)
                first, last = WIND_BLOCKS[step]
                wide = slice(BLK + BLK * first, BLK + BLK * last)
                slopes = across(old[inner, wide, :], matrix)
                for block in range(first, last):
                    row = BLK + BLK * block
                    rows = slice(row, row + BLK)
                    c = c_ref[levels, rows, :]
                    u[levels, rows, :] = u[levels, rows, :] - c * along(old, inner, row)
                    at = BLK * (block - first)
                    v[levels, rows, :] = v[levels, rows, :] - c * slopes[:, at : at + BLK, :]
                first, last = MASS_BLOCKS[step]
                narrow = slice(BLK + BLK * first, BLK + BLK * last)
                slopes = across(v[levels, narrow, :], matrix)
                for block in range(first, last):
                    row = BLK + BLK * block
                    rows = slice(row, row + BLK)
                    at = BLK * (block - first)
                    spread_uv = along(u, levels, row) + slopes[:, at : at + BLK, :]
                    new[inner, rows, :] = vertical(old, k, size, row) - c_ref[levels, rows, :] * spread_uv
                for edge, f in ((near_edge, near_factor), (far_edge, far_factor))[: 2 if step < 2 else 1]:
                    rows = slice(edge - 4, edge + 4)
                    delta = factor_ref[f] * u[levels, rows, :] - factor_ref[f + 1] * v[levels, rows, :]
                    new[inner, rows, :] = new[inner, rows, :] - c_ref[levels, rows, :] * crossing(delta, masks)

            body()
        final = pa if SUBSTEPS % 2 == 0 else pb
        for n, (src, shift) in enumerate(((final, 2), (u, 0), (v, 0))):
            evolved = src[pl.ds(own_level + shift, OWN), 3 * BLK : 4 * BLK, :]
            packed = slice(n * FIELD, (n + 1) * FIELD)
            resid = evolved.reshape(FIELD, 128) + tendency_ref[packed, :]
            resid_ref[packed, :] = resid
            rows_ref[packed, :] = resid.astype(BF)

    for sec in range(2):
        pl.when(section == sec)(lambda sec=sec: run(sec))
    for r in range(BLK):
        column_ref[r * GROUP : (r + 1) * GROUP, :] = column_rows(resid_ref, r, 0, BLK, FIELD, 0.0)


def adjoint_kernel(
    resid_ref, other_ref, input_grad_ref, c_ref, factor_ref,
    strip, partner, rims, partner_rims, own_col, other_col,
    out_ref, pa, pb, u, v, matrix, w,
):
    section, lev = lax.axis_index("sec"), lax.axis_index("lev")
    own_level = EDGE * lev
    for ref in (pa, pb, u, v, w):
        clear(ref)
    clear_levels(pa)
    clear_levels(pb)
    masks = edge_masks()
    matrix[...] = across_matrix()

    def run(sec):
        spread_rims(
            sec, lev, strip, partner, rims, partner_rims, own_col, other_col,
            ((pa, 2, None), (u, 0, None), (v, 0, None)),
        )
        other_row, near_edge, far_edge = static_rows(sec)
        for n, (dst, shift) in enumerate(((pa, 2), (u, 0), (v, 0))):
            at = pl.ds(own_level + shift, OWN)
            packed = slice(n * FIELD, (n + 1) * FIELD)
            dst[at, 3 * BLK : 4 * BLK, :] = resid_ref[packed, :].reshape(OWN, BLK, 128)
            dst[at, other_row : other_row + BLK, :] = other_ref[packed, :].reshape(OWN, BLK, 128)
        near_factor, far_factor = (0, 2) if sec == 0 else (2, 0)
        for step in range(SUBSTEPS):
            old, new = (pa, pb) if step % 2 == 0 else (pb, pa)
            first, last = WIND_BLOCKS[step]
            wide = slice(BLK + BLK * max(first - 1, 0), BLK + BLK * min(last + 1, 5))
            first, last = MASS_BLOCKS[step]
            narrow = slice(BLK + BLK * max(first - 1, 0), BLK + BLK * min(last + 1, 5))

            def body(step=step, old=old, new=new, wide=wide, narrow=narrow):
                k, size = 0, EXT
                whole = pl.ds(0, size)
                levels = pl.ds(k, size)
                inner = pl.ds(k + 2, size)
                w[whole, wide, :] = c_ref[levels, wide, :] * old[inner, wide, :]
                first, last = WIND_BLOCKS[step]
                slopes = across(w[whole, BLK + BLK * first : BLK + BLK * last, :], matrix)
                for block in range(first, last):
                    row = BLK + BLK * block
                    rows = slice(row, row + BLK)
                    u[levels, rows, :] = u[levels, rows, :] + along(w, whole, row)
                    at = BLK * (block - first)
                    v[levels, rows, :] = v[levels, rows, :] + slopes[:, at : at + BLK, :]
                for edge, f in ((near_edge, near_factor), (far_edge, far_factor))[: 2 if step < 2 else 1]:
                    rows = slice(edge - 4, edge + 4)
                    cross = crossing(w[whole, rows, :], masks)
                    u[levels, rows, :] = u[levels, rows, :] + factor_ref[f] * cross
                    v[levels, rows, :] = v[levels, rows, :] - factor_ref[f + 1] * cross
                w[whole, narrow, :] = c_ref[levels, narrow, :] * u[levels, narrow, :]
                first, last = MASS_BLOCKS[step]
                rows = slice(BLK + BLK * first, BLK + BLK * last)
                slopes = across(c_ref[levels, rows, :] * v[levels, rows, :], matrix)
                for block in range(first, last):
                    row = BLK + BLK * block
                    at = BLK * (block - first)
                    spread_uv = along(w, whole, row) + slopes[:, at : at + BLK, :]
                    new[inner, row : row + BLK, :] = vertical(old, k, size, row) + spread_uv

            body()

    for sec in range(2):
        pl.when(section == sec)(lambda sec=sec: run(sec))
    final = pa if SUBSTEPS % 2 == 0 else pb
    for n, (src, shift) in enumerate(((final, 2), (u, 0), (v, 0))):
        packed = slice(n * FIELD, (n + 1) * FIELD)
        adjoint = src[pl.ds(own_level + shift, OWN), 3 * BLK : 4 * BLK, :].reshape(FIELD, 128)
        out_ref[packed, :] = adjoint + input_grad_ref[packed, :]


def dot(left, right):
    return lax.dot_general(left, right, (((1,), (0,)), ((), ())), preferred_element_type=F32)


def dot_t(left, right):
    return lax.dot_general(left, right, (((0,), (0,)), ((), ())), preferred_element_type=F32)


def dot_columns(left, right):
    return lax.dot_general(left, right, (((1,), (1,)), ((), ())), preferred_element_type=F32)


def silu_and_slope(values):
    sigma = 0.5 * jnp.tanh(0.5 * values) + 0.5
    silu = values * sigma
    return silu.astype(BF), sigma + silu * (1.0 - sigma)


def both_groups(own_ref, other_ref):
    parts = [
        jnp.concatenate([ref[r * GROUP : (r + 1) * GROUP, :] for ref in (own_ref, other_ref)], axis=0)
        for r in range(STRIPE // 128)
    ]
    return jnp.concatenate(parts, axis=1)


def to_fields(out_ref, first, values, minus_ref=None, minus_first=None):
    for r in range(STRIPE // 128):
        for n in range(3):
            value = values[n * OWN : (n + 1) * OWN, r * 128 : (r + 1) * 128]
            if minus_ref is not None:
                value = value - minus_ref[pl.ds(n * OWN * 16 + minus_first + r, OWN, stride=16), :]
            out_ref[pl.ds(n * FIELD + first + r, OWN, stride=BLK), :] = value


def network_kernel(
    own_ref, other_ref, first_ref, second_ref, third_t_ref, target_ref,
    feat_ref, one_ref, two_ref, slope_one_ref, slope_two_ref, tendency_ref,
):
    feat = both_groups(own_ref, other_ref)
    feat_ref[...] = feat
    one, slope = silu_and_slope(dot_t(first_ref[...], feat))
    one_ref[...] = one
    slope_one_ref[...] = slope
    two, slope = silu_and_slope(dot_t(second_ref[...], one))
    two_ref[...] = two
    slope_two_ref[...] = slope
    row = pl.program_id(0) * (STRIPE // 128)
    at = BLK * lax.axis_index("sec") + row
    to_fields(tendency_ref, row, dot(third_t_ref[:GROUP, :], two), target_ref, at)


def back_kernel(
    own_ref, other_ref, feat_ref, third_t_ref, second_ref, first_ref, one_ref, two_ref, slope_one_ref, slope_two_ref,
    given_ref, kept_ref, input_grad_ref, err_one_ref, err_two_ref, total_ref,
):
    step = pl.program_id(0)
    resid = both_groups(own_ref, other_ref)
    err_two = (dot_t(third_t_ref[...], resid) * slope_two_ref[...]).astype(BF)
    err_two_ref[...] = err_two
    err_one = (dot(second_ref[...], err_two) * slope_one_ref[...]).astype(BF)
    err_one_ref[...] = err_one
    to_fields(input_grad_ref, step * (STRIPE // 128), dot(first_ref[:GROUP, :], err_one))
    feats, hid = feat_ref.shape[0], one_ref.shape[0]
    half = pl.ds(pl.multiple_of(256 * lax.axis_index("lev"), 256), 256)

    def clear_total():
        total_ref[...] = jnp.zeros(total_ref.shape, F32)

    pl.when(step == 0)(clear_total)

    def add(rows, left, right):
        total_ref[rows, :] = total_ref[rows, :] + dot_columns(left, right)

    add(slice(0, feats), feat_ref[...], err_one_ref[half, :])
    add(slice(feats, feats + hid), one_ref[...], err_two_ref[half, :])
    add(slice(feats + hid, 2 * feats + hid), resid, two_ref[half, :])

    def finish():
        for sec in range(2):

            def share(sec=sec):
                kept_ref[...] = total_ref[:, 128 * sec : 128 * sec + 128]
                given_ref[...] = total_ref[:, 128 - 128 * sec : 256 - 128 * sec].astype(BF)

            pl.when(lax.axis_index("sec") == sec)(share)

    pl.when(step == COLS // STRIPE - 1)(finish)


def join_kernel(near_ref, far_ref, strip_ref, edge_ref):
    strip_ref[: 3 * FIELD, :] = near_ref[...]
    strip_ref[3 * FIELD :, :] = far_ref[...]
    for n in range(3):
        corner(edge_ref, n, near_ref, n * FIELD, far_ref, n * FIELD, lax.axis_index("lev"))


def add_kernel(kept_ref, received_ref, out_ref):
    out_ref[...] = (kept_ref[...] + received_ref[...].astype(F32)).astype(BF)


def mean_kernel(parts_ref, out_ref):
    total = parts_ref[0].astype(F32)
    for tile in range(1, parts_ref.shape[0]):
        total = total + parts_ref[tile].astype(F32)
    mean = (total / (COLS * out_ref.shape[0])).astype(BF)
    for device in range(out_ref.shape[0]):
        out_ref[device] = mean


def place_rows_kernel(mine_ref, theirs_ref, out_ref):
    for sec in range(2):

        def run(sec=sec):
            for n in range(3):
                packed = slice(n * FIELD, (n + 1) * FIELD)
                for core, ref in ((sec, mine_ref), (1 - sec, theirs_ref)):
                    out_ref[n, :, BLK * core : BLK * core + BLK, :] = ref[packed, :].reshape(OWN, BLK, 128)

        pl.when(lax.axis_index("sec") == sec)(run)


def spread_gradients_kernel(own_ref, partner_ref, first_ref, bias_ref, second_ref, third_t_ref):
    section = lax.axis_index("sec")
    hid = second_ref.shape[0]
    share = own_ref.shape[1]

    def feature_rows(out, row, lanes, lev, values):
        group, at = divmod(row, GROUP)
        if at < 3 * OWN:
            field, level = divmod(at, OWN)
            to = (2 * field + (lev + group) % 2) * OWN + level
            out[to : to + 8, lanes] = values

    def run(sec):
        blocks = [(tile, lev, core) for tile in range(own_ref.shape[0] // 2) for lev in range(2) for core in range(2)]
        for tile, lev, core in blocks:
            lanes = slice(256 * lev + 128 * core, 256 * lev + 128 * core + 128)
            block = (own_ref if core == sec else partner_ref)[2 * tile + lev].astype(F32)
            for part in range(0, share, 8):
                row = tile * share + part
                values = block[part : part + 8, :]
                if row < 2 * GROUP:
                    feature_rows(first_ref, row, lanes, lev, values)
                    if row == 3 * OWN:
                        bias_ref[:, lanes] = values[:1, :]
                elif row < 2 * GROUP + hid:
                    second_ref[row - 2 * GROUP : row - 2 * GROUP + 8, lanes] = values
                else:
                    feature_rows(third_t_ref, row - 2 * GROUP - hid, lanes, lev, values)

    for sec in range(2):
        pl.when(section == sec)(lambda sec=sec: run(sec))


def whole(value):
    return pl.BlockSpec(value.shape, lambda i: (0,) * len(value.shape), pipeline_mode=pl.Buffered(1))


def stripes(value, along):
    if along:
        return pl.BlockSpec((value.shape[0], STRIPE), lambda i: (0, i))
    return pl.BlockSpec((STRIPE // 128 * GROUP, 128), lambda i: (i, 0))


def first_rows(rows, value):
    return pl.BlockSpec((rows, *value.shape[1:]), lambda i: (0,) * len(value.shape), pipeline_mode=pl.Buffered(1))


def call(kernel, n_smem, operands, outs, scratch=(), flops=0, limit=40, steps=1, in_along=None, out_along=None):
    def specs(values, along):
        along = along or [None] * len(values)
        return [whole(v) if at is None else first_rows(at, v) if at > 1 else stripes(v, at) for v, at in zip(values, along, strict=True)]

    smem = pl.BlockSpec(memory_space=pltpu.SMEM)
    return pl.pallas_call(
        kernel,
        grid=(steps,),
        out_shape=outs,
        in_specs=[smem] * n_smem + specs(operands[n_smem:], in_along),
        out_specs=specs(outs, out_along),
        scratch_shapes=list(scratch),
        compiler_params=pltpu.CompilerParams(vmem_limit_bytes=limit * MIB),
        cost_estimate=pl.CostEstimate(flops=flops, bytes_accessed=0, transcendentals=0),
    )(*operands)


def stencil_scratch(extra=()):
    mass = pltpu.VMEM((EXT + 4, ROWS, 128), F32)
    wind = pltpu.VMEM((EXT, ROWS, 128), F32)
    return [mass, mass, wind, wind, pltpu.VMEM((256, 128), BF), *extra]


def shape(*dims, dtype=F32):
    return jax.ShapeDtypeStruct(dims, dtype)


def swap(value, axis):
    return lax.ppermute(value, axis, [(0, 1), (1, 0)])


def strip_swaps(strip, edges, tiles):
    pairs = [(tiles + t, t + 1) for t in range(tiles - 1)]
    pairs += [(b, a) for a, b in pairs]
    cross = [(2 * a + lev, 2 * b + 1 - lev) for a, b in pairs for lev in range(2)]
    return lax.ppermute(strip, ("sec", "tile"), pairs), lax.ppermute(edges, ("sec", "tile", "lev"), cross)


def local(state, sound, target, edge_turn, w_first, b_first, w_second, w_third):
    tiles = lax.axis_size("tile")
    hid, feats = w_second.shape[0], 2 * GROUP

    state, sound, target = state.reshape(-1, 128), sound.reshape(-1, 128), target.reshape(-1, 128)
    strip, edges, columns, first, third_t = call(
        pack_kernel, 1, (edge_turn, state, sound, w_first, w_third.T, b_first[None]),
        (shape(8 * FIELD + 16, 128, dtype=BF), shape(4 * RIM, 128, dtype=BF), shape(BLK * GROUP + RIM, 128, dtype=BF), shape(feats, hid, dtype=BF), shape(feats, hid, dtype=BF)),
        limit=60,
    )
    own_col = swap(columns, "lev")
    strip, rims = strip_swaps(strip, edges, tiles)

    activations = (shape(feats, COLS, dtype=BF), shape(hid, COLS, dtype=BF), shape(hid, COLS, dtype=BF), shape(hid, COLS), shape(hid, COLS))
    feat, one, two, slope_one, slope_two, tendency = call(
        network_kernel, 0, (columns, own_col, first, w_second, third_t, target),
        (*activations, shape(3 * FIELD, 128)),
        steps=COLS // STRIPE, flops=LONG, in_along=(0, 0, None, None, None, None), out_along=(1, 1, 1, 1, 1, None),
    )

    other_col = swap(own_col, "sec")
    strip, rims, tendency = lax.optimization_barrier((strip, rims, tendency))
    resid, r_rows, r_columns, coeff, factors = call(
        forward_kernel, 1,
        (edge_turn, state, sound, tendency, strip, swap(strip, "sec"), rims, swap(rims, "sec"), own_col, other_col),
        (shape(3 * FIELD, 128), shape(3 * FIELD, 128, dtype=BF), shape(BLK * GROUP, 128, dtype=BF), shape(EXT, ROWS, 128), shape(4, BLK, 128)),
        stencil_scratch(), flops=LONG, in_along=(*[None] * 4, 4 * FIELD + 16, *[None] * 4),
    )

    r_own_col = swap(r_columns, "lev")
    r_other = swap(resid, "sec")
    r_strip, r_edges = call(
        join_kernel, 0, (r_rows, swap(r_rows, "sec")),
        (shape(6 * FIELD, 128, dtype=BF), shape(3 * RIM, 128, dtype=BF)), limit=16,
    )
    r_strip, r_rims = strip_swaps(r_strip, r_edges, tiles)
    r_own_col, r_rims = lax.optimization_barrier((r_own_col, r_rims))

    n_rows = 2 * feats + hid
    given, kept, input_grad = call(
        back_kernel, 0, (r_columns, r_own_col, feat, third_t, w_second, first, one, two, slope_one, slope_two),
        (shape(n_rows, 128, dtype=BF), shape(n_rows, 128), shape(3 * FIELD, 128)),
        (pltpu.VMEM((hid, STRIPE), BF), pltpu.VMEM((hid, STRIPE), BF), pltpu.VMEM((n_rows, 256), F32)),
        flops=LONG, steps=COLS // STRIPE, in_along=(0, 0, 1, None, None, None, 1, 1, 1, 1),
    )
    received = swap(given, "sec")
    share = n_rows // tiles
    (partial,) = call(add_kernel, 0, (kept, received), (shape(n_rows, 128, dtype=BF),), limit=16)
    partial = partial.reshape(tiles, share, 128)
    parts = lax.all_to_all(partial, "tile", 0, 0)
    (everywhere,) = call(mean_kernel, 0, (parts,), (shape(2 * tiles, share, 128, dtype=BF),), limit=16, flops=LONG)
    everywhere, coeff = lax.optimization_barrier((everywhere, coeff))
    r_partner, r_partner_rims, r_other_col = swap(r_strip, "sec"), swap(r_rims, "sec"), swap(r_own_col, "sec")
    gathered = lax.all_to_all(everywhere, ("tile", "lev"), 0, 0)
    (mine,) = call(
        adjoint_kernel, 0,
        (resid, r_other, input_grad, coeff, factors, r_strip, r_partner, r_rims, r_partner_rims, r_own_col, r_other_col),
        (shape(3 * FIELD, 128),), stencil_scratch((pltpu.VMEM((EXT, ROWS, 128), F32),)), flops=LONG, limit=60,
        in_along=(*[None] * 6, 3 * FIELD, *[None] * 4),
    )
    theirs, gathered = lax.optimization_barrier((swap(mine, "sec"), gathered))
    (state_grad,) = call(place_rows_kernel, 0, (mine, theirs), (shape(3, OWN, 2 * BLK, 128),), limit=16)
    g_first, g_bias, g_second, g_third_t = call(
        spread_gradients_kernel, 0, (gathered, swap(gathered, "sec")),
        (shape(6 * OWN, hid), shape(1, hid), shape(hid, hid), shape(6 * OWN, hid)), limit=16,
    )
    return (state_grad, g_first, g_bias.reshape(hid), g_second, g_third_t.T)


def solution(mesh):
    placed = (
        P(None, "lev", "tile", None),
        P("lev", "tile", None),
        P(None, "lev", "tile", None),
        P("tile", None),
        P(),
        P(),
        P(),
        P(),
    )
    return jax.shard_map(
        local,
        mesh=mesh,
        in_specs=placed,
        out_specs=(P(None, "lev", "tile", None), P(), P(), P(), P()),
        check_vma=False,
    )
```

```python
import jax
import jax.numpy as jnp
from jax import lax
from jax.experimental import pallas as pl
from jax.experimental.pallas import tpu as pltpu
from jax.sharding import PartitionSpec as P

SUBSTEPS = 4
COURANT = 0.3
DIFFUSION = 0.08
UNIT = 1.0 / 12.0

BLK = 8
OWN = 40
EDGE = 8
EXT = OWN + EDGE
ROWS = 7 * BLK
WIND_BLOCKS = ((0, 5), (0, 5), (1, 4), (1, 4))
MASS_BLOCKS = ((0, 5), (1, 4), (1, 4), (2, 3))
FIELD = OWN * BLK
RIM = EDGE * BLK
NEAR_EDGE, FAR_EDGE = 6, 2
COLS = BLK * 128
GROUP = 128
PAD = GROUP - 3 * OWN
STRIPE = 512
MIB = 1024 * 1024
LONG = 20_000_000_000
F32 = jnp.float32
BF = jnp.bfloat16


def roll(values, steps, axis):
    return pltpu.roll(values, steps % values.shape[axis], axis)


def across_matrix():
    source = lax.broadcasted_iota(jnp.int32, (256, 128), 0)
    target = lax.broadcasted_iota(jnp.int32, (256, 128), 1)
    apart = (source - target) & 127
    near = jnp.where(apart == 1, 8.0, 0.0) - jnp.where(apart == 127, 8.0, 0.0)
    far = jnp.where(apart == 126, 1.0, 0.0) - jnp.where(apart == 2, 1.0, 0.0)
    return (near + far).astype(BF)


def across(values, matrix):
    flat = values.reshape(-1, 128)
    high = flat.astype(BF)
    low = (flat - high.astype(F32)).astype(BF)
    return dot(jnp.concatenate([high, low], axis=1), matrix[...]).reshape(values.shape)


def along(ref, levels, row):
    def take(steps):
        return ref[levels, row + steps : row + steps + BLK, :]

    return 8.0 * (take(1) - take(-1)) - (take(2) - take(-2))


def vertical(ref, k, size, row):
    v = ref[pl.ds(k, size + 4), row : row + BLK, :]
    near = v[3 : 3 + size] + v[1 : 1 + size]
    far = v[4 : 4 + size] + v[0:size]
    return (1.0 - 30.0 * UNIT * DIFFUSION) * v[2 : 2 + size] + (UNIT * DIFFUSION) * (16.0 * near - far)


def edge_masks():
    i = lax.broadcasted_iota(jnp.int32, (1, BLK, 128), 1)

    def at(row, value):
        return jnp.where(i == row, value, 0.0)

    return at(4, -8.0), at(4, 1.0) + at(5, 1.0), at(3, 8.0), at(3, -1.0) + at(2, -1.0)


def crossing(values, masks):
    m1, m2, m3, m4 = masks
    return (
        m1 * roll(values, 1, 1)
        + m2 * roll(values, 2, 1)
        + m3 * roll(values, -1, 1)
        + m4 * roll(values, -2, 1)
    )


def quarter_turn(quarter):
    cosine = jnp.where(quarter == 0, 1.0, 0.0) - jnp.where(quarter == 2, 1.0, 0.0)
    sine = jnp.where(quarter == 1, 1.0, 0.0) - jnp.where(quarter == 3, 1.0, 0.0)
    return cosine, sine


def clear(ref):
    levels = ref.shape[0]
    zeros = jnp.zeros((levels, BLK, 128), F32)
    ref[:, 0:BLK, :] = zeros
    ref[:, ROWS - BLK : ROWS, :] = zeros


def clear_levels(ref):
    for level in (0, 1, EXT + 2, EXT + 3):
        ref[level] = jnp.zeros((ROWS, 128), F32)


def spread(src, start, count, dst, level, row, scale=None):
    def body(i, _):
        rows = src[pl.ds(pl.multiple_of(start + i * 16, 16), 16), :].astype(F32)
        if scale is not None:
            rows = rows * scale
        dst[pl.ds(level + 2 * i, 2), row : row + BLK, :] = rows.reshape(2, BLK, 128)
        return 0

    if count > EDGE:
        lax.fori_loop(0, count // 2, body, 0, unroll=20)
    else:
        for i in range(count // 2):
            body(i, 0)


def spread_column_edge(columns, n, dst, level, row, lev, scale=None):
    if n == 3:
        spread(columns, BLK * GROUP, EDGE, dst, level, row, scale)
        return
    skip = n * OWN % 16
    for r in range(BLK):
        start = pl.multiple_of(r * GROUP + n * OWN - skip + (OWN - EDGE) * lev, 16)
        values = columns[pl.ds(start, 16), :].astype(F32)
        dst[pl.ds(level, EDGE), row + r, :] = values[skip : skip + EDGE, :]


def static_rows(sec):
    return 32 - 16 * sec, 24 + 8 * sec, 40 - 24 * sec


def spread_rims(sec, lev, strip, partner, rims, partner_rims, own_col, other_col, fields):
    own_level, edge_level = EDGE * lev, OWN * (1 - lev)
    count = len(fields)
    far_start = strip.shape[0] - count * FIELD
    far_row, near_row, partner_row = (8, 16, 40) if sec == 0 else (40, 32, 8)
    near_level, far_level = edge_level + (EDGE - NEAR_EDGE) * lev, edge_level + (EDGE - FAR_EDGE) * lev
    for n, (dst, shift, scale) in enumerate(fields):
        dst[pl.ds(edge_level + shift, EDGE), :, :] = jnp.zeros((EDGE, ROWS, 128), F32)
        spread(strip, far_start + n * FIELD, OWN, dst, own_level + shift, far_row, scale)
        spread(strip, n * FIELD, OWN, dst, own_level + shift, near_row, scale)
        spread(partner, n * FIELD, OWN, dst, own_level + shift, partner_row, scale)
        spread(rims, n * RIM, NEAR_EDGE, dst, near_level + shift, near_row, scale)
        spread(partner_rims, n * RIM, NEAR_EDGE, dst, near_level + shift, partner_row, scale)
        spread(rims, n * RIM + NEAR_EDGE * BLK, FAR_EDGE, dst, far_level + shift, far_row, scale)
        for columns, row in ((own_col, 3 * BLK), (other_col, static_rows(sec)[0])):
            spread_column_edge(columns, n, dst, edge_level + shift, row, lev, scale)


def column_rows(ref, row, start, stride, step, fill):
    fields = [ref[pl.ds(n * step + start + row, OWN, stride=stride), :] for n in range(3)]
    return jnp.concatenate([*fields, jnp.full((PAD, 128), fill, F32)], axis=0).astype(BF)


def by_group(out_ref, weights_ref, lev, bias_ref=None):
    hid = out_ref.shape[1]
    values = weights_ref[...].astype(F32)
    padding = jnp.zeros((PAD, hid), F32)
    own_padding = padding
    if bias_ref is not None:
        rest = bias_ref[...]
        row = lax.broadcasted_iota(jnp.int32, (PAD, hid), 0)
        for n in range(3):
            part = rest.astype(BF).astype(F32)
            own_padding = jnp.where(row == n, part, own_padding)
            rest = rest - part
    groups = [[values[(2 * n + g) * OWN : (2 * n + g + 1) * OWN] for n in range(3)] for g in range(2)]
    for group in range(2):

        def run(group=group):
            parts = [*groups[group], own_padding, *groups[1 - group], padding]
            out_ref[...] = jnp.concatenate(parts, axis=0).astype(BF)

        pl.when(lev == group)(run)


def corner(edge_ref, n, near_ref, near, far_ref, far, lev):
    for src, start, at, levels in ((near_ref, near, 0, NEAR_EDGE), (far_ref, far, NEAR_EDGE, FAR_EDGE)):
        rows = pl.ds(pl.multiple_of(start + (OWN - levels) * BLK * (1 - lev), 16), levels * BLK)
        edge_ref[n * RIM + at * BLK : n * RIM + (at + levels) * BLK, :] = src[rows, :]


def pack_kernel(
    turn_ref, state_ref, sound_ref, first_ref, third_t_ref, bias_ref,
    strip_ref, edge_ref, column_ref, first_out_ref, third_out_ref,
):
    sec, lev = lax.axis_index("sec"), lax.axis_index("lev")
    by_group(first_out_ref, first_ref, lev, bias_ref)
    by_group(third_out_ref, third_t_ref, lev)
    far_start = 4 * FIELD + 16
    for half in range(2):

        def run(half=half):
            for n in range(4):
                src = state_ref[n * OWN * 16 : (n + 1) * OWN * 16, :] if n < 3 else sound_ref[...]
                for at, block in ((n * FIELD, half), (far_start + n * FIELD, 1 - half)):
                    field = src.reshape(OWN, 16, 128)[:, block * BLK : block * BLK + BLK, :]
                    strip_ref[at : at + FIELD, :] = field.reshape(FIELD, 128).astype(BF)
            for r in range(BLK):
                features = column_rows(state_ref, r, BLK * half, 16, OWN * 16, 1.0)
                column_ref[r * GROUP : (r + 1) * GROUP, :] = features

        pl.when(sec == half)(run)
    for n in range(4):
        near, far = n * FIELD, far_start + n * FIELD
        if n == 3:
            start = pl.multiple_of(near + (FIELD - RIM) * (1 - lev), 16)
            column_ref[BLK * GROUP :, :] = strip_ref[pl.ds(start, RIM), :]
        corner(edge_ref, n, strip_ref, near, strip_ref, far, lev)
    i = lax.broadcasted_iota(jnp.int32, (16, 128), 0)
    factors = jnp.zeros((16, 128), F32)
    for n, value in enumerate((*quarter_turn(turn_ref[0, 0]), *quarter_turn(turn_ref[0, 1]))):
        factors = jnp.where(i == n, value, factors)
    strip_ref[4 * FIELD : far_start, :] = factors.astype(BF)


def forward_kernel(
    turn_ref, state_ref, sound_ref, tendency_ref,
    strip, partner, rims, partner_rims, own_col, other_col,
    resid_ref, rows_ref, column_ref, c_ref, factor_ref, pa, pb, u, v, matrix,
):
    section, lev = lax.axis_index("sec"), lax.axis_index("lev")
    own_level = EDGE * lev
    for ref in (pa, pb, u, v, c_ref):
        clear(ref)
    clear_levels(pa)
    clear_levels(pb)
    cos_low, sin_low = quarter_turn(turn_ref[0, 0])
    cos_high, sin_high = quarter_turn(turn_ref[0, 1])
    below = lax.broadcasted_iota(jnp.int32, (BLK, 128), 0) < 4

    def factors(low, high):
        low = low[4 * FIELD : 4 * FIELD + 16, :].astype(F32)
        high = high[4 * FIELD : 4 * FIELD + 16, :].astype(F32)
        factor_ref[0] = jnp.where(below, cos_low, low[2:3, :]) - 1.0
        factor_ref[1] = jnp.where(below, sin_low, low[3:4, :])
        factor_ref[2] = jnp.where(below, high[0:1, :], cos_high) - 1.0
        factor_ref[3] = jnp.where(below, high[1:2, :], sin_high)

    pl.when(section == 0)(lambda: factors(strip, partner))
    pl.when(section == 1)(lambda: factors(partner, strip))
    masks = edge_masks()
    matrix[...] = across_matrix()

    def run(sec):
        unit = COURANT * UNIT
        spread_rims(
            sec, lev, strip, partner, rims, partner_rims, own_col, other_col,
            ((pa, 2, None), (u, 0, None), (v, 0, None), (c_ref, 0, unit)),
        )
        _, near_edge, far_edge = static_rows(sec)
        tile_row = 24 - 8 * sec
        for n, (dst, shift) in enumerate(((pa, 2), (u, 0), (v, 0))):
            field = state_ref[n * OWN * 16 : (n + 1) * OWN * 16, :].reshape(OWN, 16, 128)
            dst[pl.ds(own_level + shift, OWN), tile_row : tile_row + 16, :] = field
        field = unit * sound_ref[...].reshape(OWN, 16, 128)
        c_ref[pl.ds(own_level, OWN), tile_row : tile_row + 16, :] = field
        near_factor, far_factor = (0, 2) if sec == 0 else (2, 0)
        for step in range(SUBSTEPS):
            old, new = (pa, pb) if step % 2 == 0 else (pb, pa)

            def body(step=step, old=old, new=new):
                k, size = 0, EXT
                levels = pl.ds(k, size)
                inner = pl.ds(k + 2, size)
                first, last = WIND_BLOCKS[step]
                wide = slice(BLK + BLK * first, BLK + BLK * last)
                slopes = across(old[inner, wide, :], matrix)
                for block in range(first, last):
                    row = BLK + BLK * block
                    rows = slice(row, row + BLK)
                    c = c_ref[levels, rows, :]
                    u[levels, rows, :] = u[levels, rows, :] - c * along(old, inner, row)
                    at = BLK * (block - first)
                    v[levels, rows, :] = v[levels, rows, :] - c * slopes[:, at : at + BLK, :]
                first, last = MASS_BLOCKS[step]
                narrow = slice(BLK + BLK * first, BLK + BLK * last)
                slopes = across(v[levels, narrow, :], matrix)
                for block in range(first, last):
                    row = BLK + BLK * block
                    rows = slice(row, row + BLK)
                    at = BLK * (block - first)
                    spread_uv = along(u, levels, row) + slopes[:, at : at + BLK, :]
                    new[inner, rows, :] = vertical(old, k, size, row) - c_ref[levels, rows, :] * spread_uv
                for edge, f in ((near_edge, near_factor), (far_edge, far_factor))[: 2 if step < 2 else 1]:
                    rows = slice(edge - 4, edge + 4)
                    delta = factor_ref[f] * u[levels, rows, :] - factor_ref[f + 1] * v[levels, rows, :]
                    new[inner, rows, :] = new[inner, rows, :] - c_ref[levels, rows, :] * crossing(delta, masks)

            body()
        final = pa if SUBSTEPS % 2 == 0 else pb
        for n, (src, shift) in enumerate(((final, 2), (u, 0), (v, 0))):
            evolved = src[pl.ds(own_level + shift, OWN), 3 * BLK : 4 * BLK, :]
            packed = slice(n * FIELD, (n + 1) * FIELD)
            resid = evolved.reshape(FIELD, 128) + tendency_ref[packed, :]
            resid_ref[packed, :] = resid
            rows_ref[packed, :] = resid.astype(BF)

    for sec in range(2):
        pl.when(section == sec)(lambda sec=sec: run(sec))
    for r in range(BLK):
        column_ref[r * GROUP : (r + 1) * GROUP, :] = column_rows(resid_ref, r, 0, BLK, FIELD, 0.0)


def adjoint_kernel(
    resid_ref, other_ref, input_grad_ref, c_ref, factor_ref,
    strip, partner, rims, partner_rims, own_col, other_col,
    out_ref, pa, pb, u, v, matrix, w,
):
    section, lev = lax.axis_index("sec"), lax.axis_index("lev")
    own_level = EDGE * lev
    for ref in (pa, pb, u, v, w):
        clear(ref)
    clear_levels(pa)
    clear_levels(pb)
    masks = edge_masks()
    matrix[...] = across_matrix()

    def run(sec):
        spread_rims(
            sec, lev, strip, partner, rims, partner_rims, own_col, other_col,
            ((pa, 2, None), (u, 0, None), (v, 0, None)),
        )
        other_row, near_edge, far_edge = static_rows(sec)
        for n, (dst, shift) in enumerate(((pa, 2), (u, 0), (v, 0))):
            at = pl.ds(own_level + shift, OWN)
            packed = slice(n * FIELD, (n + 1) * FIELD)
            dst[at, 3 * BLK : 4 * BLK, :] = resid_ref[packed, :].reshape(OWN, BLK, 128)
            dst[at, other_row : other_row + BLK, :] = other_ref[packed, :].astype(F32).reshape(OWN, BLK, 128)
        near_factor, far_factor = (0, 2) if sec == 0 else (2, 0)
        for step in range(SUBSTEPS):
            old, new = (pa, pb) if step % 2 == 0 else (pb, pa)
            first, last = WIND_BLOCKS[step]
            wide = slice(BLK + BLK * max(first - 1, 0), BLK + BLK * min(last + 1, 5))
            first, last = MASS_BLOCKS[step]
            narrow = slice(BLK + BLK * max(first - 1, 0), BLK + BLK * min(last + 1, 5))

            def body(step=step, old=old, new=new, wide=wide, narrow=narrow):
                k, size = 0, EXT
                whole = pl.ds(0, size)
                levels = pl.ds(k, size)
                inner = pl.ds(k + 2, size)
                w[whole, wide, :] = c_ref[levels, wide, :] * old[inner, wide, :]
                first, last = WIND_BLOCKS[step]
                slopes = across(w[whole, BLK + BLK * first : BLK + BLK * last, :], matrix)
                for block in range(first, last):
                    row = BLK + BLK * block
                    rows = slice(row, row + BLK)
                    u[levels, rows, :] = u[levels, rows, :] + along(w, whole, row)
                    at = BLK * (block - first)
                    v[levels, rows, :] = v[levels, rows, :] + slopes[:, at : at + BLK, :]
                for edge, f in ((near_edge, near_factor), (far_edge, far_factor))[: 2 if step < 2 else 1]:
                    rows = slice(edge - 4, edge + 4)
                    cross = crossing(w[whole, rows, :], masks)
                    u[levels, rows, :] = u[levels, rows, :] + factor_ref[f] * cross
                    v[levels, rows, :] = v[levels, rows, :] - factor_ref[f + 1] * cross
                w[whole, narrow, :] = c_ref[levels, narrow, :] * u[levels, narrow, :]
                first, last = MASS_BLOCKS[step]
                rows = slice(BLK + BLK * first, BLK + BLK * last)
                slopes = across(c_ref[levels, rows, :] * v[levels, rows, :], matrix)
                for block in range(first, last):
                    row = BLK + BLK * block
                    at = BLK * (block - first)
                    spread_uv = along(w, whole, row) + slopes[:, at : at + BLK, :]
                    new[inner, row : row + BLK, :] = vertical(old, k, size, row) + spread_uv

            body()

    for sec in range(2):
        pl.when(section == sec)(lambda sec=sec: run(sec))
    final = pa if SUBSTEPS % 2 == 0 else pb
    for n, (src, shift) in enumerate(((final, 2), (u, 0), (v, 0))):
        packed = slice(n * FIELD, (n + 1) * FIELD)
        adjoint = src[pl.ds(own_level + shift, OWN), 3 * BLK : 4 * BLK, :].reshape(FIELD, 128)
        out_ref[packed, :] = adjoint + input_grad_ref[packed, :]


def dot(left, right):
    return lax.dot_general(left, right, (((1,), (0,)), ((), ())), preferred_element_type=F32)


def dot_t(left, right):
    return lax.dot_general(left, right, (((0,), (0,)), ((), ())), preferred_element_type=F32)


def dot_columns(left, right):
    return lax.dot_general(left, right, (((1,), (1,)), ((), ())), preferred_element_type=F32)


def silu_and_slope(values):
    sigma = 0.5 * jnp.tanh(0.5 * values) + 0.5
    silu = values * sigma
    return silu.astype(BF), sigma + silu * (1.0 - sigma)


def both_groups(own_ref, other_ref):
    parts = [
        jnp.concatenate([ref[r * GROUP : (r + 1) * GROUP, :] for ref in (own_ref, other_ref)], axis=0)
        for r in range(STRIPE // 128)
    ]
    return jnp.concatenate(parts, axis=1)


def to_fields(out_ref, first, values, minus_ref=None, minus_first=None):
    for r in range(STRIPE // 128):
        for n in range(3):
            value = values[n * OWN : (n + 1) * OWN, r * 128 : (r + 1) * 128]
            if minus_ref is not None:
                value = value - minus_ref[pl.ds(n * OWN * 16 + minus_first + r, OWN, stride=16), :]
            out_ref[pl.ds(n * FIELD + first + r, OWN, stride=BLK), :] = value


def network_kernel(
    own_ref, other_ref, first_ref, second_ref, third_t_ref, target_ref,
    feat_ref, one_ref, two_ref, slope_one_ref, slope_two_ref, tendency_ref,
):
    feat = both_groups(own_ref, other_ref)
    feat_ref[...] = feat
    one, slope = silu_and_slope(dot_t(first_ref[...], feat))
    one_ref[...] = one
    slope_one_ref[...] = slope
    two, slope = silu_and_slope(dot_t(second_ref[...], one))
    two_ref[...] = two
    slope_two_ref[...] = slope
    row = pl.program_id(0) * (STRIPE // 128)
    at = BLK * lax.axis_index("sec") + row
    to_fields(tendency_ref, row, dot(third_t_ref[:GROUP, :], two), target_ref, at)


def back_kernel(
    own_ref, other_ref, feat_ref, third_t_ref, second_ref, first_ref, one_ref, two_ref, slope_one_ref, slope_two_ref,
    given_ref, kept_ref, input_grad_ref, err_one_ref, err_two_ref, total_ref,
):
    step = pl.program_id(0)
    resid = both_groups(own_ref, other_ref)
    err_two = (dot_t(third_t_ref[...], resid) * slope_two_ref[...]).astype(BF)
    err_two_ref[...] = err_two
    err_one = (dot(second_ref[...], err_two) * slope_one_ref[...]).astype(BF)
    err_one_ref[...] = err_one
    to_fields(input_grad_ref, step * (STRIPE // 128), dot(first_ref[:GROUP, :], err_one))
    feats, hid = feat_ref.shape[0], one_ref.shape[0]
    half = pl.ds(pl.multiple_of(256 * lax.axis_index("lev"), 256), 256)

    def clear_total():
        total_ref[...] = jnp.zeros(total_ref.shape, F32)

    pl.when(step == 0)(clear_total)

    def add(rows, left, right):
        total_ref[rows, :] = total_ref[rows, :] + dot_columns(left, right)

    add(slice(0, feats), feat_ref[...], err_one_ref[half, :])
    add(slice(feats, feats + hid), one_ref[...], err_two_ref[half, :])
    add(slice(feats + hid, 2 * feats + hid), resid, two_ref[half, :])

    def finish():
        for sec in range(2):

            def share(sec=sec):
                kept_ref[...] = total_ref[:, 128 * sec : 128 * sec + 128]
                given_ref[...] = total_ref[:, 128 - 128 * sec : 256 - 128 * sec].astype(BF)

            pl.when(lax.axis_index("sec") == sec)(share)

    pl.when(step == COLS // STRIPE - 1)(finish)


def join_kernel(near_ref, far_ref, strip_ref, edge_ref):
    strip_ref[: 3 * FIELD, :] = near_ref[...]
    strip_ref[3 * FIELD :, :] = far_ref[...]
    for n in range(3):
        corner(edge_ref, n, near_ref, n * FIELD, far_ref, n * FIELD, lax.axis_index("lev"))


def add_kernel(kept_ref, received_ref, out_ref):
    out_ref[...] = (kept_ref[...] + received_ref[...].astype(F32)).astype(BF)


def mean_kernel(parts_ref, out_ref):
    total = parts_ref[0].astype(F32)
    for tile in range(1, parts_ref.shape[0]):
        total = total + parts_ref[tile].astype(F32)
    mean = (total / (COLS * out_ref.shape[0])).astype(BF)
    for device in range(out_ref.shape[0]):
        out_ref[device] = mean


def place_rows_kernel(mine_ref, theirs_ref, out_ref):
    for sec in range(2):

        def run(sec=sec):
            for n in range(3):
                packed = slice(n * FIELD, (n + 1) * FIELD)
                for core, ref in ((sec, mine_ref), (1 - sec, theirs_ref)):
                    out_ref[n, :, BLK * core : BLK * core + BLK, :] = ref[packed, :].reshape(OWN, BLK, 128)

        pl.when(lax.axis_index("sec") == sec)(run)


def spread_gradients_kernel(own_ref, partner_ref, first_ref, bias_ref, second_ref, third_t_ref):
    section = lax.axis_index("sec")
    hid = second_ref.shape[0]
    share = own_ref.shape[1]

    def feature_rows(out, row, lanes, lev, values):
        group, at = divmod(row, GROUP)
        if at < 3 * OWN:
            field, level = divmod(at, OWN)
            to = (2 * field + (lev + group) % 2) * OWN + level
            out[to : to + 8, lanes] = values

    def run(sec):
        blocks = [(tile, lev, core) for tile in range(own_ref.shape[0] // 2) for lev in range(2) for core in range(2)]
        for tile, lev, core in blocks:
            lanes = slice(256 * lev + 128 * core, 256 * lev + 128 * core + 128)
            block = (own_ref if core == sec else partner_ref)[2 * tile + lev].astype(F32)
            for part in range(0, share, 8):
                row = tile * share + part
                values = block[part : part + 8, :]
                if row < 2 * GROUP:
                    feature_rows(first_ref, row, lanes, lev, values)
                    if row == 3 * OWN:
                        bias_ref[:, lanes] = values[:1, :]
                elif row < 2 * GROUP + hid:
                    second_ref[row - 2 * GROUP : row - 2 * GROUP + 8, lanes] = values
                else:
                    feature_rows(third_t_ref, row - 2 * GROUP - hid, lanes, lev, values)

    for sec in range(2):
        pl.when(section == sec)(lambda sec=sec: run(sec))


def whole(value):
    return pl.BlockSpec(value.shape, lambda i: (0,) * len(value.shape), pipeline_mode=pl.Buffered(1))


def stripes(value, along):
    if along:
        return pl.BlockSpec((value.shape[0], STRIPE), lambda i: (0, i))
    return pl.BlockSpec((STRIPE // 128 * GROUP, 128), lambda i: (i, 0))


def first_rows(rows, value):
    return pl.BlockSpec((rows, *value.shape[1:]), lambda i: (0,) * len(value.shape), pipeline_mode=pl.Buffered(1))


def call(kernel, n_smem, operands, outs, scratch=(), flops=0, limit=40, steps=1, in_along=None, out_along=None):
    def specs(values, along):
        along = along or [None] * len(values)
        return [whole(v) if at is None else first_rows(at, v) if at > 1 else stripes(v, at) for v, at in zip(values, along, strict=True)]

    smem = pl.BlockSpec(memory_space=pltpu.SMEM)
    return pl.pallas_call(
        kernel,
        grid=(steps,),
        out_shape=outs,
        in_specs=[smem] * n_smem + specs(operands[n_smem:], in_along),
        out_specs=specs(outs, out_along),
        scratch_shapes=list(scratch),
        compiler_params=pltpu.CompilerParams(vmem_limit_bytes=limit * MIB),
        cost_estimate=pl.CostEstimate(flops=flops, bytes_accessed=0, transcendentals=0),
    )(*operands)


def stencil_scratch(extra=()):
    mass = pltpu.VMEM((EXT + 4, ROWS, 128), F32)
    wind = pltpu.VMEM((EXT, ROWS, 128), F32)
    return [mass, mass, wind, wind, pltpu.VMEM((256, 128), BF), *extra]


def shape(*dims, dtype=F32):
    return jax.ShapeDtypeStruct(dims, dtype)


def swap(value, axis):
    return lax.ppermute(value, axis, [(0, 1), (1, 0)])


def strip_swaps(strip, edges, tiles):
    pairs = [(tiles + t, t + 1) for t in range(tiles - 1)]
    pairs += [(b, a) for a, b in pairs]
    cross = [(2 * a + lev, 2 * b + 1 - lev) for a, b in pairs for lev in range(2)]
    return lax.ppermute(strip, ("sec", "tile"), pairs), lax.ppermute(edges, ("sec", "tile", "lev"), cross)


def local(state, sound, target, edge_turn, w_first, b_first, w_second, w_third):
    tiles = lax.axis_size("tile")
    hid, feats = w_second.shape[0], 2 * GROUP

    state, sound, target = state.reshape(-1, 128), sound.reshape(-1, 128), target.reshape(-1, 128)
    strip, edges, columns, first, third_t = call(
        pack_kernel, 1, (edge_turn, state, sound, w_first, w_third.T, b_first[None]),
        (shape(8 * FIELD + 16, 128, dtype=BF), shape(4 * RIM, 128, dtype=BF), shape(BLK * GROUP + RIM, 128, dtype=BF), shape(feats, hid, dtype=BF), shape(feats, hid, dtype=BF)),
        limit=60,
    )
    own_col = swap(columns, "lev")
    strip, rims = strip_swaps(strip, edges, tiles)

    activations = (shape(feats, COLS, dtype=BF), shape(hid, COLS, dtype=BF), shape(hid, COLS, dtype=BF), shape(hid, COLS), shape(hid, COLS))
    feat, one, two, slope_one, slope_two, tendency = call(
        network_kernel, 0, (columns, own_col, first, w_second, third_t, target),
        (*activations, shape(3 * FIELD, 128)),
        steps=COLS // STRIPE, flops=LONG, in_along=(0, 0, None, None, None, None), out_along=(1, 1, 1, 1, 1, None),
    )

    other_col = swap(own_col, "sec")
    strip, rims, tendency = lax.optimization_barrier((strip, rims, tendency))
    resid, r_rows, r_columns, coeff, factors = call(
        forward_kernel, 1,
        (edge_turn, state, sound, tendency, strip, swap(strip, "sec"), rims, swap(rims, "sec"), own_col, other_col),
        (shape(3 * FIELD, 128), shape(3 * FIELD, 128, dtype=BF), shape(BLK * GROUP, 128, dtype=BF), shape(EXT, ROWS, 128), shape(4, BLK, 128)),
        stencil_scratch(), flops=LONG, in_along=(*[None] * 4, 4 * FIELD + 16, *[None] * 4),
    )

    r_own_col = swap(r_columns, "lev")
    r_other = swap(r_rows, "sec")
    r_strip, r_edges = call(
        join_kernel, 0, (r_rows, r_other),
        (shape(6 * FIELD, 128, dtype=BF), shape(3 * RIM, 128, dtype=BF)), limit=16,
    )
    r_strip, r_rims = strip_swaps(r_strip, r_edges, tiles)
    r_own_col, r_rims = lax.optimization_barrier((r_own_col, r_rims))

    n_rows = 2 * feats + hid
    given, kept, input_grad = call(
        back_kernel, 0, (r_columns, r_own_col, feat, third_t, w_second, first, one, two, slope_one, slope_two),
        (shape(n_rows, 128, dtype=BF), shape(n_rows, 128), shape(3 * FIELD, 128)),
        (pltpu.VMEM((hid, STRIPE), BF), pltpu.VMEM((hid, STRIPE), BF), pltpu.VMEM((n_rows, 256), F32)),
        flops=LONG, steps=COLS // STRIPE, in_along=(0, 0, 1, None, None, None, 1, 1, 1, 1),
    )
    received = swap(given, "sec")
    share = n_rows // tiles
    (partial,) = call(add_kernel, 0, (kept, received), (shape(n_rows, 128, dtype=BF),), limit=16)
    partial = partial.reshape(tiles, share, 128)
    parts = lax.all_to_all(partial, "tile", 0, 0)
    (everywhere,) = call(mean_kernel, 0, (parts,), (shape(2 * tiles, share, 128, dtype=BF),), limit=16, flops=LONG)
    everywhere, coeff = lax.optimization_barrier((everywhere, coeff))
    r_partner, r_partner_rims, r_other_col = swap(r_strip, "sec"), swap(r_rims, "sec"), swap(r_own_col, "sec")
    gathered = lax.all_to_all(everywhere, ("tile", "lev"), 0, 0)
    (mine,) = call(
        adjoint_kernel, 0,
        (resid, r_other, input_grad, coeff, factors, r_strip, r_partner, r_rims, r_partner_rims, r_own_col, r_other_col),
        (shape(3 * FIELD, 128),), stencil_scratch((pltpu.VMEM((EXT, ROWS, 128), F32),)), flops=LONG, limit=60,
        in_along=(*[None] * 6, 3 * FIELD, *[None] * 4),
    )
    theirs, gathered = lax.optimization_barrier((swap(mine, "sec"), gathered))
    (state_grad,) = call(place_rows_kernel, 0, (mine, theirs), (shape(3, OWN, 2 * BLK, 128),), limit=16)
    g_first, g_bias, g_second, g_third_t = call(
        spread_gradients_kernel, 0, (gathered, swap(gathered, "sec")),
        (shape(6 * OWN, hid), shape(1, hid), shape(hid, hid), shape(6 * OWN, hid)), limit=16,
    )
    return (state_grad, g_first, g_bias.reshape(hid), g_second, g_third_t.T)


def solution(mesh):
    placed = (
        P(None, "lev", "tile", None),
        P("lev", "tile", None),
        P(None, "lev", "tile", None),
        P("tile", None),
        P(),
        P(),
        P(),
        P(),
    )
    return jax.shard_map(
        local,
        mesh=mesh,
        in_specs=placed,
        out_specs=(P(None, "lev", "tile", None), P(), P(), P(), P()),
        check_vma=False,
    )
```
